256 devices in a mesh: tile: 32 (over y, z_lo, x), ens: 8 (over z_hi, core).
Axes of the slice: x: 4, y: 4, z: 8 (z_hi: 4, z_lo: 2; z = z_hi * 2 + z_lo), core: 2. Of those that a mesh axis runs over, the one named last changes fastest.
Arguments:
- network_conditions: bfloat16 [8, 96, 8, 8, 256], P('ens', 'tile'), may hold values from -6 to 6
- subsequent_targets: bfloat16 [8, 96, 8, 8, 256], P('ens', 'tile'), may hold values from -6 to 6
- w_first: bfloat16 [3, 3, 256, 256], replicated, may hold values from -0.125 to 0.125
- w_second: bfloat16 [3, 3, 256, 256], replicated, may hold values from -0.125 to 0.125
- tile_links: int32 [96, 16], P('tile'), may hold values from -1 to 383, as said below
Outputs:
- layer_prognosis: bfloat16 [8, 96, 8, 8, 256], P('ens', 'tile')
- condition_derivative: float32 [8, 96, 8, 8, 256], P('ens', 'tile')
- initial_kernel_slope: float32 [3, 3, 256, 256], replicated
- latter_kernel_slope: float32 [3, 3, 256, 256], replicated
The draws below stay inside these ranges and needn't reach their ends.
Inputs may be any that keep to these rules, and one draw needn't show every extreme that they name: tile_links describes a cubed sphere of 6 faces of 4 x 4 tiles. The tiles are numbered face by face: face q holds tiles q * 4 * 4 to (q + 1) * 4 * 4 - 1, in row-major order of its 4 x 4 grid, and which cube face is face q is drawn. Row p: columns 0 to 3 name the tile beyond the north, east, south and west edge of tile p; columns 4 to 7 hold e + 4 f, where e is the edge of that tile that touches tile p and f is 1 when the cells along the two edges run opposite ways, else 0; columns 8 to 11 hold 4 m + k for the corners 0 to 3, tile m lying diagonally across with its corner k at the same point, or -1 where only three tiles meet; columns 12 to 15 hold the number of tiles meeting at those corners, 3 or 4. The relation is symmetric: the tile beyond edge e of p names p beyond its edge given by column 4+e, with the same f, and likewise for corners.
All inputs are finite; a program needn't handle non-finite values.
Results may differ from the reference program's by a relative error of at most 0.0034.
Values may be sent and summed in bfloat16 or wider, within the bound.
No kernel may reach another device: no remote copies, remote signals or barrier semaphores. Data moves between devices by JAX's collectives and lax.ppermute only.
A program may use at most 64 MiB of HBM per device.

```python
import math
import jax
import jax.numpy as jnp
import numpy as np
from jax import lax

C = 256
K = 4
S = 8
TILES = 96
MEMBERS = 8
COUNT = 49152


def cube_tables(faces_side):
    half_side = faces_side / 2.0
    normals = np.array([[1, 0, 0], [0, 1, 0], [-1, 0, 0], [0, -1, 0], [0, 0, 1], [0, 0, -1]], dtype=np.float32)
    right_axes = np.array([[0, 1, 0], [-1, 0, 0], [0, -1, 0], [1, 0, 0], [1, 0, 0], [1, 0, 0]], dtype=np.float32)
    down_axes = np.stack([right_axes[:, 1] * normals[:, 2] - right_axes[:, 2] * normals[:, 1], right_axes[:, 2] * normals[:, 0] - right_axes[:, 0] * normals[:, 2], right_axes[:, 0] * normals[:, 1] - right_axes[:, 1] * normals[:, 0]], axis=1)
    tile_count = 6 * faces_side * faces_side
    centers = np.zeros((tile_count, 3), dtype=np.float32)
    normal_of = np.zeros((tile_count, 3), dtype=np.float32)
    step_vectors = np.zeros((tile_count, 4, 3), dtype=np.float32)
    run_vectors = np.zeros((tile_count, 4, 3), dtype=np.float32)
    vertices = np.zeros((tile_count, 4, 3), dtype=np.float32)
    for face_index in range(6):
        right_axis = right_axes[face_index]
        down_axis = down_axes[face_index]
        for down_index in range(faces_side):
            for right_index in range(faces_side):
                tile_index = (face_index * faces_side + down_index) * faces_side + right_index
                center = normals[face_index] * half_side + right_axis * (right_index - half_side + 0.5) + down_axis * (down_index - half_side + 0.5)
                centers[tile_index] = center
                normal_of[tile_index] = normals[face_index]
                step_vectors[tile_index] = np.stack([-down_axis, right_axis, down_axis, -right_axis])
                run_vectors[tile_index] = np.stack([right_axis, down_axis, right_axis, down_axis])
                vertices[tile_index] = np.stack([center + 0.5 * (-right_axis - down_axis), center + 0.5 * (right_axis - down_axis), center + 0.5 * (right_axis + down_axis), center + 0.5 * (-right_axis + down_axis)])
    neighbours = np.zeros((tile_count, 4), dtype=np.int32)
    for tile_index in range(tile_count):
        axis_normal = int(np.argmax(np.abs(normal_of[tile_index])))
        for edge_index in range(4):
            probe = centers[tile_index] + step_vectors[tile_index, edge_index]
            if np.max(np.abs(probe)) > half_side + 0.25:
                axis_over = int(np.argmax(np.abs(probe)))
                probe[axis_over] = np.sign(probe[axis_over]) * half_side
                probe[axis_normal] = np.sign(probe[axis_normal]) * (half_side - 0.5)
            distance = np.sum((centers - probe) * (centers - probe), axis=1)
            neighbours[tile_index, edge_index] = int(np.argmin(distance))
    link_table = np.zeros((tile_count, 16), dtype=np.int32)
    flat_vertices = vertices.reshape(tile_count * 4, 3)
    side_edges = [(0, 3), (0, 1), (1, 2), (2, 3)]
    for tile_index in range(tile_count):
        for edge_index in range(4):
            outside_tile = int(neighbours[tile_index, edge_index])
            back_edge = [other_edge for other_edge in range(4) if neighbours[outside_tile, other_edge] == tile_index][0]
            flip_bit = 1 if np.dot(run_vectors[tile_index, edge_index], run_vectors[outside_tile, back_edge]) < 0 else 0
            link_table[tile_index, edge_index] = outside_tile
            link_table[tile_index, 4 + edge_index] = back_edge + 4 * flip_bit
        for corner_index in range(4):
            spacing = np.sum(np.abs(flat_vertices - vertices[tile_index, corner_index]), axis=1)
            matches = [found for found in range(tile_count * 4) if spacing[found] < 0.001]
            meeting = len(matches)
            near_tiles = [tile_index, int(neighbours[tile_index, side_edges[corner_index][0]]), int(neighbours[tile_index, side_edges[corner_index][1]])]
            diagonal_corner = -1
            if meeting == 4:
                diagonal_corner = [found for found in matches if found // 4 not in near_tiles][0]
            link_table[tile_index, 8 + corner_index] = diagonal_corner
            link_table[tile_index, 12 + corner_index] = meeting
    return link_table


def draw_tile_links(key, part):
    base_table = jnp.asarray(cube_tables(K), dtype=jnp.int32)
    face_tiles = K * K
    face_order = jax.random.permutation(key, 6).astype(jnp.int32)
    base_index = jnp.arange(TILES, dtype=jnp.int32)
    grid_position = (face_order[base_index // face_tiles] * face_tiles + base_index % face_tiles).astype(jnp.int32)
    tile_order = jnp.argsort(grid_position).astype(jnp.int32)
    selected_entry = base_table[tile_order]
    outside_tile = grid_position[selected_entry[:, 0:4]]
    diagonal_corner = selected_entry[:, 8:12]
    clamped_value = jnp.maximum(diagonal_corner, 0)
    renamed_tiles = jnp.where(diagonal_corner >= 0, grid_position[clamped_value // 4] * 4 + clamped_value % 4, -1)
    return jnp.concatenate([outside_tile, selected_entry[:, 4:8], renamed_tiles, selected_entry[:, 12:16]], axis=1).astype(jnp.int32)


def steps_of(own_key, shape, split, smallest, largest):
    factor_of = 1.0
    for dim, parts in split:
        draws = jax.random.uniform(jax.random.fold_in(jax.random.fold_in(own_key, 6), dim), (parts,), jnp.float32, smallest / len(split), largest / len(split))
        factor_of = factor_of * jnp.repeat(jnp.exp(draws), shape[dim] // parts).reshape((-1,) + (1,) * (len(shape) - 1 - dim))
    return factor_of


def scatter_about(key, shape, scale, bound, cuts=(), held_as=jnp.bfloat16):
    entries = scale * jax.random.normal(key, shape, jnp.float32)
    if cuts:
        entries = entries * steps_of(key, shape, cuts, -0.22, 0.18)
    return jnp.clip(entries, -bound, bound).astype(held_as)


def setup_inputs(seed: int = 0) -> dict:
    keys = jax.random.split(jax.random.key(seed), 6)
    network_conditions = scatter_about(keys[0], (MEMBERS, TILES, S, S, C), 1.0, 6.0, ((0, 8), (1, 32)))
    subsequent_targets = scatter_about(keys[1], (MEMBERS, TILES, S, S, C), 1.0, 6.0, ((0, 8), (1, 32)))
    w_first = scatter_about(keys[2], (3, 3, C, C), (9 * C) ** -0.5, 0.125)
    w_second = scatter_about(keys[3], (3, 3, C, C), (9 * C) ** -0.5, 0.125)
    tile_links = draw_tile_links(jax.random.fold_in(keys[5], 71), 0)
    return dict(network_conditions=network_conditions, subsequent_targets=subsequent_targets, w_first=w_first, w_second=w_second, tile_links=tile_links)


tanh_scale = 0.7978845608028654
cubic_term = 0.044715
layout_names = ('NHWC', 'HWIO', 'NHWC')

def gelu_value(inputs):
    return 0.5 * inputs * (1.0 + jnp.tanh(tanh_scale * (inputs + cubic_term * inputs * inputs * inputs)))

def gelu_slope(inputs):
    tangent = jnp.tanh(tanh_scale * (inputs + cubic_term * inputs * inputs * inputs))
    return 0.5 * (1.0 + tangent) + 0.5 * inputs * (1.0 - tangent * tangent) * tanh_scale * (1.0 + 3.0 * cubic_term * inputs * inputs)

def rim_frame(values):
    length = values.shape[1]
    edge_cells = jnp.stack([values[:, 0], values[:, :, length - 1], values[:, length - 1], values[:, :, 0]], axis=1)
    corner_cells = jnp.stack([values[:, 0, 0], values[:, 0, length - 1], values[:, length - 1, length - 1], values[:, length - 1, 0]], axis=1)
    return (edge_cells, corner_cells)

def move_frames(edge_cells, corner_cells, tile_links):
    number = edge_cells.shape[0]
    length = edge_cells.shape[2]
    channels = edge_cells.shape[3]
    source = (tile_links[:, 0:4] * 4 + tile_links[:, 4:8] % 4).reshape(-1)
    turned = (tile_links[:, 4:8] // 4 == 1)[:, :, None, None]
    ghost_rows = jnp.take(edge_cells.reshape(number * 4, length, channels), source, axis=0).reshape(number, 4, length, channels)
    ghost_rows = jnp.where(turned, ghost_rows[:, :, ::-1], ghost_rows)
    across = tile_links[:, 8:12].reshape(-1)
    ghost_corners = jnp.take(corner_cells.reshape(number * 4, channels), jnp.maximum(across, 0), axis=0).reshape(number, 4, channels)
    ghost_corners = jnp.where((across >= 0).reshape(number, 4)[:, :, None], ghost_corners, jnp.zeros_like(ghost_corners))
    return (ghost_rows, ghost_corners)

def with_ghosts(values, ghost_rows, ghost_corners, tile_links):
    length = values.shape[1]
    widened = ghost_rows.astype(jnp.float32)
    meeting = tile_links[:, 12:16]
    blended = jnp.stack([0.5 * (widened[:, 0, 0] + widened[:, 3, 0]), 0.5 * (widened[:, 0, length - 1] + widened[:, 1, 0]), 0.5 * (widened[:, 1, length - 1] + widened[:, 2, length - 1]), 0.5 * (widened[:, 2, 0] + widened[:, 3, length - 1])], axis=1)
    corner = jnp.where((meeting == 4)[:, :, None], ghost_corners.astype(jnp.float32), blended).astype(values.dtype)
    ghost_rows = ghost_rows.astype(values.dtype)
    middle = jnp.concatenate([ghost_rows[:, 3][:, :, None], values, ghost_rows[:, 1][:, :, None]], axis=2)
    top_row = jnp.concatenate([corner[:, 0][:, None], ghost_rows[:, 0], corner[:, 1][:, None]], axis=1)
    bottom = jnp.concatenate([corner[:, 3][:, None], ghost_rows[:, 2], corner[:, 2][:, None]], axis=1)
    return jnp.concatenate([top_row[:, None], middle, bottom[:, None]], axis=1)

def ghost_grads(full, tile_links):
    length = full.shape[1] - 2
    meeting = tile_links[:, 12:16]
    corners = jnp.stack([full[:, 0, 0], full[:, 0, length + 1], full[:, length + 1, length + 1], full[:, length + 1, 0]], axis=1)
    half_corner = jnp.where((meeting == 3)[:, :, None], 0.5 * corners, jnp.zeros_like(corners))
    north_row = full[:, 0, 1:length + 1].at[:, 0].add(half_corner[:, 0]).at[:, length - 1].add(half_corner[:, 1])
    east_column = full[:, 1:length + 1, length + 1].at[:, 0].add(half_corner[:, 1]).at[:, length - 1].add(half_corner[:, 2])
    south_row = full[:, length + 1, 1:length + 1].at[:, length - 1].add(half_corner[:, 2]).at[:, 0].add(half_corner[:, 3])
    west_column = full[:, 1:length + 1, 0].at[:, 0].add(half_corner[:, 0]).at[:, length - 1].add(half_corner[:, 3])
    edge_cells = jnp.stack([north_row, east_column, south_row, west_column], axis=1).astype(jnp.bfloat16)
    kept = jnp.where((meeting == 4)[:, :, None], corners, jnp.zeros_like(corners)).astype(jnp.bfloat16)
    return (edge_cells, kept)

def add_returns(full, ghost_rows, ghost_corners):
    length = full.shape[1] - 2
    interior = full[:, 1:length + 1, 1:length + 1]
    ghost_rows = ghost_rows.astype(jnp.float32)
    ghost_corners = ghost_corners.astype(jnp.float32)
    interior = interior.at[:, 0, :].add(ghost_rows[:, 0])
    interior = interior.at[:, :, length - 1].add(ghost_rows[:, 1])
    interior = interior.at[:, length - 1, :].add(ghost_rows[:, 2])
    interior = interior.at[:, :, 0].add(ghost_rows[:, 3])
    interior = interior.at[:, 0, 0].add(ghost_corners[:, 0])
    interior = interior.at[:, 0, length - 1].add(ghost_corners[:, 1])
    interior = interior.at[:, length - 1, length - 1].add(ghost_corners[:, 2])
    interior = interior.at[:, length - 1, 0].add(ghost_corners[:, 3])
    return interior

def convolve(padded, kernel):
    return lax.conv_general_dilated(padded.astype(jnp.float32), kernel.astype(jnp.float32), (1, 1), 'VALID', dimension_numbers=layout_names, precision=lax.Precision.HIGHEST)

def spread_back(gradient, kernel):
    turned_kernel = jnp.transpose(kernel[::-1, ::-1], (0, 1, 3, 2))
    return lax.conv_general_dilated(gradient.astype(jnp.float32), turned_kernel.astype(jnp.float32), (1, 1), ((2, 2), (2, 2)), dimension_numbers=layout_names, precision=lax.Precision.HIGHEST)

def weight_grad(padded, gradient):
    length = gradient.shape[1]
    channels = gradient.shape[3]
    flat_grad = gradient.reshape(-1, channels)
    tap_list = []
    for tap_down in range(3):
        for tap_across in range(3):
            window = padded[:, tap_down:tap_down + length, tap_across:tap_across + length].reshape(-1, channels)
            tap_list.append(jnp.dot(window.T, flat_grad, preferred_element_type=jnp.float32))
    return jnp.stack(tap_list).reshape(3, 3, channels, channels)

def one_member(field_here, goal_here, w_first, w_second, tile_links):
    edge_cells, corner_cells = rim_frame(field_here)
    ghost_rows, ghost_corners = move_frames(edge_cells, corner_cells, tile_links)
    field_pad = with_ghosts(field_here, ghost_rows, ghost_corners, tile_links)
    pre_first = convolve(field_pad, w_first)
    hidden = gelu_value(pre_first).astype(jnp.bfloat16)
    edge_cells, corner_cells = rim_frame(hidden)
    ghost_rows, ghost_corners = move_frames(edge_cells, corner_cells, tile_links)
    hidden_pad = with_ghosts(hidden, ghost_rows, ghost_corners, tile_links)
    pre_second = convolve(hidden_pad, w_second)
    estimated_states = field_here.astype(jnp.float32) + pre_second
    layer_prognosis = estimated_states.astype(jnp.bfloat16)
    misfit = estimated_states - goal_here.astype(jnp.float32)
    misfit_low = misfit.astype(jnp.bfloat16)
    closing_filter_aggregate = weight_grad(hidden_pad, misfit_low)
    spread = spread_back(misfit_low, w_second)
    edge_cells, corner_cells = ghost_grads(spread, tile_links)
    ghost_rows, ghost_corners = move_frames(edge_cells, corner_cells, tile_links)
    hidden_grad = add_returns(spread, ghost_rows, ghost_corners)
    first_low = (hidden_grad * gelu_slope(pre_first)).astype(jnp.bfloat16)
    opening_filter_aggregate = weight_grad(field_pad, first_low)
    spread = spread_back(first_low, w_first)
    edge_cells, corner_cells = ghost_grads(spread, tile_links)
    ghost_rows, ghost_corners = move_frames(edge_cells, corner_cells, tile_links)
    condition_derivative = misfit + add_returns(spread, ghost_rows, ghost_corners)
    return (layer_prognosis, condition_derivative, opening_filter_aggregate, closing_filter_aggregate)

def reference(network_conditions, subsequent_targets, w_first, w_second, tile_links):

    def projected_sample(sample_couple):
        return one_member(sample_couple[0], sample_couple[1], w_first, w_second, tile_links)
    layer_prognosis, condition_derivative, opening_filter_aggregate, closing_filter_aggregate = lax.map(projected_sample, (network_conditions, subsequent_targets))
    gradient_scale = 1.0 / math.sqrt(COUNT)
    initial_kernel_slope = lax.optimization_barrier(jnp.sum(opening_filter_aggregate, axis=0)) * gradient_scale
    latter_kernel_slope = lax.optimization_barrier(jnp.sum(closing_filter_aggregate, axis=0)) * gradient_scale
    return (layer_prognosis, condition_derivative, initial_kernel_slope, latter_kernel_slope)
```

```python
import math

import jax
import jax.numpy as jnp
from jax import lax
from jax.sharding import PartitionSpec as P

tanh_scale = 0.7978845608028654
cubic_term = 0.044715
layout_names = ("NHWC", "HWIO", "NHWC")
slot_rows = 32


def gelu_value(inputs):
    return (
        0.5
        * inputs
        * (1.0 + jnp.tanh(tanh_scale * (inputs + cubic_term * inputs * inputs * inputs)))
    )


def gelu_slope(inputs):
    tangent = jnp.tanh(tanh_scale * (inputs + cubic_term * inputs * inputs * inputs))
    return 0.5 * (1.0 + tangent) + 0.5 * inputs * (1.0 - tangent * tangent) * tanh_scale * (
        1.0 + 3.0 * cubic_term * inputs * inputs
    )


def rim_frame(values):
    length = values.shape[1]
    edge_cells = jnp.stack(
        [values[:, 0], values[:, :, length - 1], values[:, length - 1], values[:, :, 0]], axis=1
    )
    corner_cells = jnp.stack(
        [
            values[:, 0, 0],
            values[:, 0, length - 1],
            values[:, length - 1, length - 1],
            values[:, length - 1, 0],
        ],
        axis=1,
    )
    return (edge_cells, corner_cells)


def routes(tile_links):
    number = tile_links.shape[0]
    here = lax.axis_index("tile")
    strips = 4 * number

    def rows_of(tile, side, valid, base, width, local_base):
        device = tile // number
        source = (tile % number) * 4 + side
        near = (device[:, None] == device[None, :]) & valid[None, :]
        order = jnp.arange(strips)
        send_rank = jnp.sum(near & (order[None, :] < order[:, None]), axis=1)
        take_rank = jnp.sum(near & (source[None, :] < source[:, None]), axis=1)
        own = device == here
        send = jnp.where(own | ~valid, -width, device * slot_rows + base + send_rank * width)
        take = jnp.where(
            own,
            local_base + source * width,
            device * slot_rows + base + take_rank * width,
        )
        return send, jnp.where(valid, take, -width)

    across = tile_links[:, 8:12].reshape(-1)
    code = tile_links[:, 4:8].reshape(-1)
    total = lax.axis_size("tile") * slot_rows
    always = jnp.ones((strips,), bool)
    send_edge, take_edge = rows_of(
        tile_links[:, 0:4].reshape(-1), code % 4, always, 0, 8, total
    )
    send_corner, take_corner = rows_of(
        jnp.maximum(across, 0) // 4, jnp.maximum(across, 0) % 4, across >= 0, 24, 1, total + 8 * strips
    )
    step = jnp.arange(8)
    forward = send_edge[:, None] + step[None, :]
    backward = take_edge[:, None] + jnp.where((code // 4 == 1)[:, None], 7 - step, step)
    send_rows = jnp.concatenate([forward.reshape(-1), send_corner])
    take_rows = jnp.concatenate([backward.reshape(-1), take_corner])
    cells = 9 * strips
    pack = (jnp.arange(total)[:, None] == send_rows[None, :]).astype(jnp.bfloat16)
    unpack = (take_rows[:, None] == jnp.arange(total + cells)[None, :]).astype(jnp.bfloat16)
    return pack, unpack


def move_frames(edge_cells, corner_cells, pack, unpack):
    number, _, length, channels = edge_cells.shape
    frame = jnp.concatenate(
        [edge_cells.reshape(-1, channels), corner_cells.reshape(-1, channels)], axis=0
    )
    sent = jnp.dot(pack, frame, preferred_element_type=jnp.float32).astype(jnp.bfloat16)
    got = lax.all_to_all(sent, "tile", 0, 0, tiled=True)
    out = jnp.dot(
        unpack, jnp.concatenate([got, frame], axis=0), preferred_element_type=jnp.float32
    ).astype(jnp.bfloat16)
    strips = 4 * number * length
    return (
        out[:strips].reshape(number, 4, length, channels),
        out[strips:].reshape(number, 4, channels),
    )


sizes = {"x": 4, "y": 4, "z": 8, "core": 2}


def place_of(x, y, z, core):
    return ((y * 2 + z % 2) * 4 + x) * 8 + (z // 2) * 2 + core


def shifted(values, axis, by):
    pairs = []
    for x in range(4):
        for y in range(4):
            for z in range(8):
                for core in range(2):
                    at = {"x": x, "y": y, "z": z, "core": core}
                    to = dict(at)
                    to[axis] = (at[axis] + by) % sizes[axis]
                    pairs.append((place_of(**at), place_of(**to)))
    return lax.ppermute(values, ("tile", "ens"), pairs)


def coordinates():
    tile = lax.axis_index("tile")
    ens = lax.axis_index("ens")
    return {
        "x": tile % 4,
        "y": tile // 8,
        "z": (ens // 2) * 2 + (tile // 4) % 2,
        "core": ens % 2,
    }


def scatter_sum(values, axis, where):
    size = sizes[axis]
    mine = where[axis]
    parts = values.reshape((size, values.shape[0] // size) + values.shape[1:])
    total = lax.dynamic_index_in_dim(parts, mine, 0, keepdims=False)
    moved = [
        shifted(lax.dynamic_index_in_dim(parts, (mine + k) % size, 0, keepdims=False), axis, k)
        for k in range(1, size)
    ]
    for part in moved:
        total = total + part
    return total


def gather_parts(values, axis, where):
    size = sizes[axis]
    parts = [values] + [shifted(values, axis, size - k) for k in range(1, size)]
    double = jnp.stack(parts + parts[:-1])
    ordered = lax.dynamic_slice_in_dim(double, (size - where[axis]) % size, size, 0)
    return ordered.reshape((size * values.shape[0],) + values.shape[1:])


def all_sum(values):
    where = coordinates()
    for axis in ("core", "x", "y", "z"):
        values = scatter_sum(values, axis, where)
    return values


def all_parts(values):
    where = coordinates()
    for axis in ("z", "y", "x", "core"):
        values = gather_parts(values, axis, where)
    return values


def with_ghosts(values, ghost_rows, ghost_corners, tile_links):
    length = values.shape[1]
    widened = ghost_rows.astype(jnp.float32)
    meeting = tile_links[:, 12:16]
    blended = jnp.stack(
        [
            0.5 * (widened[:, 0, 0] + widened[:, 3, 0]),
            0.5 * (widened[:, 0, length - 1] + widened[:, 1, 0]),
            0.5 * (widened[:, 1, length - 1] + widened[:, 2, length - 1]),
            0.5 * (widened[:, 2, 0] + widened[:, 3, length - 1]),
        ],
        axis=1,
    )
    corner = jnp.where(
        (meeting == 4)[:, :, None], ghost_corners.astype(jnp.float32), blended
    ).astype(values.dtype)
    middle = jnp.concatenate(
        [ghost_rows[:, 3][:, :, None], values, ghost_rows[:, 1][:, :, None]], axis=2
    )
    top_row = jnp.concatenate(
        [corner[:, 0][:, None], ghost_rows[:, 0], corner[:, 1][:, None]], axis=1
    )
    bottom = jnp.concatenate(
        [corner[:, 3][:, None], ghost_rows[:, 2], corner[:, 2][:, None]], axis=1
    )
    return jnp.concatenate([top_row[:, None], middle, bottom[:, None]], axis=1)


def ghost_grads(full, tile_links):
    length = full.shape[1] - 2
    meeting = tile_links[:, 12:16]
    corners = jnp.stack(
        [
            full[:, 0, 0],
            full[:, 0, length + 1],
            full[:, length + 1, length + 1],
            full[:, length + 1, 0],
        ],
        axis=1,
    )
    half_corner = jnp.where((meeting == 3)[:, :, None], 0.5 * corners, jnp.zeros_like(corners))
    north_row = (
        full[:, 0, 1 : length + 1]
        .at[:, 0]
        .add(half_corner[:, 0])
        .at[:, length - 1]
        .add(half_corner[:, 1])
    )
    east_column = (
        full[:, 1 : length + 1, length + 1]
        .at[:, 0]
        .add(half_corner[:, 1])
        .at[:, length - 1]
        .add(half_corner[:, 2])
    )
    south_row = (
        full[:, length + 1, 1 : length + 1]
        .at[:, length - 1]
        .add(half_corner[:, 2])
        .at[:, 0]
        .add(half_corner[:, 3])
    )
    west_column = (
        full[:, 1 : length + 1, 0]
        .at[:, 0]
        .add(half_corner[:, 0])
        .at[:, length - 1]
        .add(half_corner[:, 3])
    )
    edge_cells = jnp.stack([north_row, east_column, south_row, west_column], axis=1).astype(
        jnp.bfloat16
    )
    kept = jnp.where((meeting == 4)[:, :, None], corners, jnp.zeros_like(corners)).astype(
        jnp.bfloat16
    )
    return (edge_cells, kept)


def add_returns(full, ghost_rows, ghost_corners):
    length = full.shape[1] - 2
    interior = full[:, 1 : length + 1, 1 : length + 1]
    ghost_rows = ghost_rows.astype(jnp.float32)
    ghost_corners = ghost_corners.astype(jnp.float32)
    interior = interior.at[:, 0, :].add(ghost_rows[:, 0])
    interior = interior.at[:, :, length - 1].add(ghost_rows[:, 1])
    interior = interior.at[:, length - 1, :].add(ghost_rows[:, 2])
    interior = interior.at[:, :, 0].add(ghost_rows[:, 3])
    interior = interior.at[:, 0, 0].add(ghost_corners[:, 0])
    interior = interior.at[:, 0, length - 1].add(ghost_corners[:, 1])
    interior = interior.at[:, length - 1, length - 1].add(ghost_corners[:, 2])
    interior = interior.at[:, length - 1, 0].add(ghost_corners[:, 3])
    return interior


def convolve(padded, kernel):
    return lax.conv_general_dilated(
        padded,
        kernel,
        (1, 1),
        "VALID",
        dimension_numbers=layout_names,
        preferred_element_type=jnp.float32,
    )


def spread_back(gradient, kernel):
    turned_kernel = jnp.transpose(kernel[::-1, ::-1], (0, 1, 3, 2))
    return lax.conv_general_dilated(
        gradient,
        turned_kernel,
        (1, 1),
        ((2, 2), (2, 2)),
        dimension_numbers=layout_names,
        preferred_element_type=jnp.float32,
    )


def weight_grad(padded, gradient):
    length = gradient.shape[1]
    channels = gradient.shape[3]
    flat_grad = gradient.reshape(-1, channels)
    tap_list = []
    for tap_down in range(3):
        for tap_across in range(3):
            window = padded[
                :, tap_down : tap_down + length, tap_across : tap_across + length
            ].reshape(-1, channels)
            tap_list.append(
                lax.dot_general(
                    window, flat_grad, (((0,), (0,)), ((), ())), preferred_element_type=jnp.float32
                )
            )
    return jnp.stack(tap_list).reshape(3, 3, channels, channels)


def per_device(network_conditions, subsequent_targets, w_first, w_second, tile_links):
    field_here = network_conditions[0]
    goal_here = subsequent_targets[0]
    number = field_here.shape[0]
    length = field_here.shape[1]
    gradient_scale = 1.0 / math.sqrt(
        lax.axis_size("ens") * lax.axis_size("tile") * number * length * length
    )
    pack, unpack = routes(tile_links)
    edge_cells, corner_cells = rim_frame(field_here)
    ghost_rows, ghost_corners = move_frames(edge_cells, corner_cells, pack, unpack)
    field_pad = with_ghosts(field_here, ghost_rows, ghost_corners, tile_links)
    pre_first = convolve(field_pad, w_first)
    hidden = gelu_value(pre_first).astype(jnp.bfloat16)
    edge_cells, corner_cells = rim_frame(hidden)
    ghost_rows, ghost_corners = move_frames(edge_cells, corner_cells, pack, unpack)
    hidden_pad = with_ghosts(hidden, ghost_rows, ghost_corners, tile_links)
    pre_second = convolve(hidden_pad, w_second)
    estimated_states = field_here.astype(jnp.float32) + pre_second
    layer_prognosis = estimated_states.astype(jnp.bfloat16)
    misfit = estimated_states - goal_here.astype(jnp.float32)
    misfit_low = misfit.astype(jnp.bfloat16)
    closing_filter_aggregate = weight_grad(hidden_pad, misfit_low)
    spread = spread_back(misfit_low, w_second)
    edge_cells, corner_cells = ghost_grads(spread, tile_links)
    ghost_rows, ghost_corners = move_frames(edge_cells, corner_cells, pack, unpack)
    hidden_grad = add_returns(spread, ghost_rows, ghost_corners)
    first_low = (hidden_grad * gelu_slope(pre_first)).astype(jnp.bfloat16)
    opening_filter_aggregate = weight_grad(field_pad, first_low)
    channels = field_here.shape[-1]
    terms = jnp.concatenate(
        [
            opening_filter_aggregate.reshape(9 * channels, channels),
            closing_filter_aggregate.reshape(9 * channels, channels),
        ],
        axis=0,
    )
    slopes = all_parts((all_sum(terms.reshape(256, 18, channels)) * gradient_scale).astype(jnp.bfloat16))
    slopes = slopes.astype(jnp.float32).reshape(2, 3, 3, channels, channels)
    spread = spread_back(first_low, w_first)
    edge_cells, corner_cells = ghost_grads(spread, tile_links)
    ghost_rows, ghost_corners = move_frames(edge_cells, corner_cells, pack, unpack)
    condition_derivative = misfit + add_returns(spread, ghost_rows, ghost_corners)
    return (
        layer_prognosis[None],
        condition_derivative[None],
        slopes[0],
        slopes[1],
    )


def solution(mesh):
    return jax.shard_map(
        per_device,
        mesh=mesh,
        in_specs=(
            P("ens", "tile", None, None, None),
            P("ens", "tile", None, None, None),
            P(),
            P(),
            P("tile", None),
        ),
        out_specs=(
            P("ens", "tile", None, None, None),
            P("ens", "tile", None, None, None),
            P(),
            P(),
        ),
        check_vma=False,
    )
```

```python
import math

import jax
import jax.numpy as jnp
from jax import lax
from jax.experimental import pallas as pl
from jax.experimental.pallas import tpu as pltpu
from jax.sharding import PartitionSpec as P

tanh_scale = 0.7978845608028654
cubic_term = 0.044715
layout_names = ("NHWC", "HWIO", "NHWC")
slot_rows = 32


def gelu_value(inputs):
    return (
        0.5
        * inputs
        * (1.0 + jnp.tanh(tanh_scale * (inputs + cubic_term * inputs * inputs * inputs)))
    )


def gelu_slope(inputs):
    tangent = jnp.tanh(tanh_scale * (inputs + cubic_term * inputs * inputs * inputs))
    return 0.5 * (1.0 + tangent) + 0.5 * inputs * (1.0 - tangent * tangent) * tanh_scale * (
        1.0 + 3.0 * cubic_term * inputs * inputs
    )


def rim_frame(values):
    length = values.shape[1]
    edge_cells = jnp.stack(
        [values[:, 0], values[:, :, length - 1], values[:, length - 1], values[:, :, 0]], axis=1
    )
    corner_cells = jnp.stack(
        [
            values[:, 0, 0],
            values[:, 0, length - 1],
            values[:, length - 1, length - 1],
            values[:, length - 1, 0],
        ],
        axis=1,
    )
    return (edge_cells, corner_cells)


def routes(tile_links):
    number = tile_links.shape[0]
    here = lax.axis_index("tile")
    strips = 4 * number

    def rows_of(tile, side, valid, base, width, local_base):
        device = tile // number
        source = (tile % number) * 4 + side
        near = (device[:, None] == device[None, :]) & valid[None, :]
        order = jnp.arange(strips)
        send_rank = jnp.sum(near & (order[None, :] < order[:, None]), axis=1)
        take_rank = jnp.sum(near & (source[None, :] < source[:, None]), axis=1)
        own = device == here
        send = jnp.where(own | ~valid, -width, device * slot_rows + base + send_rank * width)
        take = jnp.where(
            own,
            local_base + source * width,
            device * slot_rows + base + take_rank * width,
        )
        return send, jnp.where(valid, take, -width)

    across = tile_links[:, 8:12].reshape(-1)
    code = tile_links[:, 4:8].reshape(-1)
    total = lax.axis_size("tile") * slot_rows
    always = jnp.ones((strips,), bool)
    send_edge, take_edge = rows_of(
        tile_links[:, 0:4].reshape(-1), code % 4, always, 0, 8, total
    )
    send_corner, take_corner = rows_of(
        jnp.maximum(across, 0) // 4, jnp.maximum(across, 0) % 4, across >= 0, 24, 1, total + 8 * strips
    )
    step = jnp.arange(8)
    forward = send_edge[:, None] + step[None, :]
    backward = take_edge[:, None] + jnp.where((code // 4 == 1)[:, None], 7 - step, step)
    send_rows = jnp.concatenate([forward.reshape(-1), send_corner])
    take_rows = jnp.concatenate([backward.reshape(-1), take_corner])
    cells = 9 * strips
    pack = (jnp.arange(total)[:, None] == send_rows[None, :]).astype(jnp.bfloat16)
    unpack = (take_rows[:, None] == jnp.arange(total + cells)[None, :]).astype(jnp.bfloat16)
    return pack, unpack


def move_frames(edge_cells, corner_cells, pack, unpack):
    number, _, length, channels = edge_cells.shape
    frame = jnp.concatenate(
        [edge_cells.reshape(-1, channels), corner_cells.reshape(-1, channels)], axis=0
    )
    sent = jnp.dot(pack, frame, preferred_element_type=jnp.float32).astype(jnp.bfloat16)
    got = lax.all_to_all(sent, "tile", 0, 0, tiled=True)
    out = jnp.dot(
        unpack, jnp.concatenate([got, frame], axis=0), preferred_element_type=jnp.float32
    ).astype(jnp.bfloat16)
    strips = 4 * number * length
    return (
        out[:strips].reshape(number, 4, length, channels),
        out[strips:].reshape(number, 4, channels),
    )


sizes = {"x": 4, "y": 4, "z": 8, "core": 2}


def place_of(x, y, z, core):
    return ((y * 2 + z % 2) * 4 + x) * 8 + (z // 2) * 2 + core


def shifted(values, axis, by):
    pairs = []
    for x in range(4):
        for y in range(4):
            for z in range(8):
                for core in range(2):
                    at = {"x": x, "y": y, "z": z, "core": core}
                    to = dict(at)
                    to[axis] = (at[axis] + by) % sizes[axis]
                    pairs.append((place_of(**at), place_of(**to)))
    return lax.ppermute(values, ("tile", "ens"), pairs)


def coordinates():
    tile = lax.axis_index("tile")
    ens = lax.axis_index("ens")
    return {
        "x": tile % 4,
        "y": tile // 8,
        "z": (ens // 2) * 2 + (tile // 4) % 2,
        "core": ens % 2,
    }


def pool_halves(values, where, pick):
    lanes = values.shape[-1] // 2
    low, high = values[..., :lanes], values[..., lanes:]
    parts = []
    for k in range(4):
        part = jnp.where(pick((where["x"] + k) % 4) == 0, low, high)
        parts.append(shifted(part, "x", k) if k else part)
    return parts


def slope_kernel(core_ref, *refs):
    pads, grads = refs[:4], refs[4:8]
    kept_ref, sent_ref, wide, total = refs[8:]
    for n in range(4):
        wide[3 * n : 3 * n + 3] = pads[n][...].astype(jnp.float32)
    flat = jnp.concatenate(
        [g[...].astype(jnp.float32).reshape(192, 128) for g in grads], axis=0
    ).astype(jnp.bfloat16)
    low = core_ref[0] == 0
    for across in range(3):
        columns = wide[:, :, across : across + 8, :]
        for down in range(3):
            window = columns[:, down : down + 8].reshape(768, 128).astype(jnp.bfloat16)
            out = lax.dot_general(
                window, flat, (((0,), (0,)), ((), ())), preferred_element_type=jnp.float32
            )
            tap = (3 * down + across) * 64
            total[0, tap : tap + 64] = jnp.where(low, out[:64], out[64:])
            total[1, tap : tap + 64] = jnp.where(low, out[64:], out[:64])
    for j in range(32):
        kept_ref[j] = total[0, 18 * j : 18 * j + 18]
        sent_ref[j] = total[1, 18 * j : 18 * j + 18]


def slope_terms(pads, grads, where):
    shape = jax.ShapeDtypeStruct((32, 18, 128), jnp.float32)
    vmem = pl.BlockSpec(memory_space=pltpu.VMEM)
    kept, sent = pl.pallas_call(
        slope_kernel,
        out_shape=(shape, shape),
        in_specs=[pl.BlockSpec(memory_space=pltpu.SMEM)] + [vmem] * 8,
        out_specs=(vmem, vmem),
        scratch_shapes=[
            pltpu.VMEM((12, 10, 10, 128), jnp.float32),
            pltpu.VMEM((2, 576, 128), jnp.float32),
        ],
        compiler_params=pltpu.CompilerParams(vmem_limit_bytes=40 * 2**20),
        cost_estimate=pl.CostEstimate(
            flops=2 * 9 * 768 * 128 * 128, bytes_accessed=2000000, transcendentals=0
        ),
        name="slope_terms",
    )(jnp.reshape(where["core"], (1,)), *pads, *grads)
    return kept + shifted(sent, "core", 1)


def spread_kernel(x_ref, *refs):
    parts = refs[:8]
    first_ref, second_ref, total = refs[8:]
    x, core = x_ref[0], x_ref[1]
    for k in range(4):
        quarter = lax.rem(x + 4 - k, 4)
        column = pl.multiple_of(lax.rem(quarter, 2) * 128, 128)
        for other in range(2):
            side = core if other == 0 else 1 - core
            row = pl.multiple_of((quarter // 2) * 128 + side * 64, 64)
            for j in range(32):
                piece = parts[4 * other + k][j].astype(jnp.float32)
                total[0, 18 * j : 18 * j + 18] = piece[:18]
                total[1, 18 * j : 18 * j + 18] = piece[18:36]
            first_ref[:, pl.ds(row, 64), pl.ds(column, 128)] = total[0].reshape(9, 64, 128)
            second_ref[:, pl.ds(row, 64), pl.ds(column, 128)] = total[1].reshape(9, 64, 128)


def spread_slopes(parts, where):
    shape = jax.ShapeDtypeStruct((9, 256, 256), jnp.float32)
    vmem = pl.BlockSpec(memory_space=pltpu.VMEM)
    return pl.pallas_call(
        spread_kernel,
        out_shape=(shape, shape),
        in_specs=[pl.BlockSpec(memory_space=pltpu.SMEM)] + [vmem] * 8,
        out_specs=(vmem, vmem),
        scratch_shapes=[pltpu.VMEM((2, 576, 128), jnp.float32)],
        compiler_params=pltpu.CompilerParams(vmem_limit_bytes=40 * 2**20),
        cost_estimate=pl.CostEstimate(flops=1000, bytes_accessed=7000000, transcendentals=0),
        name="spread_slopes",
    )(jnp.stack([where["x"], where["core"]]), *parts)


def plane_groups():
    return [
        [place_of(x, y, z, core) for y in range(4) for z in range(8)]
        for x in range(4)
        for core in range(2)
    ]


def plane_exchange(values):
    return lax.all_to_all(
        values, ("tile", "ens"), 0, 0, axis_index_groups=plane_groups(), tiled=True
    )


def finish_slopes(first, second, scale, where):
    terms = plane_exchange(jnp.concatenate([first, second], axis=-1))
    mine = jnp.sum(terms, axis=0) * scale
    mine = jnp.concatenate([mine[:, :128], mine[:, 128:]], axis=0).astype(jnp.bfloat16)
    plane = plane_exchange(jnp.broadcast_to(mine[None], (32,) + mine.shape))
    own = [plane] + [shifted(plane, "x", k) for k in range(1, 4)]
    other = [shifted(part, "core", 1) for part in own]
    return spread_slopes(own + other, where)


def with_ghosts(values, ghost_rows, ghost_corners, tile_links):
    length = values.shape[1]
    widened = ghost_rows.astype(jnp.float32)
    meeting = tile_links[:, 12:16]
    blended = jnp.stack(
        [
            0.5 * (widened[:, 0, 0] + widened[:, 3, 0]),
            0.5 * (widened[:, 0, length - 1] + widened[:, 1, 0]),
            0.5 * (widened[:, 1, length - 1] + widened[:, 2, length - 1]),
            0.5 * (widened[:, 2, 0] + widened[:, 3, length - 1]),
        ],
        axis=1,
    )
    corner = jnp.where(
        (meeting == 4)[:, :, None], ghost_corners.astype(jnp.float32), blended
    ).astype(values.dtype)
    middle = jnp.concatenate(
        [ghost_rows[:, 3][:, :, None], values, ghost_rows[:, 1][:, :, None]], axis=2
    )
    top_row = jnp.concatenate(
        [corner[:, 0][:, None], ghost_rows[:, 0], corner[:, 1][:, None]], axis=1
    )
    bottom = jnp.concatenate(
        [corner[:, 3][:, None], ghost_rows[:, 2], corner[:, 2][:, None]], axis=1
    )
    return jnp.concatenate([top_row[:, None], middle, bottom[:, None]], axis=1)


def ghost_grads(full, tile_links):
    length = full.shape[1] - 2
    meeting = tile_links[:, 12:16]
    corners = jnp.stack(
        [
            full[:, 0, 0],
            full[:, 0, length + 1],
            full[:, length + 1, length + 1],
            full[:, length + 1, 0],
        ],
        axis=1,
    )
    half_corner = jnp.where((meeting == 3)[:, :, None], 0.5 * corners, jnp.zeros_like(corners))
    north_row = (
        full[:, 0, 1 : length + 1]
        .at[:, 0]
        .add(half_corner[:, 0])
        .at[:, length - 1]
        .add(half_corner[:, 1])
    )
    east_column = (
        full[:, 1 : length + 1, length + 1]
        .at[:, 0]
        .add(half_corner[:, 1])
        .at[:, length - 1]
        .add(half_corner[:, 2])
    )
    south_row = (
        full[:, length + 1, 1 : length + 1]
        .at[:, length - 1]
        .add(half_corner[:, 2])
        .at[:, 0]
        .add(half_corner[:, 3])
    )
    west_column = (
        full[:, 1 : length + 1, 0]
        .at[:, 0]
        .add(half_corner[:, 0])
        .at[:, length - 1]
        .add(half_corner[:, 3])
    )
    edge_cells = jnp.stack([north_row, east_column, south_row, west_column], axis=1).astype(
        jnp.bfloat16
    )
    kept = jnp.where((meeting == 4)[:, :, None], corners, jnp.zeros_like(corners)).astype(
        jnp.bfloat16
    )
    return (edge_cells, kept)


def add_returns(full, ghost_rows, ghost_corners):
    length = full.shape[1] - 2
    interior = full[:, 1 : length + 1, 1 : length + 1]
    ghost_rows = ghost_rows.astype(jnp.float32)
    ghost_corners = ghost_corners.astype(jnp.float32)
    interior = interior.at[:, 0, :].add(ghost_rows[:, 0])
    interior = interior.at[:, :, length - 1].add(ghost_rows[:, 1])
    interior = interior.at[:, length - 1, :].add(ghost_rows[:, 2])
    interior = interior.at[:, :, 0].add(ghost_rows[:, 3])
    interior = interior.at[:, 0, 0].add(ghost_corners[:, 0])
    interior = interior.at[:, 0, length - 1].add(ghost_corners[:, 1])
    interior = interior.at[:, length - 1, length - 1].add(ghost_corners[:, 2])
    interior = interior.at[:, length - 1, 0].add(ghost_corners[:, 3])
    return interior


def convolve(padded, kernel):
    return lax.conv_general_dilated(
        padded,
        kernel,
        (1, 1),
        "VALID",
        dimension_numbers=layout_names,
        preferred_element_type=jnp.float32,
    )


def spread_back(gradient, kernel):
    turned_kernel = jnp.transpose(kernel[::-1, ::-1], (0, 1, 3, 2))
    return lax.conv_general_dilated(
        gradient,
        turned_kernel,
        (1, 1),
        ((2, 2), (2, 2)),
        dimension_numbers=layout_names,
        preferred_element_type=jnp.float32,
    )


def per_device(network_conditions, subsequent_targets, w_first, w_second, tile_links):
    field_here = network_conditions[0]
    goal_here = subsequent_targets[0]
    number = field_here.shape[0]
    length = field_here.shape[1]
    gradient_scale = 1.0 / math.sqrt(
        lax.axis_size("ens") * lax.axis_size("tile") * number * length * length
    )
    pack, unpack = routes(tile_links)
    edge_cells, corner_cells = rim_frame(field_here)
    ghost_rows, ghost_corners = move_frames(edge_cells, corner_cells, pack, unpack)
    field_pad = with_ghosts(field_here, ghost_rows, ghost_corners, tile_links)
    where = coordinates()
    field_parts = pool_halves(field_pad, where, lambda x: x // 2)
    pre_first = convolve(field_pad, w_first)
    hidden = gelu_value(pre_first).astype(jnp.bfloat16)
    edge_cells, corner_cells = rim_frame(hidden)
    ghost_rows, ghost_corners = move_frames(edge_cells, corner_cells, pack, unpack)
    hidden_pad = with_ghosts(hidden, ghost_rows, ghost_corners, tile_links)
    pre_second = convolve(hidden_pad, w_second)
    estimated_states = field_here.astype(jnp.float32) + pre_second
    layer_prognosis = estimated_states.astype(jnp.bfloat16)
    misfit = estimated_states - goal_here.astype(jnp.float32)
    misfit_low = misfit.astype(jnp.bfloat16)
    closing_terms = slope_terms(
        pool_halves(hidden_pad, where, lambda x: x // 2),
        pool_halves(misfit_low, where, lambda x: x % 2),
        where,
    )
    spread = spread_back(misfit_low, w_second)
    edge_cells, corner_cells = ghost_grads(spread, tile_links)
    ghost_rows, ghost_corners = move_frames(edge_cells, corner_cells, pack, unpack)
    hidden_grad = add_returns(spread, ghost_rows, ghost_corners)
    first_low = (hidden_grad * gelu_slope(pre_first)).astype(jnp.bfloat16)
    opening_terms = slope_terms(
        field_parts, pool_halves(first_low, where, lambda x: x % 2), where
    )
    slopes = finish_slopes(opening_terms, closing_terms, gradient_scale, where)
    spread = spread_back(first_low, w_first)
    edge_cells, corner_cells = ghost_grads(spread, tile_links)
    ghost_rows, ghost_corners = move_frames(edge_cells, corner_cells, pack, unpack)
    condition_derivative = misfit + add_returns(spread, ghost_rows, ghost_corners)
    return (
        layer_prognosis[None],
        condition_derivative[None],
        slopes[0].reshape(w_first.shape),
        slopes[1].reshape(w_second.shape),
    )


def solution(mesh):
    return jax.shard_map(
        per_device,
        mesh=mesh,
        in_specs=(
            P("ens", "tile", None, None, None),
            P("ens", "tile", None, None, None),
            P(),
            P(),
            P("tile", None),
        ),
        out_specs=(
            P("ens", "tile", None, None, None),
            P("ens", "tile", None, None, None),
            P(),
            P(),
        ),
        check_vma=False,
    )
```

```python
import math

import jax
import jax.numpy as jnp
from jax import lax
from jax.experimental import pallas as pl
from jax.experimental.pallas import tpu as pltpu
from jax.sharding import PartitionSpec as P

tanh_scale = 0.7978845608028654
cubic_term = 0.044715
slot_rows = 32
send_rows = 1024
bf16, f32 = jnp.bfloat16, jnp.float32


def gelu_value(inputs):
    return (
        0.5
        * inputs
        * (1.0 + jnp.tanh(tanh_scale * (inputs + cubic_term * inputs * inputs * inputs)))
    )


def gelu_slope(inputs):
    tangent = jnp.tanh(tanh_scale * (inputs + cubic_term * inputs * inputs * inputs))
    return 0.5 * (1.0 + tangent) + 0.5 * inputs * (1.0 - tangent * tangent) * tanh_scale * (
        1.0 + 3.0 * cubic_term * inputs * inputs
    )


sizes = {"x": 4, "y": 4, "z": 8, "core": 2}


def place_of(x, y, z, core):
    return ((y * 2 + z % 2) * 4 + x) * 8 + (z // 2) * 2 + core


def shifted(values, axis, by):
    pairs = []
    for x in range(4):
        for y in range(4):
            for z in range(8):
                for core in range(2):
                    at = {"x": x, "y": y, "z": z, "core": core}
                    to = dict(at)
                    to[axis] = (at[axis] + by) % sizes[axis]
                    pairs.append((place_of(**at), place_of(**to)))
    return lax.ppermute(values, ("tile", "ens"), pairs)


def coordinates():
    tile = lax.axis_index("tile")
    ens = lax.axis_index("ens")
    return {
        "x": tile % 4,
        "y": tile // 8,
        "z": (ens // 2) * 2 + (tile // 4) % 2,
        "core": ens % 2,
    }


edge_starts = ((0, 3), (0, 1), (1, 2), (2, 3))
corner_ends = ((0, 0), (7, 0), (7, 7), (0, 7))
corner_cells = ((0, 0), (0, 1), (1, 1), (1, 0))
strips = [(tile, edge) for tile in range(3) for edge in range(4)]


def edge_slices(tile, edge, low, high):
    inner = slice(1, 9)
    return (
        (tile, low, inner),
        (tile, inner, high),
        (tile, high, inner),
        (tile, inner, low),
    )[edge]


def corner_at(corner, low, high):
    down, across = corner_cells[corner]
    return (high if down else low), (high if across else low)


def take_frame(grid, frame, links, low, high, kept):
    for i, (tile, edge) in enumerate(strips):
        frame[8 * i : 8 * i + 8] = grid[edge_slices(tile, edge, low, high)]
    for tile in range(3):
        for corner in range(4):
            row, column = corner_at(corner, low, high)
            cell = grid[tile, row, column : column + 1, :]
            if kept:
                cell = jnp.where(links[tile, 12 + corner] == 4, cell, 0.0)
            at = 96 + 4 * tile + corner
            frame[at : at + 1] = cell
    frame[108:128] = jnp.zeros((20, 256), f32)


def fill_ghosts(grid, got, links):
    for i, (tile, edge) in enumerate(strips):
        grid[edge_slices(tile, edge, 0, 9)] = got[8 * i : 8 * i + 8]
    for tile in range(3):
        for corner in range(4):
            row, column = corner_at(corner, 0, 9)
            at = 96 + 4 * tile + corner
            beside = [
                8 * (4 * tile + edge) + end
                for edge, end in zip(edge_starts[corner], corner_ends[corner])
            ]
            blend = 0.5 * (got[beside[0] : beside[0] + 1] + got[beside[1] : beside[1] + 1])
            grid[tile, row, column : column + 1, :] = jnp.where(
                links[tile, 12 + corner] == 4, got[at : at + 1], blend
            )


def split_corners(grid, links):
    for tile in range(3):
        for corner in range(4):
            row, column = corner_at(corner, 0, 9)
            near_row, near_column = corner_at(corner, 1, 8)
            cell = grid[tile, row, column : column + 1, :]
            half = jnp.where(links[tile, 12 + corner] == 3, 0.5 * cell, 0.0)
            grid[tile, row, near_column : near_column + 1, :] += half
            grid[tile, near_row, column : column + 1, :] += half


def add_returns(grid, got):
    for i, (tile, edge) in enumerate(strips):
        grid[edge_slices(tile, edge, 1, 8)] += got[8 * i : 8 * i + 8]
    for tile in range(3):
        for corner in range(4):
            row, column = corner_at(corner, 1, 8)
            at = 96 + 4 * tile + corner
            grid[tile, row, column : column + 1, :] += got[at : at + 1]


def pack_frame(pack_ref, frame, frame_ref, sent_ref):
    cells = frame[...].astype(bf16)
    frame_ref[...] = cells
    sent_ref[...] = jnp.dot(pack_ref[...], cells, preferred_element_type=f32).astype(bf16)


def unpack_frame(unpack_ref, recv_ref, frame_ref, got):
    got[...] = jnp.dot(
        unpack_ref[:, :send_rows], recv_ref[...], preferred_element_type=f32
    ) + jnp.dot(unpack_ref[:, send_rows:], frame_ref[...], preferred_element_type=f32)


def convolve(grid, weights):
    total = jnp.zeros((192, 256), f32)
    for across in range(3):
        columns = grid[:, :, across : across + 8, :]
        for down in range(3):
            window = columns[:, down : down + 8].reshape(192, 256).astype(bf16)
            total += jnp.dot(window, weights[3 * down + across], preferred_element_type=f32)
    return total


def spread_back(gradient, weights, grid, column):
    grid[...] = jnp.zeros_like(grid)
    for across in range(3):
        column[...] = jnp.zeros_like(column)
        for down in range(3):
            part = lax.dot_general(
                gradient,
                weights[3 * down + across],
                (((1,), (1,)), ((), ())),
                preferred_element_type=f32,
            )
            column[:, down : down + 8] += part.reshape(3, 8, 8, 256)
        grid[:, :, across : across + 8, :] += column[...]


def halves(place, flat, pick):
    for k in range(4):
        quarter = lax.rem(place[1] + k, 4)
        side = quarter // 2 if pick == 0 else lax.rem(quarter, 2)
        yield k, jnp.where(side == 0, flat[:, :128], flat[:, 128:]).astype(bf16)


def flatten_grid(grid, flat):
    flat[300:304] = jnp.zeros((4, 256), f32)
    for tile in range(3):
        for row in range(10):
            at = 100 * tile + 10 * row
            flat[at : at + 10] = grid[tile, row]


def route_kernel(links, place, field_ref, pack_ref, unpack_ref, frame_ref, sent_ref, grid, frame):
    here = place[0]

    def rows_of(tiles, sides, valid, base, width, local_base):
        device = [tile // 3 for tile in tiles]
        source = [lax.rem(tile, 3) * 4 + side for tile, side in zip(tiles, sides)]
        out = []
        for i in range(12):
            send_rank = take_rank = jnp.int32(0)
            for j in range(12):
                near = (device[j] == device[i]) & valid[j]
                if j < i:
                    send_rank += jnp.where(near, width, 0)
                if j != i:
                    take_rank += jnp.where(near & (source[j] < source[i]), width, 0)
            first = device[i] * slot_rows + base
            own = device[i] == here
            send = jnp.where(own | ~valid[i], -1000, first + send_rank)
            take = jnp.where(own, local_base + source[i] * width, first + take_rank)
            out.append((send, jnp.where(valid[i], take, -1000)))
        return out

    codes = [links[tile, 4 + edge] for tile, edge in strips]
    edges = rows_of(
        [links[tile, edge] for tile, edge in strips],
        [lax.rem(code, 4) for code in codes],
        [links[tile, edge] >= 0 for tile, edge in strips],
        0,
        8,
        send_rows,
    )
    across = [links[tile, 8 + corner] for tile, corner in strips]
    corners = rows_of(
        [jnp.maximum(c, 0) // 4 for c in across],
        [lax.rem(jnp.maximum(c, 0), 4) for c in across],
        [c >= 0 for c in across],
        24,
        1,
        send_rows + 96,
    )
    lane = lax.broadcasted_iota(jnp.int32, (8, 128), 1)
    row = lax.broadcasted_iota(jnp.int32, (128, 128), 0)
    send = jnp.full((8, 128), -1000, jnp.int32)
    take = jnp.full((128, 128), -1000, jnp.int32)
    for i in range(12):
        send = jnp.where(lane // 8 == i, edges[i][0] + lane % 8, send)
        send = jnp.where(lane == 96 + i, corners[i][0], send)
        turned = codes[i] // 4 == 1
        step = jnp.where(turned, 7 - row % 8, row % 8)
        take = jnp.where(row // 8 == i, edges[i][1] + step, take)
        take = jnp.where(row == 96 + i, corners[i][1], take)
    slot = lax.broadcasted_iota(jnp.int32, (send_rows, 128), 0)
    pack_ref[...] = jnp.where(slot == send[:1], 1.0, 0.0).astype(bf16)
    column = lax.broadcasted_iota(jnp.int32, (128, 128), 1)
    for m in range(9):
        unpack_ref[:, 128 * m : 128 * m + 128] = jnp.where(
            take == column + 128 * m, 1.0, 0.0
        ).astype(bf16)
    grid[:, 1:9, 1:9, :] = field_ref[...].astype(f32)
    take_frame(grid, frame, links, 1, 8, False)
    pack_frame(pack_ref, frame, frame_ref, sent_ref)


def first_kernel(
    links, place, field_ref, recv_ref, old_ref, pack_ref, unpack_ref, weights,
    hidden_ref, pre_ref, frame_ref, sent_ref, part0, part1, part2, part3,
    grid, frame, got, flat,
):
    unpack_frame(unpack_ref, recv_ref, old_ref, got)
    grid[:, 1:9, 1:9, :] = field_ref[...].astype(f32)
    fill_ghosts(grid, got, links)
    pre_first = convolve(grid, weights)
    pre_ref[...] = pre_first
    hidden = gelu_value(pre_first).astype(bf16)
    hidden_ref[...] = hidden
    flatten_grid(grid, flat)
    grid[:, 1:9, 1:9, :] = hidden.astype(f32).reshape(3, 8, 8, 256)
    take_frame(grid, frame, links, 1, 8, False)
    pack_frame(pack_ref, frame, frame_ref, sent_ref)
    parts = (part0, part1, part2, part3)
    for k, half in halves(place, flat, 0):
        parts[k][...] = half


def second_kernel(
    links, place, field_ref, goal_ref, hidden_ref, recv_ref, old_ref, pack_ref, unpack_ref, weights,
    held0, held1, held2,
    state_ref, misfit_ref, inner_ref, frame_ref, sent_ref, part0, part1, part2, part3,
    grid, frame, got, flat, column,
):
    unpack_frame(unpack_ref, recv_ref, old_ref, got)
    grid[:, 1:9, 1:9, :] = hidden_ref[...].astype(f32).reshape(3, 8, 8, 256)
    fill_ghosts(grid, got, links)
    states = field_ref[...].astype(f32).reshape(192, 256) + convolve(grid, weights)
    state_ref[...] = states.reshape(3, 8, 8, 256).astype(bf16)
    misfit = states - goal_ref[...].astype(f32).reshape(192, 256)
    misfit_ref[...] = misfit
    low = misfit.astype(bf16)
    flatten_grid(grid, flat)
    spread_back(low, weights, grid, column)
    split_corners(grid, links)
    take_frame(grid, frame, links, 0, 9, True)
    pack_frame(pack_ref, frame, frame_ref, sent_ref)
    inner_ref[...] = grid[:, 1:9, 1:9, :]
    parts = (part0, part1, part2, part3)
    for k, half in halves(place, flat, 0):
        parts[k][:304] = half
    for k, half in halves(place, low.astype(f32), 1):
        parts[k][304:] = half


def third_kernel(
    links, place, inner_ref, pre_ref, recv_ref, old_ref, pack_ref, unpack_ref, weights, held,
    last_ref, frame_ref, sent_ref, part0, part1, part2, part3,
    grid, frame, got, column,
):
    unpack_frame(unpack_ref, recv_ref, old_ref, got)
    grid[:, 1:9, 1:9, :] = inner_ref[...]
    add_returns(grid, got)
    hidden_grad = grid[:, 1:9, 1:9, :].reshape(192, 256)
    low = (hidden_grad * gelu_slope(pre_ref[...])).astype(bf16)
    parts = (part0, part1, part2, part3)
    for k, half in halves(place, low.astype(f32), 1):
        parts[k][...] = half
    spread_back(low, weights, grid, column)
    split_corners(grid, links)
    take_frame(grid, frame, links, 0, 9, True)
    pack_frame(pack_ref, frame, frame_ref, sent_ref)
    last_ref[...] = grid[:, 1:9, 1:9, :]


def last_kernel(last_ref, misfit_ref, recv_ref, old_ref, unpack_ref, out_ref, grid, got):
    unpack_frame(unpack_ref, recv_ref, old_ref, got)
    grid[:, 1:9, 1:9, :] = last_ref[...] + misfit_ref[...].reshape(3, 8, 8, 256)
    add_returns(grid, got)
    out_ref[...] = grid[:, 1:9, 1:9, :]


vmem = pl.BlockSpec(memory_space=pltpu.VMEM)
smem = pl.BlockSpec(memory_space=pltpu.SMEM)
left = pl.BlockSpec(memory_space=pl.ANY)
grid_shape = pltpu.VMEM((3, 10, 10, 256), f32)
frame_shape = pltpu.VMEM((128, 256), f32)
flat_shape = pltpu.VMEM((304, 256), f32)
column_shape = pltpu.VMEM((3, 10, 8, 256), f32)


def like(*shape, dtype=bf16):
    return jax.ShapeDtypeStruct(shape, dtype)


def run(kernel, name, args, specs, outs, scratch, flops):
    return pl.pallas_call(
        kernel,
        out_shape=outs,
        in_specs=specs,
        out_specs=jax.tree.map(lambda _: vmem, outs),
        scratch_shapes=scratch,
        compiler_params=pltpu.CompilerParams(vmem_limit_bytes=40 * 2**20),
        cost_estimate=pl.CostEstimate(flops=flops, bytes_accessed=3000000, transcendentals=0),
        name=name,
    )(*args)


def slope_kernel(split, place, *refs):
    count = 4 if split else 8
    parts = refs[:count]
    kept_ref, sent_ref, flat, wide, total = refs[count:]
    grads = []
    for n in range(4):
        flat[304 * n : 304 * n + 304] = parts[n][:304].astype(f32)
        grads.append(parts[n][304:] if split else parts[4 + n][...])
    grads = jnp.concatenate(grads, axis=0)
    low = place[2] == 0
    for across in range(3):
        for n in range(4):
            for tile in range(3):
                for row in range(10):
                    at = 304 * n + 100 * tile + 10 * row + across
                    wide[3 * n + tile, row] = flat[at : at + 8]
        for down in range(3):
            window = wide[:, down : down + 8].reshape(768, 128).astype(bf16)
            out = lax.dot_general(
                window, grads, (((0,), (0,)), ((), ())), preferred_element_type=f32
            )
            tap = (3 * down + across) * 64
            total[0, tap : tap + 64] = jnp.where(low, out[:64], out[64:])
            total[1, tap : tap + 64] = jnp.where(low, out[64:], out[:64])
    for j in range(32):
        kept_ref[j] = total[0, 18 * j : 18 * j + 18]
        sent_ref[j] = total[1, 18 * j : 18 * j + 18]


def slope_terms(parts, place, split):
    shape = like(32, 18, 128, dtype=f32)

    def kernel(*refs):
        slope_kernel(split, *refs)

    return run(
        kernel,
        "slope_terms",
        (place, *parts),
        [smem] + [vmem] * len(parts),
        (shape, shape),
        [
            pltpu.VMEM((1216, 128), f32),
            pltpu.VMEM((12, 10, 8, 128), f32),
            pltpu.VMEM((2, 576, 128), f32),
        ],
        2 * 9 * 768 * 128 * 128,
    )


def ring(parts, axis):
    return [shifted(part, axis, k) if k else part for k, part in enumerate(parts)]


def spread_kernel(place, *refs):
    parts = refs[:8]
    first_ref, second_ref, total = refs[8:]
    x, core = place[1], place[2]
    for k in range(4):
        quarter = lax.rem(x + 4 - k, 4)
        column = pl.multiple_of(lax.rem(quarter, 2) * 128, 128)
        for other in range(2):
            side = core if other == 0 else 1 - core
            row = pl.multiple_of((quarter // 2) * 128 + side * 64, 64)
            for j in range(32):
                piece = parts[4 * other + k][j].astype(jnp.float32)
                total[0, 18 * j : 18 * j + 18] = piece[:18]
                total[1, 18 * j : 18 * j + 18] = piece[18:36]
            first_ref[:, pl.ds(row, 64), pl.ds(column, 128)] = total[0].reshape(9, 64, 128)
            second_ref[:, pl.ds(row, 64), pl.ds(column, 128)] = total[1].reshape(9, 64, 128)


def spread_slopes(parts, place):
    shape = like(9, 256, 256, dtype=f32)
    return run(
        spread_kernel,
        "spread_slopes",
        (place, *parts),
        [smem] + [vmem] * 8,
        (shape, shape),
        [pltpu.VMEM((2, 576, 128), f32)],
        1000,
    )


def plane_groups():
    return [
        [place_of(x, y, z, core) for y in range(4) for z in range(8)]
        for x in range(4)
        for core in range(2)
    ]


def plane_exchange(values):
    return lax.all_to_all(
        values, ("tile", "ens"), 0, 0, axis_index_groups=plane_groups(), tiled=True
    )


def finish_slopes(first, second, scale, place):
    terms = plane_exchange(jnp.concatenate([first, second], axis=-1))
    mine = jnp.sum(terms, axis=0) * scale
    mine = jnp.concatenate([mine[:, :128], mine[:, 128:]], axis=0).astype(jnp.bfloat16)
    plane = plane_exchange(jnp.broadcast_to(mine[None], (32,) + mine.shape))
    own = [plane] + [shifted(plane, "x", k) for k in range(1, 4)]
    other = [shifted(part, "core", 1) for part in own]
    return spread_slopes(own + other, place)


def exchange(values):
    return lax.all_to_all(values, "tile", 0, 0, tiled=True)


def per_device(network_conditions, subsequent_targets, w_first, w_second, tile_links):
    field, goal = network_conditions[0], subsequent_targets[0]
    first_weights, second_weights = w_first.reshape(9, 256, 256), w_second.reshape(9, 256, 256)
    scale = 1.0 / math.sqrt(lax.axis_size("ens") * lax.axis_size("tile") * 192)
    where = coordinates()
    place = jnp.stack([lax.axis_index("tile"), where["x"], where["core"]])
    frame_like, sent_like, rows_like = like(128, 256), like(send_rows, 256), like(192, 256)
    inner_like = like(3, 8, 8, 256, dtype=f32)
    conv_flops = 2 * 9 * 192 * 256 * 256

    pack, unpack, frame, sent = run(
        route_kernel,
        "routes",
        (tile_links, place, field),
        [smem, smem, vmem],
        (like(send_rows, 128), like(128, send_rows + 128), frame_like, sent_like),
        [grid_shape, frame_shape],
        2 * send_rows * 128 * 256,
    )
    recv = exchange(sent)
    hidden, pre_first, frame, sent, *parts = run(
        first_kernel,
        "first_layer",
        (tile_links, place, field, recv, frame, pack, unpack, first_weights),
        [smem, smem] + [vmem] * 6,
        (rows_like, like(192, 256, dtype=f32), frame_like, sent_like) + (like(304, 128),) * 4,
        [grid_shape, frame_shape, frame_shape, flat_shape],
        conv_flops,
    )
    recv = exchange(sent)
    field_parts = ring(parts, "x")
    states, misfit, inner, frame, sent, *parts = run(
        second_kernel,
        "second_layer",
        (
            tile_links, place, field, goal, hidden, recv, frame, pack, unpack, second_weights,
            *field_parts[1:],
        ),
        [smem, smem] + [vmem] * 8 + [left] * 3,
        (like(3, 8, 8, 256), like(192, 256, dtype=f32), inner_like, frame_like, sent_like)
        + (like(496, 128),) * 4,
        [grid_shape, frame_shape, frame_shape, flat_shape, column_shape],
        2 * conv_flops,
    )
    recv = exchange(sent)
    closing, sent_closing = slope_terms(ring(parts, "x"), place, True)
    last, frame, sent, *parts = run(
        third_kernel,
        "first_gradient",
        (tile_links, place, inner, pre_first, recv, frame, pack, unpack, first_weights, closing),
        [smem, smem] + [vmem] * 7 + [left],
        (inner_like, frame_like, sent_like) + (like(192, 128),) * 4,
        [grid_shape, frame_shape, frame_shape, column_shape],
        conv_flops,
    )
    recv = exchange(sent)
    opening, sent_opening = slope_terms(field_parts + ring(parts, "x"), place, False)
    condition_derivative = run(
        last_kernel,
        "last_gradient",
        (last, misfit, recv, frame, unpack),
        [vmem] * 5,
        inner_like,
        [grid_shape, frame_shape],
        1000,
    )
    slopes = finish_slopes(
        opening + shifted(sent_opening, "core", 1),
        closing + shifted(sent_closing, "core", 1),
        scale,
        place,
    )
    return (
        states[None],
        condition_derivative[None],
        slopes[0].reshape(w_first.shape),
        slopes[1].reshape(w_second.shape),
    )


def solution(mesh):
    return jax.shard_map(
        per_device,
        mesh=mesh,
        in_specs=(
            P("ens", "tile", None, None, None),
            P("ens", "tile", None, None, None),
            P(),
            P(),
            P("tile", None),
        ),
        out_specs=(
            P("ens", "tile", None, None, None),
            P("ens", "tile", None, None, None),
            P(),
            P(),
        ),
        check_vma=False,
    )
```

```python
import itertools
import math

import jax
import jax.numpy as jnp
from jax import lax
from jax.experimental import pallas as pl
from jax.experimental.pallas import tpu as pltpu
from jax.sharding import PartitionSpec as P

tanh_scale = 0.7978845608028654
cubic_term = 0.044715
slot_rows = 32
send_rows = 1024
bf16, f32 = jnp.bfloat16, jnp.float32


def gelu_value(inputs):
    return (
        0.5
        * inputs
        * (1.0 + jnp.tanh(tanh_scale * (inputs + cubic_term * inputs * inputs * inputs)))
    )


def gelu_slope(inputs):
    tangent = jnp.tanh(tanh_scale * (inputs + cubic_term * inputs * inputs * inputs))
    return 0.5 * (1.0 + tangent) + 0.5 * inputs * (1.0 - tangent * tangent) * tanh_scale * (
        1.0 + 3.0 * cubic_term * inputs * inputs
    )


sizes = {"x": 4, "y": 4, "z": 8, "core": 2}


def place_of(x, y, z, core):
    return ((y * 2 + z % 2) * 4 + x) * 8 + (z // 2) * 2 + core


def shifted(values, axis, by):
    pairs = []
    for x in range(4):
        for y in range(4):
            for z in range(8):
                for core in range(2):
                    at = {"x": x, "y": y, "z": z, "core": core}
                    to = dict(at)
                    to[axis] = (at[axis] + by) % sizes[axis]
                    pairs.append((place_of(**at), place_of(**to)))
    return lax.ppermute(values, ("tile", "ens"), pairs)


def coordinates():
    tile = lax.axis_index("tile")
    ens = lax.axis_index("ens")
    return {
        "x": tile % 4,
        "y": tile // 8,
        "z": (ens // 2) * 2 + (tile // 4) % 2,
        "core": ens % 2,
    }


edge_starts = ((0, 3), (0, 1), (1, 2), (2, 3))
corner_ends = ((0, 0), (7, 0), (7, 7), (0, 7))
corner_cells = ((0, 0), (0, 1), (1, 1), (1, 0))
strips = [(tile, edge) for tile in range(3) for edge in range(4)]


def edge_slices(tile, edge, low, high):
    inner = slice(1, 9)
    return (
        (tile, low, inner),
        (tile, inner, high),
        (tile, high, inner),
        (tile, inner, low),
    )[edge]


def corner_at(corner, low, high):
    down, across = corner_cells[corner]
    return (high if down else low), (high if across else low)


def take_frame(grid, frame, links, low, high, kept):
    for i, (tile, edge) in enumerate(strips):
        frame[8 * i : 8 * i + 8] = grid[edge_slices(tile, edge, low, high)]
    for tile in range(3):
        for corner in range(4):
            row, column = corner_at(corner, low, high)
            cell = grid[tile, row, column : column + 1, :]
            if kept:
                cell = jnp.where(links[tile, 12 + corner] == 4, cell, 0.0)
            at = 96 + 4 * tile + corner
            frame[at : at + 1] = cell
    frame[108:128] = jnp.zeros((20, 256), f32)


def fill_ghosts(grid, got, links):
    for i, (tile, edge) in enumerate(strips):
        grid[edge_slices(tile, edge, 0, 9)] = got[8 * i : 8 * i + 8]
    for tile in range(3):
        for corner in range(4):
            row, column = corner_at(corner, 0, 9)
            at = 96 + 4 * tile + corner
            beside = [
                8 * (4 * tile + edge) + end
                for edge, end in zip(edge_starts[corner], corner_ends[corner])
            ]
            blend = 0.5 * (got[beside[0] : beside[0] + 1] + got[beside[1] : beside[1] + 1])
            grid[tile, row, column : column + 1, :] = jnp.where(
                links[tile, 12 + corner] == 4, got[at : at + 1], blend
            )


def split_corners(grid, links):
    for tile in range(3):
        for corner in range(4):
            row, column = corner_at(corner, 0, 9)
            near_row, near_column = corner_at(corner, 1, 8)
            cell = grid[tile, row, column : column + 1, :]
            half = jnp.where(links[tile, 12 + corner] == 3, 0.5 * cell, 0.0)
            grid[tile, row, near_column : near_column + 1, :] += half
            grid[tile, near_row, column : column + 1, :] += half


def add_returns(grid, got):
    for i, (tile, edge) in enumerate(strips):
        grid[edge_slices(tile, edge, 1, 8)] += got[8 * i : 8 * i + 8]
    for tile in range(3):
        for corner in range(4):
            row, column = corner_at(corner, 1, 8)
            at = 96 + 4 * tile + corner
            grid[tile, row, column : column + 1, :] += got[at : at + 1]


def pack_frame(pack_ref, frame, frame_ref, sent_ref):
    cells = frame[...].astype(bf16)
    frame_ref[...] = cells
    sent_ref[...] = jnp.dot(pack_ref[...], cells, preferred_element_type=f32).astype(bf16)


def unpack_frame(unpack_ref, recv_ref, frame_ref, got):
    got[...] = jnp.dot(
        unpack_ref[:, :send_rows], recv_ref[...], preferred_element_type=f32
    ) + jnp.dot(unpack_ref[:, send_rows:], frame_ref[...], preferred_element_type=f32)


def convolve(grid, weights):
    total = jnp.zeros((192, 256), f32)
    for across in range(3):
        columns = grid[:, :, across : across + 8, :]
        for down in range(3):
            window = columns[:, down : down + 8].reshape(192, 256).astype(bf16)
            total += jnp.dot(window, weights[3 * down + across], preferred_element_type=f32)
    return total


def spread_back(gradient, weights, grid, column):
    grid[...] = jnp.zeros_like(grid)
    for across in range(3):
        column[...] = jnp.zeros_like(column)
        for down in range(3):
            part = lax.dot_general(
                gradient,
                weights[3 * down + across],
                (((1,), (1,)), ((), ())),
                preferred_element_type=f32,
            )
            column[:, down : down + 8] += part.reshape(3, 8, 8, 256)
        grid[:, :, across : across + 8, :] += column[...]


def halves(place, flat, pick):
    for k in range(4):
        quarter = lax.rem(place[1] + k, 4)
        side = quarter // 2 if pick == 0 else lax.rem(quarter, 2)
        yield k, jnp.where(side == 0, flat[:, :128], flat[:, 128:]).astype(bf16)


def flatten_grid(grid, flat):
    flat[300:304] = jnp.zeros((4, 256), f32)
    for tile in range(3):
        for row in range(10):
            at = 100 * tile + 10 * row
            flat[at : at + 10] = grid[tile, row]


def route_kernel(links, place, field_ref, pack_ref, unpack_ref, frame_ref, sent_ref, grid, frame):
    here = place[0]

    def rows_of(tiles, sides, valid, base, width, local_base):
        device = [tile // 3 for tile in tiles]
        source = [lax.rem(tile, 3) * 4 + side for tile, side in zip(tiles, sides)]
        out = []
        for i in range(12):
            send_rank = take_rank = jnp.int32(0)
            for j in range(12):
                near = (device[j] == device[i]) & valid[j]
                if j < i:
                    send_rank += jnp.where(near, width, 0)
                if j != i:
                    take_rank += jnp.where(near & (source[j] < source[i]), width, 0)
            first = device[i] * slot_rows + base
            own = device[i] == here
            send = jnp.where(own | ~valid[i], -1000, first + send_rank)
            take = jnp.where(own, local_base + source[i] * width, first + take_rank)
            out.append((send, jnp.where(valid[i], take, -1000)))
        return out

    codes = [links[tile, 4 + edge] for tile, edge in strips]
    edges = rows_of(
        [links[tile, edge] for tile, edge in strips],
        [lax.rem(code, 4) for code in codes],
        [links[tile, edge] >= 0 for tile, edge in strips],
        0,
        8,
        send_rows,
    )
    across = [links[tile, 8 + corner] for tile, corner in strips]
    corners = rows_of(
        [jnp.maximum(c, 0) // 4 for c in across],
        [lax.rem(jnp.maximum(c, 0), 4) for c in across],
        [c >= 0 for c in across],
        24,
        1,
        send_rows + 96,
    )
    lane = lax.broadcasted_iota(jnp.int32, (8, 128), 1)
    row = lax.broadcasted_iota(jnp.int32, (128, 128), 0)
    send = jnp.full((8, 128), -1000, jnp.int32)
    take = jnp.full((128, 128), -1000, jnp.int32)
    for i in range(12):
        send = jnp.where(lane // 8 == i, edges[i][0] + lane % 8, send)
        send = jnp.where(lane == 96 + i, corners[i][0], send)
        turned = codes[i] // 4 == 1
        step = jnp.where(turned, 7 - row % 8, row % 8)
        take = jnp.where(row // 8 == i, edges[i][1] + step, take)
        take = jnp.where(row == 96 + i, corners[i][1], take)
    slot = lax.broadcasted_iota(jnp.int32, (send_rows, 128), 0)
    pack_ref[...] = jnp.where(slot == send[:1], 1.0, 0.0).astype(bf16)
    column = lax.broadcasted_iota(jnp.int32, (128, 128), 1)
    for m in range(9):
        unpack_ref[:, 128 * m : 128 * m + 128] = jnp.where(
            take == column + 128 * m, 1.0, 0.0
        ).astype(bf16)
    grid[:, 1:9, 1:9, :] = field_ref[...].astype(f32).reshape(3, 8, 8, 256)
    take_frame(grid, frame, links, 1, 8, False)
    pack_frame(pack_ref, frame, frame_ref, sent_ref)


def first_kernel(
    links, place, field_ref, recv_ref, old_ref, pack_ref, unpack_ref, weights,
    hidden_ref, pre_ref, frame_ref, sent_ref, part0, part1, part2, part3,
    grid, frame, got, flat,
):
    unpack_frame(unpack_ref, recv_ref, old_ref, got)
    grid[:, 1:9, 1:9, :] = field_ref[...].astype(f32).reshape(3, 8, 8, 256)
    fill_ghosts(grid, got, links)
    pre_first = convolve(grid, weights)
    pre_ref[...] = pre_first
    hidden = gelu_value(pre_first).astype(bf16)
    hidden_ref[...] = hidden
    flatten_grid(grid, flat)
    grid[:, 1:9, 1:9, :] = hidden.astype(f32).reshape(3, 8, 8, 256)
    take_frame(grid, frame, links, 1, 8, False)
    pack_frame(pack_ref, frame, frame_ref, sent_ref)
    parts = (part0, part1, part2, part3)
    for k, half in halves(place, flat, 0):
        parts[k][...] = half


def second_kernel(
    links, place, field_ref, goal_ref, hidden_ref, recv_ref, old_ref, pack_ref, unpack_ref, weights,
    held0, held1, held2,
    state_ref, misfit_ref, inner_ref, frame_ref, sent_ref, part0, part1, part2, part3,
    grid, frame, got, flat, column,
):
    unpack_frame(unpack_ref, recv_ref, old_ref, got)
    grid[:, 1:9, 1:9, :] = hidden_ref[...].astype(f32).reshape(3, 8, 8, 256)
    fill_ghosts(grid, got, links)
    states = field_ref[...].astype(f32) + convolve(grid, weights)
    state_ref[...] = states.astype(bf16)
    misfit = states - goal_ref[...].astype(f32)
    misfit_ref[...] = misfit
    low = misfit.astype(bf16)
    flatten_grid(grid, flat)
    spread_back(low, weights, grid, column)
    split_corners(grid, links)
    take_frame(grid, frame, links, 0, 9, True)
    pack_frame(pack_ref, frame, frame_ref, sent_ref)
    inner_ref[...] = grid[:, 1:9, 1:9, :]
    parts = (part0, part1, part2, part3)
    for k, half in halves(place, flat, 0):
        parts[k][:304] = half
    for k, half in halves(place, low.astype(f32), 1):
        parts[k][304:] = half


def third_kernel(
    links, place, inner_ref, pre_ref, recv_ref, old_ref, pack_ref, unpack_ref, weights, held,
    last_ref, frame_ref, sent_ref, part0, part1, part2, part3,
    grid, frame, got, column,
):
    unpack_frame(unpack_ref, recv_ref, old_ref, got)
    grid[:, 1:9, 1:9, :] = inner_ref[...]
    add_returns(grid, got)
    hidden_grad = grid[:, 1:9, 1:9, :].reshape(192, 256)
    low = (hidden_grad * gelu_slope(pre_ref[...])).astype(bf16)
    parts = (part0, part1, part2, part3)
    for k, half in halves(place, low.astype(f32), 1):
        parts[k][...] = half
    spread_back(low, weights, grid, column)
    split_corners(grid, links)
    take_frame(grid, frame, links, 0, 9, True)
    pack_frame(pack_ref, frame, frame_ref, sent_ref)
    last_ref[...] = grid[:, 1:9, 1:9, :]


def last_kernel(last_ref, misfit_ref, recv_ref, old_ref, unpack_ref, out_ref, grid, got):
    unpack_frame(unpack_ref, recv_ref, old_ref, got)
    grid[:, 1:9, 1:9, :] = last_ref[...] + misfit_ref[...].reshape(3, 8, 8, 256)
    add_returns(grid, got)
    out_ref[...] = grid[:, 1:9, 1:9, :]


smem = pl.BlockSpec(memory_space=pltpu.SMEM)
vmem = pl.BlockSpec(memory_space=pltpu.HBM)
left = pl.BlockSpec(memory_space=pl.ANY)
grid_shape = pltpu.VMEM((3, 10, 10, 256), f32)
frame_shape = pltpu.VMEM((128, 256), f32)
flat_shape = pltpu.VMEM((304, 256), f32)
column_shape = pltpu.VMEM((3, 10, 8, 256), f32)


def like(*shape, dtype=bf16):
    return jax.ShapeDtypeStruct(shape, dtype)


def run(kernel, name, args, specs, outs, scratch, flops):
    single = not isinstance(outs, tuple)
    outs = (outs,) if single else outs
    moved = [i for i, spec in enumerate(specs) if spec is vmem]
    buffers = [pltpu.VMEM(args[i].shape, args[i].dtype) for i in moved]
    results = [pltpu.VMEM(out.shape, out.dtype) for out in outs]

    def body(*refs):
        ins, refs = refs[: len(args)], refs[len(args) :]
        targets, refs = refs[: len(outs)], refs[len(outs) :]
        held, refs = refs[: len(moved)], refs[len(moved) :]
        made, refs = refs[: len(outs)], refs[len(outs) :]
        arrived, left_for, refs = refs[0], refs[1], refs[2:]
        copies = [
            pltpu.make_async_copy(ins[i], held[n], arrived.at[n]) for n, i in enumerate(moved)
        ]
        for copy in copies:
            copy.start()
        for copy in copies:
            copy.wait()
        given = list(ins)
        for n, i in enumerate(moved):
            given[i] = held[n]
        kernel(*given, *made, *refs)
        copies = [
            pltpu.make_async_copy(made[n], targets[n], left_for.at[n]) for n in range(len(outs))
        ]
        for copy in copies:
            copy.start()
        for copy in copies:
            copy.wait()

    made = pl.pallas_call(
        body,
        out_shape=outs,
        in_specs=specs,
        out_specs=tuple(vmem for _ in outs),
        scratch_shapes=[
            *buffers,
            *results,
            pltpu.SemaphoreType.DMA((max(1, len(moved)),)),
            pltpu.SemaphoreType.DMA((len(outs),)),
            *scratch,
        ],
        compiler_params=pltpu.CompilerParams(vmem_limit_bytes=40 * 2**20),
        cost_estimate=pl.CostEstimate(flops=flops, bytes_accessed=3000000, transcendentals=0),
        name=name,
    )(*args)
    return made[0] if single else made


def slope_kernel(split, place, *refs):
    count = 4 if split else 8
    parts = refs[:count]
    kept_ref, sent_ref, flat, wide, total = refs[count:]
    grads = []
    for n in range(4):
        flat[304 * n : 304 * n + 304] = parts[n][:304].astype(f32)
        grads.append(parts[n][304:] if split else parts[4 + n][...])
    grads = jnp.concatenate(grads, axis=0)
    low = place[2] == 0
    for across in range(3):
        for n in range(4):
            for tile in range(3):
                for row in range(10):
                    at = 304 * n + 100 * tile + 10 * row + across
                    wide[3 * n + tile, row] = flat[at : at + 8]
        for down in range(3):
            window = wide[:, down : down + 8].reshape(768, 128).astype(bf16)
            out = lax.dot_general(
                window, grads, (((0,), (0,)), ((), ())), preferred_element_type=f32
            )
            tap = (3 * down + across) * 64
            total[0, tap : tap + 64] = jnp.where(low, out[:64], out[64:])
            total[1, tap : tap + 64] = jnp.where(low, out[64:], out[:64])
    for j in range(4):
        kept_ref[j] = total[0, 144 * j : 144 * j + 144]
        sent_ref[j] = total[1, 144 * j : 144 * j + 144]


def slope_terms(parts, place, split):
    shape = like(4, 144, 128, dtype=f32)

    def kernel(*refs):
        slope_kernel(split, *refs)

    return run(
        kernel,
        "slope_terms",
        (place, *parts),
        [smem] + [vmem] * len(parts),
        (shape, shape),
        [
            pltpu.VMEM((1216, 128), f32),
            pltpu.VMEM((12, 10, 8, 128), f32),
            pltpu.VMEM((2, 576, 128), f32),
        ],
        2 * 9 * 768 * 128 * 128,
    )


def ring(parts, axis):
    return [shifted(part, axis, k) if k else part for k, part in enumerate(parts)]


def pair_kernel(place, kept0, got0, kept1, got1, held, *chunks):
    for k in range(4):
        at = lax.rem(place[3] + k, 4)
        chunks[k][:144] = kept0[at] + got0[at]
        chunks[k][144:] = kept1[at] + got1[at]


def plane_kernel(own, part1, part2, part3, out, total):
    total[...] = (own[...] + part1[...]) + (part2[...] + part3[...])
    for j in range(8):
        out[j] = total[36 * j : 36 * j + 36]


def spread_kernel(place, own, other, first_ref, second_ref):
    low = place[2] == 0
    for x in range(4):
        row, column = 128 * (x // 2), 128 * (x % 2)
        for n, out in enumerate((first_ref, second_ref)):
            at = slice(144 * n, 144 * n + 144)
            pair = [
                jnp.concatenate(
                    [part[4 * x + y, at].astype(f32) for y in range(4)], axis=0
                ).reshape(9, 64, 128)
                for part in (own, other)
            ]
            out[:, row : row + 64, column : column + 128] = jnp.where(low, pair[0], pair[1])
            out[:, row + 64 : row + 128, column : column + 128] = jnp.where(low, pair[1], pair[0])


def groups(along):
    axes = ("x", "y", "z", "core")
    out = []
    for fixed in itertools.product(*[range(1 if a in along else sizes[a]) for a in axes]):
        group = []
        for moving in itertools.product(*[range(sizes[a]) for a in along]):
            at = dict(zip(axes, fixed)) | dict(zip(along, moving))
            group.append(place_of(**at))
        out.append(group)
    return out


def trade(values, *along):
    return lax.all_to_all(
        values, ("tile", "ens"), 0, 0, axis_index_groups=groups(along), tiled=True
    )


def copies_of(values, count):
    return jnp.broadcast_to(values[None], (count,) + values.shape)


def finish_slopes(first, second, held, scale, place):
    chunk = like(288, 128, dtype=f32)
    chunks = run(
        pair_kernel,
        "pair_sum",
        (place, first[0], shifted(first[1], "core", 1), *second, held),
        [smem] + [vmem] * 4 + [left],
        (chunk,) * 4,
        [],
        1000,
    )
    terms = run(
        plane_kernel,
        "row_sum",
        tuple(ring(chunks, "y")),
        [vmem] * 4,
        like(8, 36, 128, dtype=f32),
        [pltpu.VMEM((288, 128), f32)],
        1000,
    )
    mine = (jnp.sum(trade(terms, "z"), axis=0) * scale).astype(bf16)
    line = trade(copies_of(mine, 8), "z").reshape(288, 128)
    plane = trade(copies_of(line, 16), "x", "y")
    shape = like(9, 256, 256, dtype=f32)
    return run(
        spread_kernel,
        "spread_slopes",
        (place, plane, shifted(plane, "core", 1)),
        [smem, vmem, vmem],
        (shape, shape),
        [],
        1000,
    )


def exchange(values):
    return lax.all_to_all(values, "tile", 0, 0, tiled=True)


def per_device(network_conditions, subsequent_targets, w_first, w_second, tile_links):
    field = network_conditions.reshape(192, 256)
    goal = subsequent_targets.reshape(192, 256)
    first_weights, second_weights = w_first.reshape(9, 256, 256), w_second.reshape(9, 256, 256)
    scale = 1.0 / math.sqrt(lax.axis_size("ens") * lax.axis_size("tile") * 192)
    where = coordinates()
    place = jnp.stack([lax.axis_index("tile"), where["x"], where["core"], where["y"]])
    frame_like, sent_like, rows_like = like(128, 256), like(send_rows, 256), like(192, 256)
    inner_like = like(3, 8, 8, 256, dtype=f32)
    conv_flops = 2 * 9 * 192 * 256 * 256

    pack, unpack, frame, sent = run(
        route_kernel,
        "routes",
        (tile_links, place, field),
        [smem, smem, vmem],
        (like(send_rows, 128), like(128, send_rows + 128), frame_like, sent_like),
        [grid_shape, frame_shape],
        2 * send_rows * 128 * 256,
    )
    recv = exchange(sent)
    hidden, pre_first, frame, sent, *parts = run(
        first_kernel,
        "first_layer",
        (tile_links, place, field, recv, frame, pack, unpack, first_weights),
        [smem, smem] + [vmem] * 6,
        (rows_like, like(192, 256, dtype=f32), frame_like, sent_like) + (like(304, 128),) * 4,
        [grid_shape, frame_shape, frame_shape, flat_shape],
        conv_flops,
    )
    recv = exchange(sent)
    field_parts = ring(parts, "x")
    states, misfit, inner, frame, sent, *parts = run(
        second_kernel,
        "second_layer",
        (
            tile_links, place, field, goal, hidden, recv, frame, pack, unpack, second_weights,
            *field_parts[1:],
        ),
        [smem, smem] + [vmem] * 8 + [left] * 3,
        (rows_like, like(192, 256, dtype=f32), inner_like, frame_like, sent_like)
        + (like(496, 128),) * 4,
        [grid_shape, frame_shape, frame_shape, flat_shape, column_shape],
        2 * conv_flops,
    )
    recv = exchange(sent)
    closing, sent_closing = slope_terms(ring(parts, "x"), place, True)
    got_closing = shifted(sent_closing, "core", 1)
    last, frame, sent, *parts = run(
        third_kernel,
        "first_gradient",
        (tile_links, place, inner, pre_first, recv, frame, pack, unpack, first_weights, got_closing),
        [smem, smem] + [vmem] * 7 + [left],
        (inner_like, frame_like, sent_like) + (like(192, 128),) * 4,
        [grid_shape, frame_shape, frame_shape, column_shape],
        conv_flops,
    )
    recv = exchange(sent)
    opening = slope_terms(field_parts + ring(parts, "x"), place, False)
    condition_derivative = run(
        last_kernel,
        "last_gradient",
        (last, misfit, recv, frame, unpack),
        [vmem] * 5,
        inner_like,
        [grid_shape, frame_shape],
        1000,
    )
    slopes = finish_slopes(opening, (closing, got_closing), recv, scale, place)
    return (
        states.reshape(network_conditions.shape),
        condition_derivative[None],
        slopes[0].reshape(w_first.shape),
        slopes[1].reshape(w_second.shape),
    )


def solution(mesh):
    return jax.shard_map(
        per_device,
        mesh=mesh,
        in_specs=(
            P("ens", "tile", None, None, None),
            P("ens", "tile", None, None, None),
            P(),
            P(),
            P("tile", None),
        ),
        out_specs=(
            P("ens", "tile", None, None, None),
            P("ens", "tile", None, None, None),
            P(),
            P(),
        ),
        check_vma=False,
    )
```

```python
import itertools
import math

import jax
import jax.numpy as jnp
from jax import lax
from jax.experimental import pallas as pl
from jax.experimental.pallas import tpu as pltpu
from jax.sharding import PartitionSpec as P

tanh_scale = 0.7978845608028654
cubic_term = 0.044715
slot_rows = 32
send_rows = 1024
bf16, f32 = jnp.bfloat16, jnp.float32


def gelu_value(inputs):
    return (
        0.5
        * inputs
        * (1.0 + jnp.tanh(tanh_scale * (inputs + cubic_term * inputs * inputs * inputs)))
    )


def gelu_slope(inputs):
    tangent = jnp.tanh(tanh_scale * (inputs + cubic_term * inputs * inputs * inputs))
    return 0.5 * (1.0 + tangent) + 0.5 * inputs * (1.0 - tangent * tangent) * tanh_scale * (
        1.0 + 3.0 * cubic_term * inputs * inputs
    )


sizes = {"x": 4, "y": 4, "z": 8, "core": 2}


def place_of(x, y, z, core):
    return ((y * 2 + z % 2) * 4 + x) * 8 + (z // 2) * 2 + core


def shifted(values, axis, by):
    pairs = []
    for x in range(4):
        for y in range(4):
            for z in range(8):
                for core in range(2):
                    at = {"x": x, "y": y, "z": z, "core": core}
                    to = dict(at)
                    to[axis] = (at[axis] + by) % sizes[axis]
                    pairs.append((place_of(**at), place_of(**to)))
    return lax.ppermute(values, ("tile", "ens"), pairs)


def placing():
    tile, ens = lax.axis_index("tile"), lax.axis_index("ens")
    return tile, lax.rem(tile, 4), lax.rem(ens, 2), tile // 8


edge_starts = ((0, 3), (0, 1), (1, 2), (2, 3))
corner_ends = ((0, 0), (7, 0), (7, 7), (0, 7))
corner_cells = ((0, 0), (0, 1), (1, 1), (1, 0))
strips = [(tile, edge) for tile in range(3) for edge in range(4)]


def edge_slices(tile, edge, low, high):
    inner = slice(1, 9)
    return (
        (tile, low, inner),
        (tile, inner, high),
        (tile, high, inner),
        (tile, inner, low),
    )[edge]


def corner_at(corner, low, high):
    down, across = corner_cells[corner]
    return (high if down else low), (high if across else low)


def take_frame(grid, frame, links, low, high, kept):
    for i, (tile, edge) in enumerate(strips):
        frame[8 * i : 8 * i + 8] = grid[edge_slices(tile, edge, low, high)]
    for tile in range(3):
        for corner in range(4):
            row, column = corner_at(corner, low, high)
            cell = grid[tile, row, column : column + 1, :]
            if kept:
                cell = jnp.where(links[tile, 12 + corner] == 4, cell, 0.0)
            at = 96 + 4 * tile + corner
            frame[at : at + 1] = cell
    frame[108:128] = jnp.zeros((20, 256), f32)


def fill_ghosts(grid, got, links):
    for i, (tile, edge) in enumerate(strips):
        grid[edge_slices(tile, edge, 0, 9)] = got[8 * i : 8 * i + 8]
    for tile in range(3):
        for corner in range(4):
            row, column = corner_at(corner, 0, 9)
            at = 96 + 4 * tile + corner
            beside = [
                8 * (4 * tile + edge) + end
                for edge, end in zip(edge_starts[corner], corner_ends[corner])
            ]
            blend = 0.5 * (got[beside[0] : beside[0] + 1] + got[beside[1] : beside[1] + 1])
            grid[tile, row, column : column + 1, :] = jnp.where(
                links[tile, 12 + corner] == 4, got[at : at + 1], blend
            )


def split_corners(grid, links):
    for tile in range(3):
        for corner in range(4):
            row, column = corner_at(corner, 0, 9)
            near_row, near_column = corner_at(corner, 1, 8)
            cell = grid[tile, row, column : column + 1, :]
            half = jnp.where(links[tile, 12 + corner] == 3, 0.5 * cell, 0.0)
            grid[tile, row, near_column : near_column + 1, :] += half
            grid[tile, near_row, column : column + 1, :] += half


def add_returns(grid, got):
    for i, (tile, edge) in enumerate(strips):
        grid[edge_slices(tile, edge, 1, 8)] += got[8 * i : 8 * i + 8]
    for tile in range(3):
        for corner in range(4):
            row, column = corner_at(corner, 1, 8)
            at = 96 + 4 * tile + corner
            grid[tile, row, column : column + 1, :] += got[at : at + 1]


def pack_frame(pack_ref, frame, frame_ref, sent_ref):
    cells = frame[...].astype(bf16)
    frame_ref[...] = cells
    sent_ref[...] = jnp.dot(pack_ref[...], cells, preferred_element_type=f32).astype(bf16)


def unpack_frame(unpack_ref, recv_ref, frame_ref, got):
    got[...] = jnp.dot(
        unpack_ref[:, :send_rows], recv_ref[...], preferred_element_type=f32
    ) + jnp.dot(unpack_ref[:, send_rows:], frame_ref[...], preferred_element_type=f32)


def convolve(grid, weights):
    total = jnp.zeros((192, 256), f32)
    for across in range(3):
        columns = grid[:, :, across : across + 8, :]
        for down in range(3):
            window = columns[:, down : down + 8].reshape(192, 256).astype(bf16)
            total += jnp.dot(window, weights[3 * down + across], preferred_element_type=f32)
    return total


def spread_back(gradient, weights, grid, column):
    grid[...] = jnp.zeros_like(grid)
    for across in range(3):
        column[...] = jnp.zeros_like(column)
        for down in range(3):
            part = lax.dot_general(
                gradient,
                weights[3 * down + across],
                (((1,), (1,)), ((), ())),
                preferred_element_type=f32,
            )
            column[:, down : down + 8] += part.reshape(3, 8, 8, 256)
        grid[:, :, across : across + 8, :] += column[...]


def halves(place, flat, pick):
    for k in range(4):
        quarter = lax.rem(place[1] + k, 4)
        side = quarter // 2 if pick == 0 else lax.rem(quarter, 2)
        yield k, jnp.where(side == 0, flat[:, :128], flat[:, 128:]).astype(bf16)


def flatten_grid(grid, flat):
    flat[300:304] = jnp.zeros((4, 256), f32)
    for tile in range(3):
        for row in range(10):
            at = 100 * tile + 10 * row
            flat[at : at + 10] = grid[tile, row]


def route_kernel(place, links, field_ref, pack_ref, unpack_ref, frame_ref, sent_ref, grid, frame):
    here = place[0]

    def rows_of(tiles, sides, valid, base, width, local_base):
        device = [tile // 3 for tile in tiles]
        source = [lax.rem(tile, 3) * 4 + side for tile, side in zip(tiles, sides)]
        out = []
        for i in range(12):
            send_rank = take_rank = jnp.int32(0)
            for j in range(12):
                near = (device[j] == device[i]) & valid[j]
                if j < i:
                    send_rank += jnp.where(near, width, 0)
                if j != i:
                    take_rank += jnp.where(near & (source[j] < source[i]), width, 0)
            first = device[i] * slot_rows + base
            own = device[i] == here
            send = jnp.where(own | ~valid[i], -1000, first + send_rank)
            take = jnp.where(own, local_base + source[i] * width, first + take_rank)
            out.append((send, jnp.where(valid[i], take, -1000)))
        return out

    codes = [links[tile, 4 + edge] for tile, edge in strips]
    edges = rows_of(
        [links[tile, edge] for tile, edge in strips],
        [lax.rem(code, 4) for code in codes],
        [links[tile, edge] >= 0 for tile, edge in strips],
        0,
        8,
        send_rows,
    )
    across = [links[tile, 8 + corner] for tile, corner in strips]
    corners = rows_of(
        [jnp.maximum(c, 0) // 4 for c in across],
        [lax.rem(jnp.maximum(c, 0), 4) for c in across],
        [c >= 0 for c in across],
        24,
        1,
        send_rows + 96,
    )
    lane = lax.broadcasted_iota(jnp.int32, (8, 128), 1)
    row = lax.broadcasted_iota(jnp.int32, (128, 128), 0)
    send = jnp.full((8, 128), -1000, jnp.int32)
    take = jnp.full((128, 128), -1000, jnp.int32)
    for i in range(12):
        send = jnp.where(lane // 8 == i, edges[i][0] + lane % 8, send)
        send = jnp.where(lane == 96 + i, corners[i][0], send)
        turned = codes[i] // 4 == 1
        step = jnp.where(turned, 7 - row % 8, row % 8)
        take = jnp.where(row // 8 == i, edges[i][1] + step, take)
        take = jnp.where(row == 96 + i, corners[i][1], take)
    slot = lax.broadcasted_iota(jnp.int32, (send_rows, 128), 0)
    pack_ref[...] = jnp.where(slot == send[:1], 1.0, 0.0).astype(bf16)
    column = lax.broadcasted_iota(jnp.int32, (128, 128), 1)
    for m in range(9):
        unpack_ref[:, 128 * m : 128 * m + 128] = jnp.where(
            take == column + 128 * m, 1.0, 0.0
        ).astype(bf16)
    grid[:, 1:9, 1:9, :] = field_ref[...].astype(f32).reshape(3, 8, 8, 256)
    take_frame(grid, frame, links, 1, 8, False)
    pack_frame(pack_ref, frame, frame_ref, sent_ref)


def first_kernel(
    place, links, field_ref, recv_ref, old_ref, pack_ref, unpack_ref, weights,
    hidden_ref, pre_ref, frame_ref, sent_ref, part0, part1, part2, part3,
    grid, frame, got, flat,
):
    unpack_frame(unpack_ref, recv_ref, old_ref, got)
    grid[:, 1:9, 1:9, :] = field_ref[...].astype(f32).reshape(3, 8, 8, 256)
    fill_ghosts(grid, got, links)
    pre_first = convolve(grid, weights)
    pre_ref[...] = pre_first
    hidden = gelu_value(pre_first).astype(bf16)
    hidden_ref[...] = hidden
    flatten_grid(grid, flat)
    grid[:, 1:9, 1:9, :] = hidden.astype(f32).reshape(3, 8, 8, 256)
    take_frame(grid, frame, links, 1, 8, False)
    pack_frame(pack_ref, frame, frame_ref, sent_ref)
    parts = (part0, part1, part2, part3)
    for k, half in halves(place, flat, 0):
        parts[k][...] = half


def second_kernel(
    place, links, field_ref, goal_ref, hidden_ref, recv_ref, old_ref, pack_ref, unpack_ref, weights,
    held0, held1, held2,
    state_ref, misfit_ref, inner_ref, frame_ref, sent_ref, part0, part1, part2, part3,
    grid, frame, got, flat, column,
):
    unpack_frame(unpack_ref, recv_ref, old_ref, got)
    grid[:, 1:9, 1:9, :] = hidden_ref[...].astype(f32).reshape(3, 8, 8, 256)
    fill_ghosts(grid, got, links)
    states = field_ref[...].astype(f32) + convolve(grid, weights)
    state_ref[...] = states.astype(bf16)
    misfit = states - goal_ref[...].astype(f32)
    misfit_ref[...] = misfit
    low = misfit.astype(bf16)
    flatten_grid(grid, flat)
    spread_back(low, weights, grid, column)
    split_corners(grid, links)
    take_frame(grid, frame, links, 0, 9, True)
    pack_frame(pack_ref, frame, frame_ref, sent_ref)
    inner_ref[...] = grid[:, 1:9, 1:9, :]
    parts = (part0, part1, part2, part3)
    for k, half in halves(place, flat, 0):
        parts[k][:304] = half
    for k, half in halves(place, low.astype(f32), 1):
        parts[k][304:] = half


def third_kernel(
    place, links, inner_ref, pre_ref, recv_ref, old_ref, unpack_ref, weights, *refs,
):
    last_ref, frame_ref, part0, part1, part2, part3, grid, frame, got, column = refs[3:]
    unpack_frame(unpack_ref, recv_ref, old_ref, got)
    grid[:, 1:9, 1:9, :] = inner_ref[...]
    add_returns(grid, got)
    hidden_grad = grid[:, 1:9, 1:9, :].reshape(192, 256)
    low = (hidden_grad * gelu_slope(pre_ref[...])).astype(bf16)
    parts = (part0, part1, part2, part3)
    for k, half in halves(place, low.astype(f32), 1):
        parts[k][...] = half
    spread_back(low, weights, grid, column)
    split_corners(grid, links)
    take_frame(grid, frame, links, 0, 9, True)
    frame_ref[...] = frame[...].astype(bf16)
    last_ref[...] = grid[:, 1:9, 1:9, :]


def last_kernel(place, last_ref, misfit_ref, recv_ref, old_ref, unpack_ref, out_ref, grid, got):
    unpack_frame(unpack_ref, recv_ref, old_ref, got)
    grid[:, 1:9, 1:9, :] = last_ref[...] + misfit_ref[...].reshape(3, 8, 8, 256)
    add_returns(grid, got)
    out_ref[...] = grid[:, 1:9, 1:9, :]


moved_in = pl.BlockSpec(memory_space=pltpu.HBM)
landed = pl.BlockSpec(memory_space=pl.ANY)
left = pl.BlockSpec()
grid_shape = pltpu.VMEM((3, 10, 10, 256), f32)
frame_shape = pltpu.VMEM((128, 256), f32)
flat_shape = pltpu.VMEM((304, 256), f32)
column_shape = pltpu.VMEM((3, 10, 8, 256), f32)


def like(*shape, dtype=bf16):
    return jax.ShapeDtypeStruct(shape, dtype)


def run(kernel, name, args, specs, outs, scratch, flops):
    single = not isinstance(outs, tuple)
    outs = (outs,) if single else outs
    moved = [i for i, spec in enumerate(specs) if spec is not left]
    buffers = [
        (pltpu.SMEM if args[i].dtype == jnp.int32 else pltpu.VMEM)(args[i].shape, args[i].dtype)
        for i in moved
    ]
    results = [pltpu.VMEM(out.shape, out.dtype) for out in outs]

    def body(*refs):
        ins, refs = refs[: len(args)], refs[len(args) :]
        targets, refs = refs[: len(outs)], refs[len(outs) :]
        held, refs = refs[: len(moved)], refs[len(moved) :]
        made, refs = refs[: len(outs)], refs[len(outs) :]
        arrived, left_for, refs = refs[0], refs[1], refs[2:]
        copies = [
            pltpu.make_async_copy(ins[i], held[n], arrived.at[n]) for n, i in enumerate(moved)
        ]
        for copy in copies:
            copy.start()
        for copy in copies:
            copy.wait()
        given = list(ins)
        place = placing()
        for n, i in enumerate(moved):
            given[i] = held[n]
        kernel(place, *given, *made, *refs)
        copies = [
            pltpu.make_async_copy(made[n], targets[n], left_for.at[n]) for n in range(len(outs))
        ]
        for copy in copies:
            copy.start()
        for copy in copies:
            copy.wait()

    made = pl.pallas_call(
        body,
        out_shape=tuple(pltpu.HBM(out.shape, out.dtype) for out in outs),
        in_specs=[landed if spec is left else spec for spec in specs],
        out_specs=tuple(moved_in for _ in outs),
        scratch_shapes=[
            *buffers,
            *results,
            pltpu.SemaphoreType.DMA((max(1, len(moved)),)),
            pltpu.SemaphoreType.DMA((len(outs),)),
            *scratch,
        ],
        compiler_params=pltpu.CompilerParams(vmem_limit_bytes=40 * 2**20),
        cost_estimate=pl.CostEstimate(flops=flops, bytes_accessed=3000000, transcendentals=0),
        name=name,
    )(
        *[
            pltpu.with_memory_space_constraint(arg, pltpu.HBM) if spec is moved_in else arg
            for arg, spec in zip(args, specs)
        ]
    )
    return made[0] if single else made


def slope_kernel(split, place, *refs):
    count = 4 if split else 8
    parts = refs[:count]
    kept_ref, sent_ref, flat, wide, total = refs[count:]
    grads = []
    for n in range(4):
        flat[304 * n : 304 * n + 304] = parts[n][:304].astype(f32)
        grads.append(parts[n][304:] if split else parts[4 + n][...])
    grads = jnp.concatenate(grads, axis=0)
    low = place[2] == 0
    for across in range(3):
        for n in range(4):
            for tile in range(3):
                for row in range(10):
                    at = 304 * n + 100 * tile + 10 * row + across
                    wide[3 * n + tile, row] = flat[at : at + 8]
        for down in range(3):
            window = wide[:, down : down + 8].reshape(768, 128).astype(bf16)
            out = lax.dot_general(
                window, grads, (((0,), (0,)), ((), ())), preferred_element_type=f32
            )
            tap = (3 * down + across) * 64
            total[0, tap : tap + 64] = jnp.where(low, out[:64], out[64:])
            total[1, tap : tap + 64] = jnp.where(low, out[64:], out[:64])
    for j in range(4):
        kept_ref[j] = total[0, 144 * j : 144 * j + 144]
        sent_ref[j] = total[1, 144 * j : 144 * j + 144]


def slope_terms(parts, split, *packing):
    shape = like(4, 144, 128, dtype=f32)
    count = len(parts)
    outs = (shape, shape) + ((like(send_rows, 256),) if packing else ())

    def kernel(place, *refs):
        ins, refs = refs[: count + len(packing)], refs[count + len(packing) :]
        if packing:
            pack_ref, frame_ref = ins[count:]
            refs[2][...] = jnp.dot(
                pack_ref[...], frame_ref[...], preferred_element_type=f32
            ).astype(bf16)
        slope_kernel(split, place, *ins[:count], *refs[:2], *refs[len(outs) :])

    return run(
        kernel,
        "slope_terms",
        (*parts, *packing),
        ([moved_in] + [landed] * 3) * (count // 4) + [moved_in] * len(packing),
        outs,
        [
            pltpu.VMEM((1216, 128), f32),
            pltpu.VMEM((12, 10, 8, 128), f32),
            pltpu.VMEM((2, 576, 128), f32),
        ],
        2 * 9 * 768 * 128 * 128,
    )


def ring(parts, axis):
    return [shifted(part, axis, k) if k else part for k, part in enumerate(parts)]


def pair_kernel(place, kept0, got0, kept1, got1, *chunks):
    for k in range(4):
        at = lax.rem(place[3] + k, 4)
        chunks[k][:144] = kept0[at] + got0[at]
        chunks[k][144:] = kept1[at] + got1[at]


def plane_kernel(place, own, part1, part2, part3, held, out, total):
    total[...] = (own[...] + part1[...]) + (part2[...] + part3[...])
    for j in range(8):
        out[j] = total[36 * j : 36 * j + 36]


def spread_kernel(place, own, other, first_ref, second_ref):
    low = place[2] == 0
    for x in range(4):
        row, column = 128 * (x // 2), 128 * (x % 2)
        for n, out in enumerate((first_ref, second_ref)):
            at = slice(144 * n, 144 * n + 144)
            pair = [
                jnp.concatenate(
                    [part[4 * x + y, at].astype(f32) for y in range(4)], axis=0
                ).reshape(9, 64, 128)
                for part in (own, other)
            ]
            out[:, row : row + 64, column : column + 128] = jnp.where(low, pair[0], pair[1])
            out[:, row + 64 : row + 128, column : column + 128] = jnp.where(low, pair[1], pair[0])


def groups(along):
    axes = ("x", "y", "z", "core")
    out = []
    for fixed in itertools.product(*[range(1 if a in along else sizes[a]) for a in axes]):
        group = []
        for moving in itertools.product(*[range(sizes[a]) for a in along]):
            at = dict(zip(axes, fixed)) | dict(zip(along, moving))
            group.append(place_of(**at))
        out.append(group)
    return out


def trade(values, *along):
    return lax.all_to_all(
        values, ("tile", "ens"), 0, 0, axis_index_groups=groups(along), tiled=True
    )


def copies_of(values, count):
    return jnp.broadcast_to(values[None], (count,) + values.shape)


def finish_slopes(chunks, held, scale):
    terms = run(
        plane_kernel,
        "row_sum",
        (*ring(chunks, "y"), held),
        [moved_in] + [landed] * 3 + [left],
        like(8, 36, 128, dtype=f32),
        [pltpu.VMEM((288, 128), f32)],
        1000,
    )
    mine = (jnp.sum(trade(terms, "z"), axis=0) * scale).astype(bf16)
    line = trade(copies_of(mine, 8), "z").reshape(288, 128)
    plane = trade(copies_of(line, 16), "x", "y")
    shape = like(9, 256, 256, dtype=f32)
    return run(
        spread_kernel,
        "spread_slopes",
        (plane, shifted(plane, "core", 1)),
        [landed, landed],
        (shape, shape),
        [],
        1000,
    )


def exchange(values):
    return lax.all_to_all(values, "tile", 0, 0, tiled=True)


def per_device(network_conditions, subsequent_targets, w_first, w_second, tile_links):
    field = network_conditions.reshape(192, 256)
    goal = subsequent_targets.reshape(192, 256)
    first_weights, second_weights = w_first.reshape(9, 256, 256), w_second.reshape(9, 256, 256)
    scale = 1.0 / math.sqrt(lax.axis_size("ens") * lax.axis_size("tile") * 192)
    frame_like, sent_like, rows_like = like(128, 256), like(send_rows, 256), like(192, 256)
    inner_like = like(3, 8, 8, 256, dtype=f32)
    conv_flops = 2 * 9 * 192 * 256 * 256

    pack, unpack, frame, sent = run(
        route_kernel,
        "routes",
        (tile_links, field),
        [moved_in, moved_in],
        (like(send_rows, 128), like(128, send_rows + 128), frame_like, sent_like),
        [grid_shape, frame_shape],
        2 * send_rows * 128 * 256,
    )
    recv = exchange(sent)
    hidden, pre_first, frame, sent, *parts = run(
        first_kernel,
        "first_layer",
        (tile_links, field, recv, frame, pack, unpack, first_weights),
        [moved_in] * 2 + [landed] + [moved_in] * 4,
        (rows_like, like(192, 256, dtype=f32), frame_like, sent_like) + (like(304, 128),) * 4,
        [grid_shape, frame_shape, frame_shape, flat_shape],
        conv_flops,
    )
    recv = exchange(sent)
    field_parts = ring(parts, "x")
    states, misfit, inner, frame, sent, *parts = run(
        second_kernel,
        "second_layer",
        (
            tile_links, field, goal, hidden, recv, frame, pack, unpack, second_weights,
            *field_parts[1:],
        ),
        [moved_in] * 4 + [landed] + [moved_in] * 4 + [left] * 3,
        (rows_like, like(192, 256, dtype=f32), inner_like, frame_like, sent_like)
        + (like(496, 128),) * 4,
        [grid_shape, frame_shape, frame_shape, flat_shape, column_shape],
        2 * conv_flops,
    )
    recv = exchange(sent)
    closing_parts = ring(parts, "x")
    closing = slope_terms(closing_parts, True)
    last, frame, *parts = run(
        third_kernel,
        "first_gradient",
        (tile_links, inner, pre_first, recv, frame, unpack, first_weights, *closing_parts[1:]),
        [moved_in] * 3 + [landed] + [moved_in] * 3 + [left] * 3,
        (inner_like, frame_like) + (like(192, 128),) * 4,
        [grid_shape, frame_shape, frame_shape, column_shape],
        conv_flops,
    )
    got_closing = shifted(closing[1], "core", 1)
    *opening, sent = slope_terms(field_parts + ring(parts, "x"), False, pack, frame)
    recv = exchange(sent)
    chunks = run(
        pair_kernel,
        "pair_sum",
        (opening[0], shifted(opening[1], "core", 1), closing[0], got_closing),
        [moved_in, landed, moved_in, landed],
        (like(288, 128, dtype=f32),) * 4,
        [],
        1000,
    )
    condition_derivative = run(
        last_kernel,
        "last_gradient",
        (last, misfit, recv, frame, unpack),
        [moved_in] * 2 + [landed] + [moved_in] * 2,
        inner_like,
        [grid_shape, frame_shape],
        1000,
    )
    slopes = finish_slopes(chunks, recv, scale)
    return (
        states.reshape(network_conditions.shape),
        condition_derivative[None],
        slopes[0].reshape(w_first.shape),
        slopes[1].reshape(w_second.shape),
    )


def solution(mesh):
    return jax.shard_map(
        per_device,
        mesh=mesh,
        in_specs=(
            P("ens", "tile", None, None, None),
            P("ens", "tile", None, None, None),
            P(),
            P(),
            P("tile", None),
        ),
        out_specs=(
            P("ens", "tile", None, None, None),
            P("ens", "tile", None, None, None),
            P(),
            P(),
        ),
        check_vma=False,
    )
```

```python
import itertools
import math

import jax
import jax.numpy as jnp
from jax import lax
from jax.experimental import pallas as pl
from jax.experimental.pallas import tpu as pltpu
from jax.sharding import PartitionSpec as P

tanh_scale = 0.7978845608028654
cubic_term = 0.044715
slot_rows = 32
send_rows = 1024
bf16, f32 = jnp.bfloat16, jnp.float32


def gelu_value(inputs):
    return (
        0.5
        * inputs
        * (1.0 + jnp.tanh(tanh_scale * (inputs + cubic_term * inputs * inputs * inputs)))
    )


def gelu_slope(inputs):
    tangent = jnp.tanh(tanh_scale * (inputs + cubic_term * inputs * inputs * inputs))
    return 0.5 * (1.0 + tangent) + 0.5 * inputs * (1.0 - tangent * tangent) * tanh_scale * (
        1.0 + 3.0 * cubic_term * inputs * inputs
    )


sizes = {"x": 4, "y": 4, "z": 8, "core": 2}


def place_of(x, y, z, core):
    return ((y * 2 + z % 2) * 4 + x) * 8 + (z // 2) * 2 + core


def shifted(values, axis, by):
    pairs = []
    for x in range(4):
        for y in range(4):
            for z in range(8):
                for core in range(2):
                    at = {"x": x, "y": y, "z": z, "core": core}
                    to = dict(at)
                    to[axis] = (at[axis] + by) % sizes[axis]
                    pairs.append((place_of(**at), place_of(**to)))
    return lax.ppermute(values, ("tile", "ens"), pairs)


def placing():
    tile, ens = lax.axis_index("tile"), lax.axis_index("ens")
    return tile, lax.rem(tile, 4), lax.rem(ens, 2), tile // 8


edge_starts = ((0, 3), (0, 1), (1, 2), (2, 3))
corner_ends = ((0, 0), (7, 0), (7, 7), (0, 7))
corner_cells = ((0, 0), (0, 1), (1, 1), (1, 0))
strips = [(tile, edge) for tile in range(3) for edge in range(4)]


def edge_slices(tile, edge, low, high):
    inner = slice(1, 9)
    return (
        (tile, low, inner),
        (tile, inner, high),
        (tile, high, inner),
        (tile, inner, low),
    )[edge]


def corner_at(corner, low, high):
    down, across = corner_cells[corner]
    return (high if down else low), (high if across else low)


def take_frame(grid, frame, links, low, high, kept):
    for i, (tile, edge) in enumerate(strips):
        frame[8 * i : 8 * i + 8] = grid[edge_slices(tile, edge, low, high)]
    for tile in range(3):
        for corner in range(4):
            row, column = corner_at(corner, low, high)
            cell = grid[tile, row, column : column + 1, :]
            if kept:
                cell = jnp.where(links[tile, 12 + corner] == 4, cell, 0.0)
            at = 96 + 4 * tile + corner
            frame[at : at + 1] = cell
    frame[108:128] = jnp.zeros((20, 256), f32)


def fill_ghosts(grid, got, links):
    for i, (tile, edge) in enumerate(strips):
        grid[edge_slices(tile, edge, 0, 9)] = got[8 * i : 8 * i + 8]
    for tile in range(3):
        for corner in range(4):
            row, column = corner_at(corner, 0, 9)
            at = 96 + 4 * tile + corner
            beside = [
                8 * (4 * tile + edge) + end
                for edge, end in zip(edge_starts[corner], corner_ends[corner])
            ]
            blend = 0.5 * (got[beside[0] : beside[0] + 1] + got[beside[1] : beside[1] + 1])
            grid[tile, row, column : column + 1, :] = jnp.where(
                links[tile, 12 + corner] == 4, got[at : at + 1], blend
            )


def split_corners(grid, links):
    for tile in range(3):
        for corner in range(4):
            row, column = corner_at(corner, 0, 9)
            near_row, near_column = corner_at(corner, 1, 8)
            cell = grid[tile, row, column : column + 1, :]
            half = jnp.where(links[tile, 12 + corner] == 3, 0.5 * cell, 0.0)
            grid[tile, row, near_column : near_column + 1, :] += half
            grid[tile, near_row, column : column + 1, :] += half


def add_returns(grid, got):
    for i, (tile, edge) in enumerate(strips):
        grid[edge_slices(tile, edge, 1, 8)] += got[8 * i : 8 * i + 8]
    for tile in range(3):
        for corner in range(4):
            row, column = corner_at(corner, 1, 8)
            at = 96 + 4 * tile + corner
            grid[tile, row, column : column + 1, :] += got[at : at + 1]


def pack_frame(pack_ref, frame, frame_ref, sent_ref):
    cells = frame[...].astype(bf16)
    frame_ref[...] = cells
    sent_ref[...] = jnp.dot(pack_ref[...], cells, preferred_element_type=f32).astype(bf16)


def unpack_frame(unpack_ref, recv_ref, frame_ref, got):
    got[...] = jnp.dot(
        unpack_ref[:, :send_rows], recv_ref[...], preferred_element_type=f32
    ) + jnp.dot(unpack_ref[:, send_rows:], frame_ref[...], preferred_element_type=f32)


def convolve(grid, weights):
    total = jnp.zeros((192, 256), f32)
    for across in range(3):
        columns = grid[:, :, across : across + 8, :]
        for down in range(3):
            window = columns[:, down : down + 8].reshape(192, 256).astype(bf16)
            total += jnp.dot(window, weights[3 * down + across], preferred_element_type=f32)
    return total


def spread_back(gradient, weights, grid, column):
    grid[...] = jnp.zeros_like(grid)
    for across in range(3):
        column[...] = jnp.zeros_like(column)
        for down in range(3):
            part = lax.dot_general(
                gradient,
                weights[3 * down + across],
                (((1,), (1,)), ((), ())),
                preferred_element_type=f32,
            )
            column[:, down : down + 8] += part.reshape(3, 8, 8, 256)
        grid[:, :, across : across + 8, :] += column[...]


def halves(place, flat, pick):
    for k in range(4):
        quarter = lax.rem(place[1] + k, 4)
        side = quarter // 2 if pick == 0 else lax.rem(quarter, 2)
        yield k, jnp.where(side == 0, flat[:, :128], flat[:, 128:]).astype(bf16)


def flatten_grid(grid, flat):
    flat[300:304] = jnp.zeros((4, 256), f32)
    for tile in range(3):
        for row in range(10):
            at = 100 * tile + 10 * row
            flat[at : at + 10] = grid[tile, row]


def route_kernel(place, links, field_ref, pack_ref, unpack_ref, frame_ref, sent_ref, grid, frame):
    here = place[0]

    def rows_of(tiles, sides, valid, base, width, local_base):
        device = [tile // 3 for tile in tiles]
        source = [lax.rem(tile, 3) * 4 + side for tile, side in zip(tiles, sides)]
        out = []
        for i in range(12):
            send_rank = take_rank = jnp.int32(0)
            for j in range(12):
                near = (device[j] == device[i]) & valid[j]
                if j < i:
                    send_rank += jnp.where(near, width, 0)
                if j != i:
                    take_rank += jnp.where(near & (source[j] < source[i]), width, 0)
            first = device[i] * slot_rows + base
            own = device[i] == here
            send = jnp.where(own | ~valid[i], -1000, first + send_rank)
            take = jnp.where(own, local_base + source[i] * width, first + take_rank)
            out.append((send, jnp.where(valid[i], take, -1000)))
        return out

    codes = [links[tile, 4 + edge] for tile, edge in strips]
    edges = rows_of(
        [links[tile, edge] for tile, edge in strips],
        [lax.rem(code, 4) for code in codes],
        [links[tile, edge] >= 0 for tile, edge in strips],
        0,
        8,
        send_rows,
    )
    across = [links[tile, 8 + corner] for tile, corner in strips]
    corners = rows_of(
        [jnp.maximum(c, 0) // 4 for c in across],
        [lax.rem(jnp.maximum(c, 0), 4) for c in across],
        [c >= 0 for c in across],
        24,
        1,
        send_rows + 96,
    )
    lane = lax.broadcasted_iota(jnp.int32, (8, 128), 1)
    row = lax.broadcasted_iota(jnp.int32, (128, 128), 0)
    send = jnp.full((8, 128), -1000, jnp.int32)
    take = jnp.full((128, 128), -1000, jnp.int32)
    for i in range(12):
        send = jnp.where(lane // 8 == i, edges[i][0] + lane % 8, send)
        send = jnp.where(lane == 96 + i, corners[i][0], send)
        turned = codes[i] // 4 == 1
        step = jnp.where(turned, 7 - row % 8, row % 8)
        take = jnp.where(row // 8 == i, edges[i][1] + step, take)
        take = jnp.where(row == 96 + i, corners[i][1], take)
    slot = lax.broadcasted_iota(jnp.int32, (send_rows, 128), 0)
    pack_ref[...] = jnp.where(slot == send[:1], 1.0, 0.0).astype(bf16)
    column = lax.broadcasted_iota(jnp.int32, (128, 128), 1)
    for m in range(9):
        unpack_ref[:, 128 * m : 128 * m + 128] = jnp.where(
            take == column + 128 * m, 1.0, 0.0
        ).astype(bf16)
    grid[:, 1:9, 1:9, :] = field_ref[...].astype(f32).reshape(3, 8, 8, 256)
    take_frame(grid, frame, links, 1, 8, False)
    pack_frame(pack_ref, frame, frame_ref, sent_ref)


def first_kernel(
    place, links, field_ref, recv_ref, old_ref, pack_ref, unpack_ref, weights,
    hidden_ref, pre_ref, frame_ref, sent_ref, part0, part1, part2, part3,
    grid, frame, got, flat,
):
    unpack_frame(unpack_ref, recv_ref, old_ref, got)
    grid[:, 1:9, 1:9, :] = field_ref[...].astype(f32).reshape(3, 8, 8, 256)
    fill_ghosts(grid, got, links)
    pre_first = convolve(grid, weights)
    pre_ref[...] = pre_first
    hidden = gelu_value(pre_first).astype(bf16)
    hidden_ref[...] = hidden
    flatten_grid(grid, flat)
    grid[:, 1:9, 1:9, :] = hidden.astype(f32).reshape(3, 8, 8, 256)
    take_frame(grid, frame, links, 1, 8, False)
    pack_frame(pack_ref, frame, frame_ref, sent_ref)
    parts = (part0, part1, part2, part3)
    for k, half in halves(place, flat, 0):
        parts[k][...] = half


def second_kernel(
    place, links, field_ref, goal_ref, hidden_ref, recv_ref, old_ref, pack_ref, unpack_ref, weights,
    held0, held1, held2,
    state_ref, misfit_ref, inner_ref, frame_ref, sent_ref, part0, part1, part2, part3,
    grid, frame, got, flat, column,
):
    unpack_frame(unpack_ref, recv_ref, old_ref, got)
    grid[:, 1:9, 1:9, :] = hidden_ref[...].astype(f32).reshape(3, 8, 8, 256)
    fill_ghosts(grid, got, links)
    states = field_ref[...].astype(f32) + convolve(grid, weights)
    state_ref[...] = states.astype(bf16)
    misfit = states - goal_ref[...].astype(f32)
    misfit_ref[...] = misfit
    low = misfit.astype(bf16)
    flatten_grid(grid, flat)
    spread_back(low, weights, grid, column)
    split_corners(grid, links)
    take_frame(grid, frame, links, 0, 9, True)
    pack_frame(pack_ref, frame, frame_ref, sent_ref)
    inner_ref[...] = grid[:, 1:9, 1:9, :]
    parts = (part0, part1, part2, part3)
    for k, half in halves(place, flat, 0):
        parts[k][:304] = half
    for k, half in halves(place, low.astype(f32), 1):
        parts[k][304:] = half


def third_kernel(
    place, links, inner_ref, pre_ref, recv_ref, old_ref, unpack_ref, weights, *refs,
):
    last_ref, frame_ref, part0, part1, part2, part3, grid, frame, got, column = refs[3:]
    unpack_frame(unpack_ref, recv_ref, old_ref, got)
    grid[:, 1:9, 1:9, :] = inner_ref[...]
    add_returns(grid, got)
    hidden_grad = grid[:, 1:9, 1:9, :].reshape(192, 256)
    low = (hidden_grad * gelu_slope(pre_ref[...])).astype(bf16)
    parts = (part0, part1, part2, part3)
    for k, half in halves(place, low.astype(f32), 1):
        parts[k][...] = half
    spread_back(low, weights, grid, column)
    split_corners(grid, links)
    take_frame(grid, frame, links, 0, 9, True)
    frame_ref[...] = frame[...].astype(bf16)
    last_ref[...] = grid[:, 1:9, 1:9, :]


def last_kernel(place, last_ref, misfit_ref, recv_ref, old_ref, unpack_ref, out_ref, grid, got):
    unpack_frame(unpack_ref, recv_ref, old_ref, got)
    grid[:, 1:9, 1:9, :] = last_ref[...] + misfit_ref[...].reshape(3, 8, 8, 256)
    add_returns(grid, got)
    out_ref[...] = grid[:, 1:9, 1:9, :]


moved_in = pl.BlockSpec(memory_space=pltpu.HBM)
landed = pl.BlockSpec(memory_space=pl.ANY)
left = pl.BlockSpec()
resting = pl.BlockSpec(memory_space=pltpu.HBM)
grid_shape = pltpu.VMEM((3, 10, 10, 256), f32)
frame_shape = pltpu.VMEM((128, 256), f32)
flat_shape = pltpu.VMEM((304, 256), f32)
column_shape = pltpu.VMEM((3, 10, 8, 256), f32)


def like(*shape, dtype=bf16):
    return jax.ShapeDtypeStruct(shape, dtype)


class Arriving:
    def __init__(self, ref, copy):
        self.ref, self.copy = ref, copy

    def settle(self):
        if self.copy is not None:
            self.copy.wait()
            self.copy = None

    def __getitem__(self, at):
        self.settle()
        return self.ref[at]


class Leaving:
    def __init__(self, ref, copy):
        self.ref, self.copy, self.started = ref, copy, False

    def send(self):
        if not self.started:
            self.copy.start()
            self.started = True

    def __getitem__(self, at):
        return self.ref[at]

    def __setitem__(self, at, value):
        self.ref[at] = value
        if at is Ellipsis:
            self.send()


def run(kernel, name, args, specs, outs, scratch, flops):
    single = not isinstance(outs, tuple)
    outs = (outs,) if single else outs
    moved = [i for i, spec in enumerate(specs) if spec is not left and spec is not resting]
    buffers = [
        (pltpu.SMEM if args[i].dtype == jnp.int32 else pltpu.VMEM)(args[i].shape, args[i].dtype)
        for i in moved
    ]
    stores = [pltpu.VMEM(out.shape, out.dtype) for out in outs]

    def body(*refs):
        ins, refs = refs[: len(args)], refs[len(args) :]
        targets, refs = refs[: len(outs)], refs[len(outs) :]
        held, refs = refs[: len(moved)], refs[len(moved) :]
        made, refs = refs[: len(outs)], refs[len(outs) :]
        arrived, left_for, refs = refs[0], refs[1], refs[2:]
        copies = [
            pltpu.make_async_copy(ins[i], held[n], arrived.at[n]) for n, i in enumerate(moved)
        ]
        for copy in copies:
            copy.start()
        given = list(ins)
        for n, i in enumerate(moved):
            given[i] = Arriving(held[n], copies[n])
        results = [
            Leaving(made[n], pltpu.make_async_copy(made[n], targets[n], left_for.at[n]))
            for n in range(len(outs))
        ]
        kernel(placing(), *given, *results, *refs)
        for n in range(len(moved)):
            given[moved[n]].settle()
        for result in results:
            result.send()
        for result in results:
            result.copy.wait()

    made = pl.pallas_call(
        body,
        out_shape=tuple(pltpu.HBM(out.shape, out.dtype) for out in outs),
        in_specs=[landed if spec is left else spec for spec in specs],
        out_specs=tuple(moved_in for _ in outs),
        scratch_shapes=[
            *buffers,
            *stores,
            pltpu.SemaphoreType.DMA((max(1, len(moved)),)),
            pltpu.SemaphoreType.DMA((len(outs),)),
            *scratch,
        ],
        compiler_params=pltpu.CompilerParams(vmem_limit_bytes=40 * 2**20),
        cost_estimate=pl.CostEstimate(flops=flops, bytes_accessed=3000000, transcendentals=0),
        name=name,
    )(
        *[
            pltpu.with_memory_space_constraint(arg, pltpu.HBM)
            if spec is moved_in or spec is resting
            else arg
            for arg, spec in zip(args, specs)
        ]
    )
    return made[0] if single else made


def slope_kernel(split, place, *refs):
    count = 4 if split else 8
    parts = refs[:count]
    kept_ref, sent_ref, flat, wide, total = refs[count:]
    grads = []
    for n in range(4):
        flat[304 * n : 304 * n + 304] = parts[n][:304].astype(f32)
        grads.append(parts[n][304:] if split else parts[4 + n][...])
    grads = jnp.concatenate(grads, axis=0)
    low = place[2] == 0
    for across in range(3):
        for n in range(4):
            for tile in range(3):
                for row in range(10):
                    at = 304 * n + 100 * tile + 10 * row + across
                    wide[3 * n + tile, row] = flat[at : at + 8]
        for down in range(3):
            window = wide[:, down : down + 8].reshape(768, 128).astype(bf16)
            out = lax.dot_general(
                window, grads, (((0,), (0,)), ((), ())), preferred_element_type=f32
            )
            tap = (3 * down + across) * 64
            total[0, tap : tap + 64] = jnp.where(low, out[:64], out[64:])
            total[1, tap : tap + 64] = jnp.where(low, out[64:], out[:64])
    for j in range(4):
        kept_ref[j] = total[0, 144 * j : 144 * j + 144]
        sent_ref[j] = total[1, 144 * j : 144 * j + 144]


def slope_terms(parts, split, packing=(), held=()):
    shape = like(4, 144, 128, dtype=f32)
    count = len(parts)
    outs = (shape, shape) + ((like(send_rows, 256),) if packing else ())

    def kernel(place, *refs):
        ins, refs = refs[: count + len(packing)], refs[count + len(packing) + len(held) :]
        if packing:
            pack_ref, frame_ref = ins[count:]
            refs[2][...] = jnp.dot(
                pack_ref[...], frame_ref[...], preferred_element_type=f32
            ).astype(bf16)
        slope_kernel(split, place, *ins[:count], *refs[:2], *refs[len(outs) :])

    return run(
        kernel,
        "slope_terms",
        (*parts, *packing, *held),
        ([moved_in] + [landed] * 3) * (count // 4) + [moved_in] * len(packing) + [resting] * len(held),
        outs,
        [
            pltpu.VMEM((1216, 128), f32),
            pltpu.VMEM((12, 10, 8, 128), f32),
            pltpu.VMEM((2, 576, 128), f32),
        ],
        2 * 9 * 768 * 128 * 128,
    )


def ring(parts, axis):
    return [shifted(part, axis, k) if k else part for k, part in enumerate(parts)]


def pair_kernel(place, kept0, got0, kept1, got1, *chunks):
    for k in range(4):
        at = lax.rem(place[3] + k, 4)
        chunks[k][:144] = kept0[at] + got0[at]
        chunks[k][144:] = kept1[at] + got1[at]


def plane_kernel(place, own, part1, part2, part3, held, out, total):
    total[...] = (own[...] + part1[...]) + (part2[...] + part3[...])
    for j in range(8):
        out[j] = total[36 * j : 36 * j + 36]


def spread_kernel(place, own, other, first_ref, second_ref):
    low = place[2] == 0
    for n, out in enumerate((first_ref, second_ref)):
        at = slice(144 * n, 144 * n + 144)
        for x in range(4):
            row, column = 128 * (x // 2), 128 * (x % 2)
            pair = [
                jnp.concatenate(
                    [part[4 * x + y, at].astype(f32) for y in range(4)], axis=0
                ).reshape(9, 64, 128)
                for part in (own, other)
            ]
            out[:, row : row + 64, column : column + 128] = jnp.where(low, pair[0], pair[1])
            out[:, row + 64 : row + 128, column : column + 128] = jnp.where(low, pair[1], pair[0])
        out.send()


def groups(along):
    axes = ("x", "y", "z", "core")
    out = []
    for fixed in itertools.product(*[range(1 if a in along else sizes[a]) for a in axes]):
        group = []
        for moving in itertools.product(*[range(sizes[a]) for a in along]):
            at = dict(zip(axes, fixed)) | dict(zip(along, moving))
            group.append(place_of(**at))
        out.append(group)
    return out


def trade(values, *along):
    return lax.all_to_all(
        values, ("tile", "ens"), 0, 0, axis_index_groups=groups(along), tiled=True
    )


def copies_of(values, count):
    return jnp.broadcast_to(values[None], (count,) + values.shape)


def finish_slopes(chunks, held, scale):
    terms = run(
        plane_kernel,
        "row_sum",
        (*ring(chunks, "y"), held),
        [moved_in] + [landed] * 3 + [left],
        like(8, 36, 128, dtype=f32),
        [pltpu.VMEM((288, 128), f32)],
        1000,
    )
    mine = (jnp.sum(trade(terms, "z"), axis=0) * scale).astype(bf16)
    line = trade(copies_of(mine, 8), "z").reshape(288, 128)
    plane = trade(copies_of(line, 16), "x", "y")
    shape = like(9, 256, 256, dtype=f32)
    return run(
        spread_kernel,
        "spread_slopes",
        (plane, shifted(plane, "core", 1)),
        [landed, landed],
        (shape, shape),
        [],
        1000,
    )


def exchange(values):
    return lax.all_to_all(values, "tile", 0, 0, tiled=True)


def per_device(network_conditions, subsequent_targets, w_first, w_second, tile_links):
    field = network_conditions.reshape(192, 256)
    goal = subsequent_targets.reshape(192, 256)
    first_weights, second_weights = w_first.reshape(9, 256, 256), w_second.reshape(9, 256, 256)
    scale = 1.0 / math.sqrt(lax.axis_size("ens") * lax.axis_size("tile") * 192)
    frame_like, sent_like, rows_like = like(128, 256), like(send_rows, 256), like(192, 256)
    inner_like = like(3, 8, 8, 256, dtype=f32)
    conv_flops = 2 * 9 * 192 * 256 * 256

    pack, unpack, frame, sent = run(
        route_kernel,
        "routes",
        (tile_links, field),
        [moved_in, moved_in],
        (like(send_rows, 128), like(128, send_rows + 128), frame_like, sent_like),
        [grid_shape, frame_shape],
        2 * send_rows * 128 * 256,
    )
    recv = exchange(sent)
    hidden, pre_first, frame, sent, *parts = run(
        first_kernel,
        "first_layer",
        (tile_links, field, recv, frame, pack, unpack, first_weights),
        [moved_in] * 2 + [landed] + [moved_in] * 4,
        (rows_like, like(192, 256, dtype=f32), frame_like, sent_like) + (like(304, 128),) * 4,
        [grid_shape, frame_shape, frame_shape, flat_shape],
        conv_flops,
    )
    recv = exchange(sent)
    field_parts = ring(parts, "x")
    states, misfit, inner, frame, sent, *parts = run(
        second_kernel,
        "second_layer",
        (
            tile_links, field, goal, hidden, recv, frame, pack, unpack, second_weights,
            *field_parts[1:],
        ),
        [moved_in] * 4 + [landed] + [moved_in] * 4 + [left] * 3,
        (rows_like, like(192, 256, dtype=f32), inner_like, frame_like, sent_like)
        + (like(496, 128),) * 4,
        [grid_shape, frame_shape, frame_shape, flat_shape, column_shape],
        2 * conv_flops,
    )
    recv = exchange(sent)
    closing_parts = ring(parts, "x")
    closing = slope_terms(closing_parts, True)
    last, frame, *parts = run(
        third_kernel,
        "first_gradient",
        (tile_links, inner, pre_first, recv, frame, unpack, first_weights, *closing_parts[1:]),
        [moved_in] * 3 + [landed] + [moved_in] * 3 + [left] * 3,
        (inner_like, frame_like) + (like(192, 128),) * 4,
        [grid_shape, frame_shape, frame_shape, column_shape],
        conv_flops,
    )
    got_closing = shifted(closing[1], "core", 1)
    *opening, sent = slope_terms(
        field_parts + ring(parts, "x"), False, (pack, frame), (closing[0],)
    )
    recv = exchange(sent)
    chunks = run(
        pair_kernel,
        "pair_sum",
        (opening[0], shifted(opening[1], "core", 1), closing[0], got_closing),
        [moved_in, landed, moved_in, landed],
        (like(288, 128, dtype=f32),) * 4,
        [],
        1000,
    )
    condition_derivative = run(
        last_kernel,
        "last_gradient",
        (last, misfit, recv, frame, unpack),
        [moved_in] * 2 + [landed] + [moved_in] * 2,
        inner_like,
        [grid_shape, frame_shape],
        1000,
    )
    slopes = finish_slopes(chunks, recv, scale)
    return (
        states.reshape(network_conditions.shape),
        condition_derivative[None],
        slopes[0].reshape(w_first.shape),
        slopes[1].reshape(w_second.shape),
    )


def solution(mesh):
    return jax.shard_map(
        per_device,
        mesh=mesh,
        in_specs=(
            P("ens", "tile", None, None, None),
            P("ens", "tile", None, None, None),
            P(),
            P(),
            P("tile", None),
        ),
        out_specs=(
            P("ens", "tile", None, None, None),
            P("ens", "tile", None, None, None),
            P(),
            P(),
        ),
        check_vma=False,
    )
```

```python
import itertools
import math

import jax
import jax.numpy as jnp
from jax import lax
from jax.experimental import pallas as pl
from jax.experimental.pallas import tpu as pltpu
from jax.sharding import PartitionSpec as P

tanh_scale = 0.7978845608028654
cubic_term = 0.044715
slot_rows = 32
send_rows = 1024
bf16, f32 = jnp.bfloat16, jnp.float32


def gelu_value(inputs):
    return (
        0.5
        * inputs
        * (1.0 + jnp.tanh(tanh_scale * (inputs + cubic_term * inputs * inputs * inputs)))
    )


def gelu_slope(inputs):
    tangent = jnp.tanh(tanh_scale * (inputs + cubic_term * inputs * inputs * inputs))
    return 0.5 * (1.0 + tangent) + 0.5 * inputs * (1.0 - tangent * tangent) * tanh_scale * (
        1.0 + 3.0 * cubic_term * inputs * inputs
    )


sizes = {"x": 4, "y": 4, "z": 8, "core": 2}


def place_of(x, y, z, core):
    return ((y * 2 + z % 2) * 4 + x) * 8 + (z // 2) * 2 + core


def shifted(values, axis, by):
    pairs = []
    for x in range(4):
        for y in range(4):
            for z in range(8):
                for core in range(2):
                    at = {"x": x, "y": y, "z": z, "core": core}
                    to = dict(at)
                    to[axis] = (at[axis] + by) % sizes[axis]
                    pairs.append((place_of(**at), place_of(**to)))
    return lax.ppermute(values, ("tile", "ens"), pairs)


def placing():
    tile, ens = lax.axis_index("tile"), lax.axis_index("ens")
    return tile, lax.rem(tile, 4), lax.rem(ens, 2), tile // 8


edge_starts = ((0, 3), (0, 1), (1, 2), (2, 3))
corner_ends = ((0, 0), (7, 0), (7, 7), (0, 7))
corner_cells = ((0, 0), (0, 1), (1, 1), (1, 0))
strips = [(tile, edge) for tile in range(3) for edge in range(4)]


def edge_slices(tile, edge, low, high):
    inner = slice(1, 9)
    return (
        (tile, low, inner),
        (tile, inner, high),
        (tile, high, inner),
        (tile, inner, low),
    )[edge]


def corner_at(corner, low, high):
    down, across = corner_cells[corner]
    return (high if down else low), (high if across else low)


def take_frame(grid, frame, links, low, high, kept):
    for i, (tile, edge) in enumerate(strips):
        frame[8 * i : 8 * i + 8] = grid[edge_slices(tile, edge, low, high)]
    for tile in range(3):
        for corner in range(4):
            row, column = corner_at(corner, low, high)
            cell = grid[tile, row, column : column + 1, :]
            if kept:
                cell = jnp.where(links[tile, 12 + corner] == 4, cell, 0.0)
            at = 96 + 4 * tile + corner
            frame[at : at + 1] = cell
    frame[108:128] = jnp.zeros((20, 256), f32)


def fill_ghosts(grid, got, links):
    for i, (tile, edge) in enumerate(strips):
        grid[edge_slices(tile, edge, 0, 9)] = got[8 * i : 8 * i + 8]
    for tile in range(3):
        for corner in range(4):
            row, column = corner_at(corner, 0, 9)
            at = 96 + 4 * tile + corner
            beside = [
                8 * (4 * tile + edge) + end
                for edge, end in zip(edge_starts[corner], corner_ends[corner])
            ]
            blend = 0.5 * (got[beside[0] : beside[0] + 1] + got[beside[1] : beside[1] + 1])
            grid[tile, row, column : column + 1, :] = jnp.where(
                links[tile, 12 + corner] == 4, got[at : at + 1], blend
            )


def split_corners(grid, links):
    for tile in range(3):
        for corner in range(4):
            row, column = corner_at(corner, 0, 9)
            near_row, near_column = corner_at(corner, 1, 8)
            cell = grid[tile, row, column : column + 1, :]
            half = jnp.where(links[tile, 12 + corner] == 3, 0.5 * cell, 0.0)
            grid[tile, row, near_column : near_column + 1, :] += half
            grid[tile, near_row, column : column + 1, :] += half


def add_returns(grid, got):
    for i, (tile, edge) in enumerate(strips):
        grid[edge_slices(tile, edge, 1, 8)] += got[8 * i : 8 * i + 8]
    for tile in range(3):
        for corner in range(4):
            row, column = corner_at(corner, 1, 8)
            at = 96 + 4 * tile + corner
            grid[tile, row, column : column + 1, :] += got[at : at + 1]


def pack_frame(pack_ref, frame, frame_ref, sent_ref):
    cells = frame[...].astype(bf16)
    frame_ref[...] = cells
    sent_ref[...] = jnp.dot(pack_ref[...], cells, preferred_element_type=f32).astype(bf16)


def unpack_frame(unpack_ref, recv_ref, frame_ref, got):
    got[...] = jnp.dot(
        unpack_ref[:, :send_rows], recv_ref[...], preferred_element_type=f32
    ) + jnp.dot(unpack_ref[:, send_rows:], frame_ref[...], preferred_element_type=f32)


def convolve(grid, weights):
    total = jnp.zeros((192, 256), f32)
    for across in range(3):
        columns = grid[:, :, across : across + 8, :]
        for down in range(3):
            window = columns[:, down : down + 8].reshape(192, 256).astype(bf16)
            total += jnp.dot(window, weights[3 * down + across], preferred_element_type=f32)
    return total


def spread_back(gradient, weights, grid, column):
    grid[...] = jnp.zeros_like(grid)
    for across in range(3):
        column[...] = jnp.zeros_like(column)
        for down in range(3):
            part = lax.dot_general(
                gradient,
                weights[3 * down + across],
                (((1,), (1,)), ((), ())),
                preferred_element_type=f32,
            )
            column[:, down : down + 8] += part.reshape(3, 8, 8, 256)
        grid[:, :, across : across + 8, :] += column[...]


def halves(place, flat, pick):
    for k in range(4):
        quarter = lax.rem(place[1] + k, 4)
        side = quarter // 2 if pick == 0 else lax.rem(quarter, 2)
        yield k, jnp.where(side == 0, flat[:, :128], flat[:, 128:]).astype(bf16)


def flatten_grid(grid, flat):
    flat[300:304] = jnp.zeros((4, 256), f32)
    for tile in range(3):
        for row in range(10):
            at = 100 * tile + 10 * row
            flat[at : at + 10] = grid[tile, row]


def route_kernel(place, links, field_ref, pack_ref, unpack_ref, frame_ref, sent_ref, grid, frame):
    here = place[0]

    def rows_of(tiles, sides, valid, base, width, local_base):
        device = [tile // 3 for tile in tiles]
        source = [lax.rem(tile, 3) * 4 + side for tile, side in zip(tiles, sides)]
        out = []
        for i in range(12):
            send_rank = take_rank = jnp.int32(0)
            for j in range(12):
                near = (device[j] == device[i]) & valid[j]
                if j < i:
                    send_rank += jnp.where(near, width, 0)
                if j != i:
                    take_rank += jnp.where(near & (source[j] < source[i]), width, 0)
            first = device[i] * slot_rows + base
            own = device[i] == here
            send = jnp.where(own | ~valid[i], -1000, first + send_rank)
            take = jnp.where(own, local_base + source[i] * width, first + take_rank)
            out.append((send, jnp.where(valid[i], take, -1000)))
        return out

    codes = [links[tile, 4 + edge] for tile, edge in strips]
    edges = rows_of(
        [links[tile, edge] for tile, edge in strips],
        [lax.rem(code, 4) for code in codes],
        [links[tile, edge] >= 0 for tile, edge in strips],
        0,
        8,
        send_rows,
    )
    across = [links[tile, 8 + corner] for tile, corner in strips]
    corners = rows_of(
        [jnp.maximum(c, 0) // 4 for c in across],
        [lax.rem(jnp.maximum(c, 0), 4) for c in across],
        [c >= 0 for c in across],
        24,
        1,
        send_rows + 96,
    )
    lane = lax.broadcasted_iota(jnp.int32, (8, 128), 1)
    row = lax.broadcasted_iota(jnp.int32, (128, 128), 0)
    send = jnp.full((8, 128), -1000, jnp.int32)
    take = jnp.full((128, 128), -1000, jnp.int32)
    for i in range(12):
        send = jnp.where(lane // 8 == i, edges[i][0] + lane % 8, send)
        send = jnp.where(lane == 96 + i, corners[i][0], send)
        turned = codes[i] // 4 == 1
        step = jnp.where(turned, 7 - row % 8, row % 8)
        take = jnp.where(row // 8 == i, edges[i][1] + step, take)
        take = jnp.where(row == 96 + i, corners[i][1], take)
    slot = lax.broadcasted_iota(jnp.int32, (send_rows, 128), 0)
    pack_ref[...] = jnp.where(slot == send[:1], 1.0, 0.0).astype(bf16)
    column = lax.broadcasted_iota(jnp.int32, (128, 128), 1)
    for m in range(9):
        unpack_ref[:, 128 * m : 128 * m + 128] = jnp.where(
            take == column + 128 * m, 1.0, 0.0
        ).astype(bf16)
    grid[:, 1:9, 1:9, :] = field_ref[...].astype(f32).reshape(3, 8, 8, 256)
    take_frame(grid, frame, links, 1, 8, False)
    pack_frame(pack_ref, frame, frame_ref, sent_ref)


def first_kernel(
    place, links, field_ref, recv_ref, old_ref, pack_ref, unpack_ref, weights,
    hidden_ref, pre_ref, frame_ref, sent_ref, part0, part1, part2, part3,
    grid, frame, got, flat,
):
    unpack_frame(unpack_ref, recv_ref, old_ref, got)
    grid[:, 1:9, 1:9, :] = field_ref[...].astype(f32).reshape(3, 8, 8, 256)
    fill_ghosts(grid, got, links)
    pre_first = convolve(grid, weights)
    pre_ref[...] = pre_first
    hidden = gelu_value(pre_first).astype(bf16)
    hidden_ref[...] = hidden
    flatten_grid(grid, flat)
    grid[:, 1:9, 1:9, :] = hidden.astype(f32).reshape(3, 8, 8, 256)
    take_frame(grid, frame, links, 1, 8, False)
    pack_frame(pack_ref, frame, frame_ref, sent_ref)
    parts = (part0, part1, part2, part3)
    for k, half in halves(place, flat, 0):
        parts[k][...] = half


def second_kernel(
    place, links, field_ref, goal_ref, hidden_ref, recv_ref, old_ref, pack_ref, unpack_ref, weights,
    held0, held1, held2,
    state_ref, misfit_ref, inner_ref, frame_ref, sent_ref, part0, part1, part2, part3,
    grid, frame, got, flat, column,
):
    unpack_frame(unpack_ref, recv_ref, old_ref, got)
    grid[:, 1:9, 1:9, :] = hidden_ref[...].astype(f32).reshape(3, 8, 8, 256)
    fill_ghosts(grid, got, links)
    states = field_ref[...].astype(f32) + convolve(grid, weights)
    state_ref[...] = states.astype(bf16)
    misfit = states - goal_ref[...].astype(f32)
    misfit_ref[...] = misfit
    low = misfit.astype(bf16)
    flatten_grid(grid, flat)
    spread_back(low, weights, grid, column)
    split_corners(grid, links)
    take_frame(grid, frame, links, 0, 9, True)
    pack_frame(pack_ref, frame, frame_ref, sent_ref)
    inner_ref[...] = grid[:, 1:9, 1:9, :]
    parts = (part0, part1, part2, part3)
    for k, half in halves(place, flat, 0):
        parts[k][:304] = half
    for k, half in halves(place, low.astype(f32), 1):
        parts[k][304:] = half


def third_kernel(
    place, links, inner_ref, pre_ref, recv_ref, old_ref, unpack_ref, weights, *refs,
):
    last_ref, frame_ref, part0, part1, part2, part3, grid, frame, got, column = refs[3:]
    unpack_frame(unpack_ref, recv_ref, old_ref, got)
    grid[:, 1:9, 1:9, :] = inner_ref[...]
    add_returns(grid, got)
    hidden_grad = grid[:, 1:9, 1:9, :].reshape(192, 256)
    low = (hidden_grad * gelu_slope(pre_ref[...])).astype(bf16)
    parts = (part0, part1, part2, part3)
    for k, half in halves(place, low.astype(f32), 1):
        parts[k][...] = half
    spread_back(low, weights, grid, column)
    split_corners(grid, links)
    take_frame(grid, frame, links, 0, 9, True)
    frame_ref[...] = frame[...].astype(bf16)
    last_ref[...] = grid[:, 1:9, 1:9, :]


def last_kernel(place, last_ref, misfit_ref, recv_ref, old_ref, unpack_ref, out_ref, grid, got):
    unpack_frame(unpack_ref, recv_ref, old_ref, got)
    grid[:, 1:9, 1:9, :] = last_ref[...] + misfit_ref[...].reshape(3, 8, 8, 256)
    add_returns(grid, got)
    out_ref[...] = grid[:, 1:9, 1:9, :]


moved_in = pl.BlockSpec(memory_space=pltpu.HBM)
landed = pl.BlockSpec(memory_space=pl.ANY)
left = pl.BlockSpec()
near = pl.BlockSpec(memory_space=pltpu.VMEM)
resting = pl.BlockSpec(memory_space=pltpu.HBM)
grid_shape = pltpu.VMEM((3, 10, 10, 256), f32)
frame_shape = pltpu.VMEM((128, 256), f32)
flat_shape = pltpu.VMEM((304, 256), f32)
column_shape = pltpu.VMEM((3, 10, 8, 256), f32)


def like(*shape, dtype=bf16):
    return jax.ShapeDtypeStruct(shape, dtype)


class Arriving:
    def __init__(self, ref, copy):
        self.ref, self.copy = ref, copy

    def settle(self):
        if self.copy is not None:
            self.copy.wait()
            self.copy = None

    def __getitem__(self, at):
        self.settle()
        return self.ref[at]


class Leaving:
    def __init__(self, ref, copy):
        self.ref, self.copy, self.started = ref, copy, False

    def send(self):
        if not self.started:
            self.copy.start()
            self.started = True

    def __getitem__(self, at):
        return self.ref[at]

    def __setitem__(self, at, value):
        self.ref[at] = value
        if at is Ellipsis:
            self.send()


def run(kernel, name, args, specs, outs, scratch, flops, kept=()):
    single = not isinstance(outs, tuple)
    outs = (outs,) if single else outs
    moved = [i for i, spec in enumerate(specs) if spec is moved_in or spec is landed]
    buffers = [
        (pltpu.SMEM if args[i].dtype == jnp.int32 else pltpu.VMEM)(args[i].shape, args[i].dtype)
        for i in moved
    ]
    away = [n for n in range(len(outs)) if n not in kept]
    stores = [pltpu.VMEM(outs[n].shape, outs[n].dtype) for n in away]

    def body(*refs):
        ins, refs = refs[: len(args)], refs[len(args) :]
        targets, refs = refs[: len(outs)], refs[len(outs) :]
        held, refs = refs[: len(moved)], refs[len(moved) :]
        made, refs = refs[: len(away)], refs[len(away) :]
        arrived, left_for, refs = refs[0], refs[1], refs[2:]
        copies = [
            pltpu.make_async_copy(ins[i], held[n], arrived.at[n]) for n, i in enumerate(moved)
        ]
        for copy in copies:
            copy.start()
        given = list(ins)
        for n, i in enumerate(moved):
            given[i] = Arriving(held[n], copies[n])
        results = list(targets)
        for m, n in enumerate(away):
            copy = pltpu.make_async_copy(made[m], targets[n], left_for.at[m])
            results[n] = Leaving(made[m], copy)
        kernel(placing(), *given, *results, *refs)
        for n in range(len(moved)):
            given[moved[n]].settle()
        for n in away:
            results[n].send()
        for n in away:
            results[n].copy.wait()

    made = pl.pallas_call(
        body,
        out_shape=tuple(
            pltpu.HBM(out.shape, out.dtype) if n in away else out for n, out in enumerate(outs)
        ),
        in_specs=[landed if spec is left else spec for spec in specs],
        out_specs=tuple(moved_in if n in away else near for n in range(len(outs))),
        scratch_shapes=[
            *buffers,
            *stores,
            pltpu.SemaphoreType.DMA((max(1, len(moved)),)),
            pltpu.SemaphoreType.DMA((max(1, len(away)),)),
            *scratch,
        ],
        compiler_params=pltpu.CompilerParams(vmem_limit_bytes=40 * 2**20),
        cost_estimate=pl.CostEstimate(flops=flops, bytes_accessed=3000000, transcendentals=0),
        name=name,
    )(
        *[
            pltpu.with_memory_space_constraint(arg, pltpu.HBM)
            if spec is moved_in or spec is resting
            else arg
            for arg, spec in zip(args, specs)
        ]
    )
    return made[0] if single else made


def slope_kernel(split, place, *refs):
    count = 4 if split else 8
    parts = refs[:count]
    kept_ref, sent_ref, flat, wide, total = refs[count:]
    grads = []
    for n in range(4):
        flat[304 * n : 304 * n + 304] = parts[n][:304].astype(f32)
        grads.append(parts[n][304:] if split else parts[4 + n][...])
    grads = jnp.concatenate(grads, axis=0)
    low = place[2] == 0
    for across in range(3):
        for n in range(4):
            for tile in range(3):
                for row in range(10):
                    at = 304 * n + 100 * tile + 10 * row + across
                    wide[3 * n + tile, row] = flat[at : at + 8]
        for down in range(3):
            window = wide[:, down : down + 8].reshape(768, 128).astype(bf16)
            out = lax.dot_general(
                window, grads, (((0,), (0,)), ((), ())), preferred_element_type=f32
            )
            tap = (3 * down + across) * 64
            total[0, tap : tap + 64] = jnp.where(low, out[:64], out[64:])
            total[1, tap : tap + 64] = jnp.where(low, out[64:], out[:64])
    for j in range(4):
        kept_ref[j] = total[0, 144 * j : 144 * j + 144]
        sent_ref[j] = total[1, 144 * j : 144 * j + 144]


def slope_terms(parts, split, packing=(), held=()):
    shape = like(4, 144, 128, dtype=f32)
    count = len(parts)
    outs = (shape, shape) + ((like(send_rows, 256),) if packing else ())

    def kernel(place, *refs):
        ins, refs = refs[: count + len(packing)], refs[count + len(packing) + len(held) :]
        if packing:
            pack_ref, frame_ref = ins[count:]
            refs[2][...] = jnp.dot(
                pack_ref[...], frame_ref[...], preferred_element_type=f32
            ).astype(bf16)
        slope_kernel(split, place, *ins[:count], *refs[:2], *refs[len(outs) :])

    return run(
        kernel,
        "slope_terms",
        (*parts, *packing, *held),
        ([moved_in] + [landed] * 3) * (count // 4 - 1)
        + [near] * 4
        + [near] * len(packing)
        + [near] * len(held),
        outs,
        [
            pltpu.VMEM((1216, 128), f32),
            pltpu.VMEM((12, 10, 8, 128), f32),
            pltpu.VMEM((2, 576, 128), f32),
        ],
        2 * 9 * 768 * 128 * 128,
        tuple(range(len(outs))),
    )


def ring(parts, axis):
    return [shifted(part, axis, k) if k else part for k, part in enumerate(parts)]


def pair_kernel(place, kept0, got0, kept1, got1, *chunks):
    for k in range(4):
        at = lax.rem(place[3] + k, 4)
        chunks[k][:144] = kept0[at] + got0[at]
        chunks[k][144:] = kept1[at] + got1[at]


def plane_kernel(place, own, part1, part2, part3, held, out, total):
    total[...] = (own[...] + part1[...]) + (part2[...] + part3[...])
    for j in range(8):
        out[j] = total[36 * j : 36 * j + 36]


def spread_kernel(place, own, other, first_ref, second_ref):
    low = place[2] == 0
    for n, out in enumerate((first_ref, second_ref)):
        at = slice(144 * n, 144 * n + 144)
        for x in range(4):
            row, column = 128 * (x // 2), 128 * (x % 2)
            pair = [
                jnp.concatenate(
                    [part[4 * x + y, at].astype(f32) for y in range(4)], axis=0
                ).reshape(9, 64, 128)
                for part in (own, other)
            ]
            out[:, row : row + 64, column : column + 128] = jnp.where(low, pair[0], pair[1])
            out[:, row + 64 : row + 128, column : column + 128] = jnp.where(low, pair[1], pair[0])
        out.send()


def groups(along):
    axes = ("x", "y", "z", "core")
    out = []
    for fixed in itertools.product(*[range(1 if a in along else sizes[a]) for a in axes]):
        group = []
        for moving in itertools.product(*[range(sizes[a]) for a in along]):
            at = dict(zip(axes, fixed)) | dict(zip(along, moving))
            group.append(place_of(**at))
        out.append(group)
    return out


def trade(values, *along):
    return lax.all_to_all(
        values, ("tile", "ens"), 0, 0, axis_index_groups=groups(along), tiled=True
    )


def copies_of(values, count):
    return jnp.broadcast_to(values[None], (count,) + values.shape)


def finish_slopes(chunks, held, scale):
    terms = run(
        plane_kernel,
        "row_sum",
        (*ring(chunks, "y"), held),
        [near] * 4 + [left],
        like(8, 36, 128, dtype=f32),
        [pltpu.VMEM((288, 128), f32)],
        1000,
        (0,),
    )
    mine = (jnp.sum(trade(terms, "z"), axis=0) * scale).astype(bf16)
    line = trade(copies_of(mine, 8), "z").reshape(288, 128)
    plane = trade(copies_of(line, 16), "x", "y")
    shape = like(9, 256, 256, dtype=f32)
    return run(
        spread_kernel,
        "spread_slopes",
        (plane, shifted(plane, "core", 1)),
        [landed, landed],
        (shape, shape),
        [],
        1000,
    )


def exchange(values):
    return lax.all_to_all(values, "tile", 0, 0, tiled=True)


def per_device(network_conditions, subsequent_targets, w_first, w_second, tile_links):
    field = network_conditions.reshape(192, 256)
    goal = subsequent_targets.reshape(192, 256)
    first_weights, second_weights = w_first.reshape(9, 256, 256), w_second.reshape(9, 256, 256)
    scale = 1.0 / math.sqrt(lax.axis_size("ens") * lax.axis_size("tile") * 192)
    frame_like, sent_like, rows_like = like(128, 256), like(send_rows, 256), like(192, 256)
    inner_like = like(3, 8, 8, 256, dtype=f32)
    conv_flops = 2 * 9 * 192 * 256 * 256

    pack, unpack, frame, sent = run(
        route_kernel,
        "routes",
        (tile_links, field),
        [moved_in, moved_in],
        (like(send_rows, 128), like(128, send_rows + 128), frame_like, sent_like),
        [grid_shape, frame_shape],
        2 * send_rows * 128 * 256,
        (0,1,2,3),
    )
    recv = exchange(sent)
    hidden, pre_first, frame, sent, *parts = run(
        first_kernel,
        "first_layer",
        (tile_links, field, recv, frame, pack, unpack, first_weights),
        [moved_in] * 2 + [near] * 4 + [moved_in],
        (rows_like, like(192, 256, dtype=f32), frame_like, sent_like) + (like(304, 128),) * 4,
        [grid_shape, frame_shape, frame_shape, flat_shape],
        conv_flops,
        (0,2,3,5,6,7),
    )
    recv = exchange(sent)
    field_parts = ring(parts, "x")
    states, misfit, inner, frame, sent, *parts = run(
        second_kernel,
        "second_layer",
        (
            tile_links, field, goal, hidden, recv, frame, pack, unpack, second_weights,
            *field_parts[1:],
        ),
        [moved_in] * 3 + [near] * 5 + [moved_in] + [left] * 3,
        (rows_like, like(192, 256, dtype=f32), inner_like, frame_like, sent_like)
        + (like(496, 128),) * 4,
        [grid_shape, frame_shape, frame_shape, flat_shape, column_shape],
        2 * conv_flops,
        (2,3,4,5,6,7,8),
    )
    recv = exchange(sent)
    closing_parts = ring(parts, "x")
    closing = slope_terms(closing_parts, True)
    last, frame, *parts = run(
        third_kernel,
        "first_gradient",
        (tile_links, inner, pre_first, recv, frame, unpack, first_weights, *closing_parts[1:]),
        [moved_in, near, moved_in] + [near] * 3 + [moved_in] + [left] * 3,
        (inner_like, frame_like) + (like(192, 128),) * 4,
        [grid_shape, frame_shape, frame_shape, column_shape],
        conv_flops,
        (1,2,3,4,5),
    )
    got_closing = shifted(closing[1], "core", 1)
    *opening, sent = slope_terms(
        field_parts + ring(parts, "x"), False, (pack, frame), (closing[0],)
    )
    recv = exchange(sent)
    chunks = run(
        pair_kernel,
        "pair_sum",
        (opening[0], shifted(opening[1], "core", 1), closing[0], got_closing),
        [near] * 4,
        (like(288, 128, dtype=f32),) * 4,
        [],
        1000,
        (0, 1, 2, 3),
    )
    condition_derivative = run(
        last_kernel,
        "last_gradient",
        (last, misfit, recv, frame, unpack),
        [moved_in] * 2 + [near] * 3,
        inner_like,
        [grid_shape, frame_shape],
        1000,
    )
    slopes = finish_slopes(chunks, recv, scale)
    return (
        states.reshape(network_conditions.shape),
        condition_derivative[None],
        slopes[0].reshape(w_first.shape),
        slopes[1].reshape(w_second.shape),
    )


def solution(mesh):
    return jax.shard_map(
        per_device,
        mesh=mesh,
        in_specs=(
            P("ens", "tile", None, None, None),
            P("ens", "tile", None, None, None),
            P(),
            P(),
            P("tile", None),
        ),
        out_specs=(
            P("ens", "tile", None, None, None),
            P("ens", "tile", None, None, None),
            P(),
            P(),
        ),
        check_vma=False,
    )
```

```python
import functools
import itertools
import math

import jax
import jax.numpy as jnp
from jax import lax
from jax.experimental import pallas as pl
from jax.experimental.pallas import tpu as pltpu
from jax.sharding import PartitionSpec as P

tanh_scale = 0.7978845608028654
cubic_term = 0.044715
slot_rows = 32
send_rows = 1024
bf16, f32 = jnp.bfloat16, jnp.float32


def gelu_value(inputs):
    return (
        0.5
        * inputs
        * (1.0 + jnp.tanh(tanh_scale * (inputs + cubic_term * inputs * inputs * inputs)))
    )


def gelu_slope(inputs):
    tangent = jnp.tanh(tanh_scale * (inputs + cubic_term * inputs * inputs * inputs))
    return 0.5 * (1.0 + tangent) + 0.5 * inputs * (1.0 - tangent * tangent) * tanh_scale * (
        1.0 + 3.0 * cubic_term * inputs * inputs
    )


sizes = {"x": 4, "y": 4, "z": 8, "core": 2}


def place_of(x, y, z, core):
    return ((y * 2 + z % 2) * 4 + x) * 8 + (z // 2) * 2 + core


def moved_to(values, axis, target):
    pairs = []
    for x in range(4):
        for y in range(4):
            for z in range(8):
                for core in range(2):
                    at = {"x": x, "y": y, "z": z, "core": core}
                    to = dict(at)
                    to[axis] = target(at[axis])
                    pairs.append((place_of(**at), place_of(**to)))
    return lax.ppermute(values, ("tile", "ens"), pairs)


def shifted(values, axis, by):
    return moved_to(values, axis, lambda at: (at + by) % sizes[axis])


def mirrored(values, bit):
    return moved_to(values, "z", lambda at: at ^ (1 << bit))


def placing():
    tile, ens = lax.axis_index("tile"), lax.axis_index("ens")
    z = (ens // 2) * 2 + lax.rem(tile // 4, 2)
    return tile, lax.rem(tile, 4), lax.rem(ens, 2), tile // 8, z


edge_starts = ((0, 3), (0, 1), (1, 2), (2, 3))
corner_ends = ((0, 0), (7, 0), (7, 7), (0, 7))
corner_cells = ((0, 0), (0, 1), (1, 1), (1, 0))
strips = [(tile, edge) for tile in range(3) for edge in range(4)]


def edge_slices(tile, edge, low, high):
    inner = slice(1, 9)
    return (
        (tile, low, inner),
        (tile, inner, high),
        (tile, high, inner),
        (tile, inner, low),
    )[edge]


def corner_at(corner, low, high):
    down, across = corner_cells[corner]
    return (high if down else low), (high if across else low)


def take_frame(grid, frame, links, low, high, kept):
    for i, (tile, edge) in enumerate(strips):
        frame[8 * i : 8 * i + 8] = grid[edge_slices(tile, edge, low, high)]
    for tile in range(3):
        for corner in range(4):
            row, column = corner_at(corner, low, high)
            cell = grid[tile, row, column : column + 1, :]
            if kept:
                cell = jnp.where(links[tile, 12 + corner] == 4, cell, 0.0)
            at = 96 + 4 * tile + corner
            frame[at : at + 1] = cell
    frame[108:128] = jnp.zeros((20, 256), f32)


def fill_ghosts(grid, got, links):
    for i, (tile, edge) in enumerate(strips):
        grid[edge_slices(tile, edge, 0, 9)] = got[8 * i : 8 * i + 8]
    for tile in range(3):
        for corner in range(4):
            row, column = corner_at(corner, 0, 9)
            at = 96 + 4 * tile + corner
            beside = [
                8 * (4 * tile + edge) + end
                for edge, end in zip(edge_starts[corner], corner_ends[corner])
            ]
            blend = 0.5 * (got[beside[0] : beside[0] + 1] + got[beside[1] : beside[1] + 1])
            grid[tile, row, column : column + 1, :] = jnp.where(
                links[tile, 12 + corner] == 4, got[at : at + 1], blend
            )


def split_corners(grid, links):
    for tile in range(3):
        for corner in range(4):
            row, column = corner_at(corner, 0, 9)
            near_row, near_column = corner_at(corner, 1, 8)
            cell = grid[tile, row, column : column + 1, :]
            half = jnp.where(links[tile, 12 + corner] == 3, 0.5 * cell, 0.0)
            grid[tile, row, near_column : near_column + 1, :] += half
            grid[tile, near_row, column : column + 1, :] += half


def add_returns(grid, got):
    for i, (tile, edge) in enumerate(strips):
        grid[edge_slices(tile, edge, 1, 8)] += got[8 * i : 8 * i + 8]
    for tile in range(3):
        for corner in range(4):
            row, column = corner_at(corner, 1, 8)
            at = 96 + 4 * tile + corner
            grid[tile, row, column : column + 1, :] += got[at : at + 1]


def pack_frame(pack_ref, frame, frame_ref, sent_ref):
    cells = frame[...].astype(bf16)
    frame_ref[...] = cells
    sent_ref[...] = jnp.dot(pack_ref[...], cells, preferred_element_type=f32).astype(bf16)


def unpack_frame(unpack_ref, recv_ref, frame_ref, got):
    got[...] = jnp.dot(
        unpack_ref[:, :send_rows], recv_ref[...], preferred_element_type=f32
    ) + jnp.dot(unpack_ref[:, send_rows:], frame_ref[...], preferred_element_type=f32)


def convolve(grid, weights):
    total = jnp.zeros((192, 256), f32)
    for across in range(3):
        columns = grid[:, :, across : across + 8, :]
        for down in range(3):
            window = columns[:, down : down + 8].reshape(192, 256).astype(bf16)
            total += jnp.dot(window, weights[3 * down + across], preferred_element_type=f32)
    return total


def spread_back(gradient, weights, grid, column):
    grid[...] = jnp.zeros_like(grid)
    for across in range(3):
        column[...] = jnp.zeros_like(column)
        for down in range(3):
            part = lax.dot_general(
                gradient,
                weights[3 * down + across],
                (((1,), (1,)), ((), ())),
                preferred_element_type=f32,
            )
            column[:, down : down + 8] += part.reshape(3, 8, 8, 256)
        grid[:, :, across : across + 8, :] += column[...]


def halves(place, flat, pick):
    for k in range(4):
        quarter = lax.rem(place[1] + k, 4)
        side = quarter // 2 if pick == 0 else lax.rem(quarter, 2)
        yield k, jnp.where(side == 0, flat[:, :128], flat[:, 128:]).astype(bf16)


def flatten_grid(grid, flat):
    flat[300:304] = jnp.zeros((4, 256), f32)
    for tile in range(3):
        for row in range(10):
            at = 100 * tile + 10 * row
            flat[at : at + 10] = grid[tile, row]


def route_kernel(place, links, field_ref, pack_ref, unpack_ref, frame_ref, sent_ref, grid, frame):
    here = place[0]

    def rows_of(tiles, sides, valid, base, width, local_base):
        device = [tile // 3 for tile in tiles]
        source = [lax.rem(tile, 3) * 4 + side for tile, side in zip(tiles, sides)]
        out = []
        for i in range(12):
            send_rank = take_rank = jnp.int32(0)
            for j in range(12):
                near = (device[j] == device[i]) & valid[j]
                if j < i:
                    send_rank += jnp.where(near, width, 0)
                if j != i:
                    take_rank += jnp.where(near & (source[j] < source[i]), width, 0)
            first = device[i] * slot_rows + base
            own = device[i] == here
            send = jnp.where(own | ~valid[i], -1000, first + send_rank)
            take = jnp.where(own, local_base + source[i] * width, first + take_rank)
            out.append((send, jnp.where(valid[i], take, -1000)))
        return out

    codes = [links[tile, 4 + edge] for tile, edge in strips]
    edges = rows_of(
        [links[tile, edge] for tile, edge in strips],
        [lax.rem(code, 4) for code in codes],
        [links[tile, edge] >= 0 for tile, edge in strips],
        0,
        8,
        send_rows,
    )
    across = [links[tile, 8 + corner] for tile, corner in strips]
    corners = rows_of(
        [jnp.maximum(c, 0) // 4 for c in across],
        [lax.rem(jnp.maximum(c, 0), 4) for c in across],
        [c >= 0 for c in across],
        24,
        1,
        send_rows + 96,
    )
    lane = lax.broadcasted_iota(jnp.int32, (8, 128), 1)
    row = lax.broadcasted_iota(jnp.int32, (128, 128), 0)
    send = jnp.full((8, 128), -1000, jnp.int32)
    take = jnp.full((128, 128), -1000, jnp.int32)
    for i in range(12):
        send = jnp.where(lane // 8 == i, edges[i][0] + lane % 8, send)
        send = jnp.where(lane == 96 + i, corners[i][0], send)
        turned = codes[i] // 4 == 1
        step = jnp.where(turned, 7 - row % 8, row % 8)
        take = jnp.where(row // 8 == i, edges[i][1] + step, take)
        take = jnp.where(row == 96 + i, corners[i][1], take)
    slot = lax.broadcasted_iota(jnp.int32, (send_rows, 128), 0)
    pack_ref[...] = jnp.where(slot == send[:1], 1.0, 0.0).astype(bf16)
    column = lax.broadcasted_iota(jnp.int32, (128, 128), 1)
    for m in range(9):
        unpack_ref[:, 128 * m : 128 * m + 128] = jnp.where(
            take == column + 128 * m, 1.0, 0.0
        ).astype(bf16)
    grid[:, 1:9, 1:9, :] = field_ref[...].astype(f32).reshape(3, 8, 8, 256)
    take_frame(grid, frame, links, 1, 8, False)
    pack_frame(pack_ref, frame, frame_ref, sent_ref)


def first_kernel(
    place, links, field_ref, recv_ref, old_ref, pack_ref, unpack_ref, weights,
    hidden_ref, pre_ref, frame_ref, sent_ref, part0, part1, part2, part3,
    grid, frame, got, flat,
):
    unpack_frame(unpack_ref, recv_ref, old_ref, got)
    grid[:, 1:9, 1:9, :] = field_ref[...].astype(f32).reshape(3, 8, 8, 256)
    fill_ghosts(grid, got, links)
    pre_first = convolve(grid, weights)
    pre_ref[...] = pre_first
    hidden = gelu_value(pre_first).astype(bf16)
    hidden_ref[...] = hidden
    flatten_grid(grid, flat)
    grid[:, 1:9, 1:9, :] = hidden.astype(f32).reshape(3, 8, 8, 256)
    take_frame(grid, frame, links, 1, 8, False)
    pack_frame(pack_ref, frame, frame_ref, sent_ref)
    parts = (part0, part1, part2, part3)
    for k, half in halves(place, flat, 0):
        parts[k][...] = half


def second_kernel(
    place, links, field_ref, goal_ref, hidden_ref, recv_ref, old_ref, pack_ref, unpack_ref, weights,
    held0, held1, held2,
    state_ref, misfit_ref, inner_ref, frame_ref, sent_ref, part0, part1, part2, part3,
    grid, frame, got, flat, column,
):
    unpack_frame(unpack_ref, recv_ref, old_ref, got)
    grid[:, 1:9, 1:9, :] = hidden_ref[...].astype(f32).reshape(3, 8, 8, 256)
    fill_ghosts(grid, got, links)
    states = field_ref[...].astype(f32) + convolve(grid, weights)
    state_ref[...] = states.astype(bf16)
    misfit = states - goal_ref[...].astype(f32)
    misfit_ref[...] = misfit
    low = misfit.astype(bf16)
    flatten_grid(grid, flat)
    spread_back(low, weights, grid, column)
    split_corners(grid, links)
    take_frame(grid, frame, links, 0, 9, True)
    pack_frame(pack_ref, frame, frame_ref, sent_ref)
    inner_ref[...] = grid[:, 1:9, 1:9, :]
    parts = (part0, part1, part2, part3)
    for k, half in halves(place, flat, 0):
        parts[k][:304] = half
    for k, half in halves(place, low.astype(f32), 1):
        parts[k][304:] = half


def third_kernel(
    place, links, inner_ref, pre_ref, recv_ref, old_ref, unpack_ref, weights, *refs,
):
    last_ref, frame_ref, part0, part1, part2, part3, grid, frame, got, column = refs[3:]
    unpack_frame(unpack_ref, recv_ref, old_ref, got)
    grid[:, 1:9, 1:9, :] = inner_ref[...]
    add_returns(grid, got)
    hidden_grad = grid[:, 1:9, 1:9, :].reshape(192, 256)
    low = (hidden_grad * gelu_slope(pre_ref[...])).astype(bf16)
    parts = (part0, part1, part2, part3)
    for k, half in halves(place, low.astype(f32), 1):
        parts[k][...] = half
    spread_back(low, weights, grid, column)
    split_corners(grid, links)
    take_frame(grid, frame, links, 0, 9, True)
    frame_ref[...] = frame[...].astype(bf16)
    last_ref[...] = grid[:, 1:9, 1:9, :]


def last_kernel(place, last_ref, misfit_ref, recv_ref, old_ref, unpack_ref, out_ref, grid, got):
    unpack_frame(unpack_ref, recv_ref, old_ref, got)
    grid[:, 1:9, 1:9, :] = last_ref[...] + misfit_ref[...].reshape(3, 8, 8, 256)
    add_returns(grid, got)
    out_ref[...] = grid[:, 1:9, 1:9, :]


moved_in = pl.BlockSpec(memory_space=pltpu.HBM)
landed = pl.BlockSpec(memory_space=pl.ANY)
left = pl.BlockSpec()
near = pl.BlockSpec(memory_space=pltpu.VMEM)
resting = pl.BlockSpec(memory_space=pltpu.HBM)
grid_shape = pltpu.VMEM((3, 10, 10, 256), f32)
frame_shape = pltpu.VMEM((128, 256), f32)
flat_shape = pltpu.VMEM((304, 256), f32)
column_shape = pltpu.VMEM((3, 10, 8, 256), f32)


def like(*shape, dtype=bf16):
    return jax.ShapeDtypeStruct(shape, dtype)


class Arriving:
    def __init__(self, ref, copy):
        self.ref, self.copy = ref, copy

    def settle(self):
        if self.copy is not None:
            self.copy.wait()
            self.copy = None

    def __getitem__(self, at):
        self.settle()
        return self.ref[at]


class ArrivingTaps:
    def __init__(self, ref, copies):
        self.taps = [Arriving(ref.at[tap], copies[tap]) for tap in range(9)]

    def settle(self):
        for tap in self.taps:
            tap.settle()

    def __getitem__(self, tap):
        return self.taps[tap][...]


class Leaving:
    def __init__(self, ref, copy):
        self.ref, self.copy, self.started = ref, copy, False

    def send(self):
        if not self.started:
            self.copy.start()
            self.started = True

    def __getitem__(self, at):
        return self.ref[at]

    def __setitem__(self, at, value):
        self.ref[at] = value
        if at is Ellipsis:
            self.send()


def run(kernel, name, args, specs, outs, scratch, flops, kept=()):
    single = not isinstance(outs, tuple)
    outs = (outs,) if single else outs
    moved = [i for i, spec in enumerate(specs) if spec is moved_in or spec is landed]
    buffers = [
        (pltpu.SMEM if args[i].dtype == jnp.int32 else pltpu.VMEM)(args[i].shape, args[i].dtype)
        for i in moved
    ]
    away = [n for n in range(len(outs)) if n not in kept]
    stores = [pltpu.VMEM(outs[n].shape, outs[n].dtype) for n in away]

    def body(*refs):
        ins, refs = refs[: len(args)], refs[len(args) :]
        targets, refs = refs[: len(outs)], refs[len(outs) :]
        held, refs = refs[: len(moved)], refs[len(moved) :]
        made, refs = refs[: len(away)], refs[len(away) :]
        arrived, left_for, by_tap, refs = refs[0], refs[1], refs[2], refs[3:]
        copies = {}
        for n, i in enumerate(moved):
            if args[i].shape[0] != 9:
                copies[n] = pltpu.make_async_copy(ins[i], held[n], arrived.at[n])
                copies[n].start()
        for n, i in enumerate(moved):
            if args[i].shape[0] == 9:
                copies[n] = {}
                for across in range(3):
                    for tap in range(across, 9, 3):
                        copies[n][tap] = pltpu.make_async_copy(
                            ins[i].at[tap], held[n].at[tap], by_tap.at[tap]
                        )
                        copies[n][tap].start()
        given = list(ins)
        for n, i in enumerate(moved):
            kind = ArrivingTaps if args[i].shape[0] == 9 else Arriving
            given[i] = kind(held[n], copies[n])
        results = list(targets)
        for m, n in enumerate(away):
            copy = pltpu.make_async_copy(made[m], targets[n], left_for.at[m])
            results[n] = Leaving(made[m], copy)
        kernel(placing(), *given, *results, *refs)
        for n in range(len(moved)):
            given[moved[n]].settle()
        for n in away:
            results[n].send()
        for n in away:
            results[n].copy.wait()

    made = pl.pallas_call(
        body,
        out_shape=tuple(
            pltpu.HBM(out.shape, out.dtype) if n in away else out for n, out in enumerate(outs)
        ),
        in_specs=[landed if spec is left else spec for spec in specs],
        out_specs=tuple(moved_in if n in away else near for n in range(len(outs))),
        scratch_shapes=[
            *buffers,
            *stores,
            pltpu.SemaphoreType.DMA((max(1, len(moved)),)),
            pltpu.SemaphoreType.DMA((max(1, len(away)),)),
            pltpu.SemaphoreType.DMA((9,)),
            *scratch,
        ],
        compiler_params=pltpu.CompilerParams(vmem_limit_bytes=40 * 2**20),
        cost_estimate=pl.CostEstimate(flops=flops, bytes_accessed=3000000, transcendentals=0),
        name=name,
    )(
        *[
            pltpu.with_memory_space_constraint(arg, pltpu.HBM)
            if spec is moved_in or spec is resting
            else arg
            for arg, spec in zip(args, specs)
        ]
    )
    return made[0] if single else made


def slope_kernel(split, place, *refs):
    count = 4 if split else 8
    parts = refs[:count]
    kept_ref, sent_ref, flat, wide, total = refs[count:]
    grads = []
    for n in range(4):
        flat[304 * n : 304 * n + 304] = parts[n][:304].astype(f32)
        grads.append(parts[n][304:] if split else parts[4 + n][...])
    grads = jnp.concatenate(grads, axis=0)
    low = place[2] == 0
    for across in range(3):
        for n in range(4):
            for tile in range(3):
                for row in range(10):
                    at = 304 * n + 100 * tile + 10 * row + across
                    wide[3 * n + tile, row] = flat[at : at + 8]
        for down in range(3):
            window = wide[:, down : down + 8].reshape(768, 128).astype(bf16)
            out = lax.dot_general(
                window, grads, (((0,), (0,)), ((), ())), preferred_element_type=f32
            )
            tap = (3 * down + across) * 64
            total[0, tap : tap + 64] = jnp.where(low, out[:64], out[64:])
            total[1, tap : tap + 64] = jnp.where(low, out[64:], out[:64])
    for j in range(4):
        kept_ref[j] = total[0, 144 * j : 144 * j + 144]
        sent_ref[j] = total[1, 144 * j : 144 * j + 144]


def slope_terms(parts, split, packing=(), held=()):
    shape = like(4, 144, 128, dtype=f32)
    count = len(parts)
    outs = (shape, shape) + ((like(send_rows, 256),) if packing else ())

    def kernel(place, *refs):
        ins, refs = refs[: count + len(packing)], refs[count + len(packing) + len(held) :]
        if packing:
            pack_ref, frame_ref = ins[count:]
            refs[2][...] = jnp.dot(
                pack_ref[...], frame_ref[...], preferred_element_type=f32
            ).astype(bf16)
        slope_kernel(split, place, *ins[:count], *refs[:2], *refs[len(outs) :])

    return run(
        kernel,
        "slope_terms",
        (*parts, *packing, *held),
        ([moved_in] + [landed] * 3) * (count // 4 - 1)
        + [near] * 4
        + [near] * len(packing)
        + [near] * len(held),
        outs,
        [
            pltpu.VMEM((1216, 128), f32),
            pltpu.VMEM((12, 10, 8, 128), f32),
            pltpu.VMEM((2, 576, 128), f32),
        ],
        2 * 9 * 768 * 128 * 128,
        tuple(range(len(outs))),
    )


def ring(parts, axis):
    return [shifted(part, axis, k) if k else part for k, part in enumerate(parts)]


def pair_kernel(place, kept0, got0, kept1, got1, *chunks):
    for k in range(4):
        at = lax.rem(place[3] + k, 4)
        chunks[k][:144] = kept0[at] + got0[at]
        chunks[k][144:] = kept1[at] + got1[at]


def bit_of(place, bit):
    return lax.rem(place[4] // (1 << bit), 2) == 0


def plane_kernel(place, own, part1, part2, part3, held, kept, sent):
    total = (own[...] + part1[...]) + (part2[...] + part3[...])
    low = bit_of(place, 0)
    kept[...] = jnp.where(low, total[:144], total[144:])
    sent[...] = jnp.where(low, total[144:], total[:144])


def halve_kernel(bit, place, own, got, kept, sent, total):
    half = own.shape[0] // 2
    total[...] = own[...] + got[...]
    low = bit_of(place, bit)
    first, second = total[:half], total[half : 2 * half]
    kept[...] = jnp.where(low, first, second)
    sent[...] = jnp.where(low, second, first)


def round_kernel(scale, place, own, got, out):
    out[...] = ((own[...] + got[...]) * scale).astype(bf16)


def join_kernel(bit, place, own, got, out, total):
    size = own.shape[0]
    low = bit_of(place, bit)
    mine, other = own[...].astype(f32), got[...].astype(f32)
    total[:size] = jnp.where(low, mine, other)
    total[size:] = jnp.where(low, other, mine)
    out[...] = total[...].astype(bf16)


def spread_kernel(place, own, other, first_ref, second_ref):
    low = place[2] == 0
    for n, out in enumerate((first_ref, second_ref)):
        at = slice(144 * n, 144 * n + 144)
        for x in range(4):
            row, column = 128 * (x // 2), 128 * (x % 2)
            pair = [
                jnp.concatenate(
                    [part[4 * x + y, at].astype(f32) for y in range(4)], axis=0
                ).reshape(9, 64, 128)
                for part in (own, other)
            ]
            out[:, row : row + 64, column : column + 128] = jnp.where(low, pair[0], pair[1])
            out[:, row + 64 : row + 128, column : column + 128] = jnp.where(low, pair[1], pair[0])
        out.send()


def groups(along):
    axes = ("x", "y", "z", "core")
    out = []
    for fixed in itertools.product(*[range(1 if a in along else sizes[a]) for a in axes]):
        group = []
        for moving in itertools.product(*[range(sizes[a]) for a in along]):
            at = dict(zip(axes, fixed)) | dict(zip(along, moving))
            group.append(place_of(**at))
        out.append(group)
    return out


def trade(values, *along):
    return lax.all_to_all(
        values, ("tile", "ens"), 0, 0, axis_index_groups=groups(along), tiled=True
    )


def copies_of(values, count):
    return jnp.broadcast_to(values[None], (count,) + values.shape)


def finish_slopes(chunks, held, scale):
    def small(kernel, name, args, outs, scratch=()):
        specs = [near] * len(args)
        return run(kernel, name, args, specs, outs, scratch, 1000, tuple(range(len(outs))))

    def rows(count, dtype=f32):
        return like(count, 128, dtype=dtype)

    kept, sent = run(
        plane_kernel,
        "row_sum",
        (*ring(chunks, "y"), held),
        [near] * 4 + [left],
        (rows(144), rows(144)),
        [],
        1000,
        (0, 1),
    )
    for bit, count in ((1, 144), (2, 72)):
        kept, sent = small(
            functools.partial(halve_kernel, bit),
            "halve_sum",
            (kept, mirrored(sent, bit - 1)),
            (rows(count // 2),) * 2,
            [pltpu.VMEM((count, 128), f32)],
        )
    (line,) = small(
        functools.partial(round_kernel, scale),
        "round_sum",
        (kept, mirrored(sent, 2)),
        (rows(36, bf16),),
    )
    for bit, count in ((2, 72), (1, 144), (0, 288)):
        (line,) = small(
            functools.partial(join_kernel, bit),
            "join_rows",
            (line, mirrored(line, bit)),
            (rows(count, bf16),),
            [pltpu.VMEM((count, 128), f32)],
        )
    plane = trade(copies_of(line, 16), "x", "y")
    shape = like(9, 256, 256, dtype=f32)
    return run(
        spread_kernel,
        "spread_slopes",
        (plane, shifted(plane, "core", 1)),
        [landed, landed],
        (shape, shape),
        [],
        1000,
    )


def exchange(values):
    return lax.all_to_all(values, "tile", 0, 0, tiled=True)


def per_device(network_conditions, subsequent_targets, w_first, w_second, tile_links):
    field = network_conditions.reshape(192, 256)
    goal = subsequent_targets.reshape(192, 256)
    first_weights, second_weights = w_first.reshape(9, 256, 256), w_second.reshape(9, 256, 256)
    scale = 1.0 / math.sqrt(lax.axis_size("ens") * lax.axis_size("tile") * 192)
    frame_like, sent_like, rows_like = like(128, 256), like(send_rows, 256), like(192, 256)
    inner_like = like(3, 8, 8, 256, dtype=f32)
    conv_flops = 2 * 9 * 192 * 256 * 256

    pack, unpack, frame, sent = run(
        route_kernel,
        "routes",
        (tile_links, field),
        [moved_in, moved_in],
        (like(send_rows, 128), like(128, send_rows + 128), frame_like, sent_like),
        [grid_shape, frame_shape],
        2 * send_rows * 128 * 256,
        (0,1,2,3),
    )
    recv = exchange(sent)
    hidden, pre_first, frame, sent, *parts = run(
        first_kernel,
        "first_layer",
        (tile_links, field, recv, frame, pack, unpack, first_weights),
        [moved_in] * 2 + [near] * 4 + [moved_in],
        (rows_like, like(192, 256, dtype=f32), frame_like, sent_like) + (like(304, 128),) * 4,
        [grid_shape, frame_shape, frame_shape, flat_shape],
        conv_flops,
        (0,2,3,5,6,7),
    )
    recv = exchange(sent)
    field_parts = ring(parts, "x")
    states, misfit, inner, frame, sent, *parts = run(
        second_kernel,
        "second_layer",
        (
            tile_links, field, goal, hidden, recv, frame, pack, unpack, second_weights,
            *field_parts[1:],
        ),
        [moved_in] * 3 + [near] * 5 + [moved_in] + [left] * 3,
        (rows_like, like(192, 256, dtype=f32), inner_like, frame_like, sent_like)
        + (like(496, 128),) * 4,
        [grid_shape, frame_shape, frame_shape, flat_shape, column_shape],
        2 * conv_flops,
        (2,3,4,5,6,7,8),
    )
    recv = exchange(sent)
    closing_parts = ring(parts, "x")
    closing = slope_terms(closing_parts, True)
    last, frame, *parts = run(
        third_kernel,
        "first_gradient",
        (tile_links, inner, pre_first, recv, frame, unpack, first_weights, *closing_parts[1:]),
        [moved_in, near, moved_in] + [near] * 3 + [moved_in] + [left] * 3,
        (inner_like, frame_like) + (like(192, 128),) * 4,
        [grid_shape, frame_shape, frame_shape, column_shape],
        conv_flops,
        (1,2,3,4,5),
    )
    got_closing = shifted(closing[1], "core", 1)
    *opening, sent = slope_terms(
        field_parts + ring(parts, "x"), False, (pack, frame), (closing[0],)
    )
    recv = exchange(sent)
    chunks = run(
        pair_kernel,
        "pair_sum",
        (opening[0], shifted(opening[1], "core", 1), closing[0], got_closing),
        [near] * 4,
        (like(288, 128, dtype=f32),) * 4,
        [],
        1000,
        (0, 1, 2, 3),
    )
    condition_derivative = run(
        last_kernel,
        "last_gradient",
        (last, misfit, recv, frame, unpack),
        [moved_in] * 2 + [near] * 3,
        inner_like,
        [grid_shape, frame_shape],
        1000,
    )
    slopes = finish_slopes(chunks, recv, scale)
    return (
        states.reshape(network_conditions.shape),
        condition_derivative[None],
        slopes[0].reshape(w_first.shape),
        slopes[1].reshape(w_second.shape),
    )


def solution(mesh):
    return jax.shard_map(
        per_device,
        mesh=mesh,
        in_specs=(
            P("ens", "tile", None, None, None),
            P("ens", "tile", None, None, None),
            P(),
            P(),
            P("tile", None),
        ),
        out_specs=(
            P("ens", "tile", None, None, None),
            P("ens", "tile", None, None, None),
            P(),
            P(),
        ),
        check_vma=False,
    )
```

```python
import itertools
import math

import jax
import jax.numpy as jnp
from jax import lax
from jax.experimental import pallas as pl
from jax.experimental.pallas import tpu as pltpu
from jax.sharding import PartitionSpec as P

tanh_scale = 0.7978845608028654
cubic_term = 0.044715
slot_rows = 32
send_rows = 1024
bf16, f32 = jnp.bfloat16, jnp.float32


def gelu_value(inputs):
    return (
        0.5
        * inputs
        * (1.0 + jnp.tanh(tanh_scale * (inputs + cubic_term * inputs * inputs * inputs)))
    )


def gelu_slope(inputs):
    tangent = jnp.tanh(tanh_scale * (inputs + cubic_term * inputs * inputs * inputs))
    return 0.5 * (1.0 + tangent) + 0.5 * inputs * (1.0 - tangent * tangent) * tanh_scale * (
        1.0 + 3.0 * cubic_term * inputs * inputs
    )


sizes = {"x": 4, "y": 4, "z": 8, "core": 2}


def place_of(x, y, z, core):
    return ((y * 2 + z % 2) * 4 + x) * 8 + (z // 2) * 2 + core


def shifted(values, axis, by):
    pairs = []
    for x in range(4):
        for y in range(4):
            for z in range(8):
                for core in range(2):
                    at = {"x": x, "y": y, "z": z, "core": core}
                    to = dict(at)
                    to[axis] = (at[axis] + by) % sizes[axis]
                    pairs.append((place_of(**at), place_of(**to)))
    return lax.ppermute(values, ("tile", "ens"), pairs)


def placing():
    tile, ens = lax.axis_index("tile"), lax.axis_index("ens")
    return tile, lax.rem(tile, 4), lax.rem(ens, 2), tile // 8


edge_starts = ((0, 3), (0, 1), (1, 2), (2, 3))
corner_ends = ((0, 0), (7, 0), (7, 7), (0, 7))
corner_cells = ((0, 0), (0, 1), (1, 1), (1, 0))
strips = [(tile, edge) for tile in range(3) for edge in range(4)]


def edge_slices(tile, edge, low, high):
    inner = slice(1, 9)
    return (
        (tile, low, inner),
        (tile, inner, high),
        (tile, high, inner),
        (tile, inner, low),
    )[edge]


def corner_at(corner, low, high):
    down, across = corner_cells[corner]
    return (high if down else low), (high if across else low)


def take_frame(grid, frame, links, low, high, kept):
    for i, (tile, edge) in enumerate(strips):
        frame[8 * i : 8 * i + 8] = grid[edge_slices(tile, edge, low, high)]
    for tile in range(3):
        for corner in range(4):
            row, column = corner_at(corner, low, high)
            cell = grid[tile, row, column : column + 1, :]
            if kept:
                cell = jnp.where(links[tile, 12 + corner] == 4, cell, 0.0)
            at = 96 + 4 * tile + corner
            frame[at : at + 1] = cell
    frame[108:128] = jnp.zeros((20, 256), f32)


def fill_ghosts(grid, got, links):
    for i, (tile, edge) in enumerate(strips):
        grid[edge_slices(tile, edge, 0, 9)] = got[8 * i : 8 * i + 8]
    for tile in range(3):
        for corner in range(4):
            row, column = corner_at(corner, 0, 9)
            at = 96 + 4 * tile + corner
            beside = [
                8 * (4 * tile + edge) + end
                for edge, end in zip(edge_starts[corner], corner_ends[corner])
            ]
            blend = 0.5 * (got[beside[0] : beside[0] + 1] + got[beside[1] : beside[1] + 1])
            grid[tile, row, column : column + 1, :] = jnp.where(
                links[tile, 12 + corner] == 4, got[at : at + 1], blend
            )


def split_corners(grid, links):
    for tile in range(3):
        for corner in range(4):
            row, column = corner_at(corner, 0, 9)
            near_row, near_column = corner_at(corner, 1, 8)
            cell = grid[tile, row, column : column + 1, :]
            half = jnp.where(links[tile, 12 + corner] == 3, 0.5 * cell, 0.0)
            grid[tile, row, near_column : near_column + 1, :] += half
            grid[tile, near_row, column : column + 1, :] += half


def add_returns(grid, got):
    for i, (tile, edge) in enumerate(strips):
        grid[edge_slices(tile, edge, 1, 8)] += got[8 * i : 8 * i + 8]
    for tile in range(3):
        for corner in range(4):
            row, column = corner_at(corner, 1, 8)
            at = 96 + 4 * tile + corner
            grid[tile, row, column : column + 1, :] += got[at : at + 1]


def pack_frame(pack_ref, frame, frame_ref, sent_ref):
    cells = frame[...].astype(bf16)
    frame_ref[...] = cells
    sent_ref[...] = jnp.dot(pack_ref[...], cells, preferred_element_type=f32).astype(bf16)


def unpack_frame(unpack_ref, recv_ref, frame_ref, got):
    got[...] = jnp.dot(
        unpack_ref[:, :send_rows], recv_ref[...], preferred_element_type=f32
    ) + jnp.dot(unpack_ref[:, send_rows:], frame_ref[...], preferred_element_type=f32)


def convolve(grid, weights):
    windows = []
    for down in range(3):
        for across in range(3):
            window = grid[:, down : down + 8, across : across + 8, :]
            windows.append(window.reshape(192, 256).astype(bf16))
    return jnp.dot(
        jnp.concatenate(windows, axis=1),
        weights[...].reshape(2304, 256),
        preferred_element_type=f32,
    )


def spread_back(gradient, weights, grid, column):
    grid[...] = jnp.zeros_like(grid)
    for across in range(3):
        column[...] = jnp.zeros_like(column)
        for down in range(3):
            part = lax.dot_general(
                gradient,
                weights[3 * down + across],
                (((1,), (1,)), ((), ())),
                preferred_element_type=f32,
            )
            column[:, down : down + 8] += part.reshape(3, 8, 8, 256)
        grid[:, :, across : across + 8, :] += column[...]


def halves(place, flat, pick):
    for k in range(4):
        quarter = lax.rem(place[1] + k, 4)
        side = quarter // 2 if pick == 0 else lax.rem(quarter, 2)
        yield k, jnp.where(side == 0, flat[:, :128], flat[:, 128:]).astype(bf16)


def flatten_grid(grid, flat):
    flat[300:304] = jnp.zeros((4, 256), f32)
    for tile in range(3):
        for row in range(10):
            at = 100 * tile + 10 * row
            flat[at : at + 10] = grid[tile, row]


def route_kernel(place, links, field_ref, pack_ref, unpack_ref, frame_ref, sent_ref, grid, frame):
    here = place[0]

    def rows_of(tiles, sides, valid, base, width, local_base):
        device = [tile // 3 for tile in tiles]
        source = [lax.rem(tile, 3) * 4 + side for tile, side in zip(tiles, sides)]
        out = []
        for i in range(12):
            send_rank = take_rank = jnp.int32(0)
            for j in range(12):
                near = (device[j] == device[i]) & valid[j]
                if j < i:
                    send_rank += jnp.where(near, width, 0)
                if j != i:
                    take_rank += jnp.where(near & (source[j] < source[i]), width, 0)
            first = device[i] * slot_rows + base
            own = device[i] == here
            send = jnp.where(own | ~valid[i], -1000, first + send_rank)
            take = jnp.where(own, local_base + source[i] * width, first + take_rank)
            out.append((send, jnp.where(valid[i], take, -1000)))
        return out

    codes = [links[tile, 4 + edge] for tile, edge in strips]
    edges = rows_of(
        [links[tile, edge] for tile, edge in strips],
        [lax.rem(code, 4) for code in codes],
        [links[tile, edge] >= 0 for tile, edge in strips],
        0,
        8,
        send_rows,
    )
    across = [links[tile, 8 + corner] for tile, corner in strips]
    corners = rows_of(
        [jnp.maximum(c, 0) // 4 for c in across],
        [lax.rem(jnp.maximum(c, 0), 4) for c in across],
        [c >= 0 for c in across],
        24,
        1,
        send_rows + 96,
    )
    lane = lax.broadcasted_iota(jnp.int32, (8, 128), 1)
    row = lax.broadcasted_iota(jnp.int32, (128, 128), 0)
    send = jnp.full((8, 128), -1000, jnp.int32)
    take = jnp.full((128, 128), -1000, jnp.int32)
    for i in range(12):
        send = jnp.where(lane // 8 == i, edges[i][0] + lane % 8, send)
        send = jnp.where(lane == 96 + i, corners[i][0], send)
        turned = codes[i] // 4 == 1
        step = jnp.where(turned, 7 - row % 8, row % 8)
        take = jnp.where(row // 8 == i, edges[i][1] + step, take)
        take = jnp.where(row == 96 + i, corners[i][1], take)
    slot = lax.broadcasted_iota(jnp.int32, (send_rows, 128), 0)
    pack_ref[...] = jnp.where(slot == send[:1], 1.0, 0.0).astype(bf16)
    column = lax.broadcasted_iota(jnp.int32, (128, 128), 1)
    for m in range(9):
        unpack_ref[:, 128 * m : 128 * m + 128] = jnp.where(
            take == column + 128 * m, 1.0, 0.0
        ).astype(bf16)
    grid[:, 1:9, 1:9, :] = field_ref[...].astype(f32).reshape(3, 8, 8, 256)
    take_frame(grid, frame, links, 1, 8, False)
    pack_frame(pack_ref, frame, frame_ref, sent_ref)


def first_kernel(
    place, links, field_ref, recv_ref, old_ref, pack_ref, unpack_ref, weights,
    hidden_ref, pre_ref, frame_ref, sent_ref, part0, part1, part2, part3,
    grid, frame, got, flat,
):
    unpack_frame(unpack_ref, recv_ref, old_ref, got)
    grid[:, 1:9, 1:9, :] = field_ref[...].astype(f32).reshape(3, 8, 8, 256)
    fill_ghosts(grid, got, links)
    pre_first = convolve(grid, weights)
    pre_ref[...] = pre_first
    hidden = gelu_value(pre_first).astype(bf16)
    hidden_ref[...] = hidden
    flatten_grid(grid, flat)
    grid[:, 1:9, 1:9, :] = hidden.astype(f32).reshape(3, 8, 8, 256)
    take_frame(grid, frame, links, 1, 8, False)
    pack_frame(pack_ref, frame, frame_ref, sent_ref)
    parts = (part0, part1, part2, part3)
    for k, half in halves(place, flat, 0):
        parts[k][...] = half


def second_kernel(
    place, links, field_ref, goal_ref, hidden_ref, recv_ref, old_ref, pack_ref, unpack_ref, weights,
    held0, held1, held2,
    state_ref, misfit_ref, inner_ref, frame_ref, sent_ref, part0, part1, part2, part3,
    grid, frame, got, flat, column,
):
    unpack_frame(unpack_ref, recv_ref, old_ref, got)
    grid[:, 1:9, 1:9, :] = hidden_ref[...].astype(f32).reshape(3, 8, 8, 256)
    fill_ghosts(grid, got, links)
    states = field_ref[...].astype(f32) + convolve(grid, weights)
    state_ref[...] = states.astype(bf16)
    misfit = states - goal_ref[...].astype(f32)
    misfit_ref[...] = misfit
    low = misfit.astype(bf16)
    flatten_grid(grid, flat)
    spread_back(low, weights, grid, column)
    split_corners(grid, links)
    take_frame(grid, frame, links, 0, 9, True)
    pack_frame(pack_ref, frame, frame_ref, sent_ref)
    inner_ref[...] = grid[:, 1:9, 1:9, :]
    parts = (part0, part1, part2, part3)
    for k, half in halves(place, flat, 0):
        parts[k][:304] = half
    for k, half in halves(place, low.astype(f32), 1):
        parts[k][304:] = half


def third_kernel(
    place, links, inner_ref, pre_ref, recv_ref, old_ref, unpack_ref, weights, *refs,
):
    last_ref, frame_ref, part0, part1, part2, part3, grid, frame, got, column = refs[3:]
    unpack_frame(unpack_ref, recv_ref, old_ref, got)
    grid[:, 1:9, 1:9, :] = inner_ref[...]
    add_returns(grid, got)
    hidden_grad = grid[:, 1:9, 1:9, :].reshape(192, 256)
    low = (hidden_grad * gelu_slope(pre_ref[...])).astype(bf16)
    parts = (part0, part1, part2, part3)
    for k, half in halves(place, low.astype(f32), 1):
        parts[k][...] = half
    spread_back(low, weights, grid, column)
    split_corners(grid, links)
    take_frame(grid, frame, links, 0, 9, True)
    frame_ref[...] = frame[...].astype(bf16)
    last_ref[...] = grid[:, 1:9, 1:9, :]


def last_kernel(place, last_ref, misfit_ref, recv_ref, old_ref, unpack_ref, out_ref, grid, got):
    unpack_frame(unpack_ref, recv_ref, old_ref, got)
    grid[:, 1:9, 1:9, :] = last_ref[...] + misfit_ref[...].reshape(3, 8, 8, 256)
    add_returns(grid, got)
    out_ref[...] = grid[:, 1:9, 1:9, :]


moved_in = pl.BlockSpec(memory_space=pltpu.HBM)
landed = pl.BlockSpec(memory_space=pl.ANY)
left = pl.BlockSpec()
near = pl.BlockSpec(memory_space=pltpu.VMEM)
resting = pl.BlockSpec(memory_space=pltpu.HBM)
grid_shape = pltpu.VMEM((3, 10, 10, 256), f32)
frame_shape = pltpu.VMEM((128, 256), f32)
flat_shape = pltpu.VMEM((304, 256), f32)
column_shape = pltpu.VMEM((3, 10, 8, 256), f32)


def like(*shape, dtype=bf16):
    return jax.ShapeDtypeStruct(shape, dtype)


class Arriving:
    def __init__(self, ref, copy):
        self.ref, self.copy = ref, copy

    def settle(self):
        if self.copy is not None:
            self.copy.wait()
            self.copy = None

    def __getitem__(self, at):
        self.settle()
        return self.ref[at]


class Leaving:
    def __init__(self, ref, copy):
        self.ref, self.copy, self.started = ref, copy, False

    def send(self):
        if not self.started:
            self.copy.start()
            self.started = True

    def __getitem__(self, at):
        return self.ref[at]

    def __setitem__(self, at, value):
        self.ref[at] = value
        if at is Ellipsis:
            self.send()


def run(kernel, name, args, specs, outs, scratch, flops, kept=()):
    single = not isinstance(outs, tuple)
    outs = (outs,) if single else outs
    moved = [i for i, spec in enumerate(specs) if spec is moved_in or spec is landed]
    buffers = [
        (pltpu.SMEM if args[i].dtype == jnp.int32 else pltpu.VMEM)(args[i].shape, args[i].dtype)
        for i in moved
    ]
    away = [n for n in range(len(outs)) if n not in kept]
    stores = [pltpu.VMEM(outs[n].shape, outs[n].dtype) for n in away]

    def body(*refs):
        ins, refs = refs[: len(args)], refs[len(args) :]
        targets, refs = refs[: len(outs)], refs[len(outs) :]
        held, refs = refs[: len(moved)], refs[len(moved) :]
        made, refs = refs[: len(away)], refs[len(away) :]
        arrived, left_for, refs = refs[0], refs[1], refs[2:]
        copies = [
            pltpu.make_async_copy(ins[i], held[n], arrived.at[n]) for n, i in enumerate(moved)
        ]
        for copy in copies:
            copy.start()
        given = list(ins)
        for n, i in enumerate(moved):
            given[i] = Arriving(held[n], copies[n])
        results = list(targets)
        for m, n in enumerate(away):
            copy = pltpu.make_async_copy(made[m], targets[n], left_for.at[m])
            results[n] = Leaving(made[m], copy)
        kernel(placing(), *given, *results, *refs)
        for n in range(len(moved)):
            given[moved[n]].settle()
        for n in away:
            results[n].send()
        for n in away:
            results[n].copy.wait()

    made = pl.pallas_call(
        body,
        out_shape=tuple(
            pltpu.HBM(out.shape, out.dtype) if n in away else out for n, out in enumerate(outs)
        ),
        in_specs=[landed if spec is left else spec for spec in specs],
        out_specs=tuple(moved_in if n in away else near for n in range(len(outs))),
        scratch_shapes=[
            *buffers,
            *stores,
            pltpu.SemaphoreType.DMA((max(1, len(moved)),)),
            pltpu.SemaphoreType.DMA((max(1, len(away)),)),
            *scratch,
        ],
        compiler_params=pltpu.CompilerParams(vmem_limit_bytes=40 * 2**20),
        cost_estimate=pl.CostEstimate(flops=flops, bytes_accessed=3000000, transcendentals=0),
        name=name,
    )(
        *[
            pltpu.with_memory_space_constraint(arg, pltpu.HBM)
            if spec is moved_in or spec is resting
            else arg
            for arg, spec in zip(args, specs)
        ]
    )
    return made[0] if single else made


def slope_kernel(split, place, *refs):
    count = 4 if split else 8
    parts = refs[:count]
    kept_ref, sent_ref, flat, wide, total = refs[count:]
    grads = []
    for n in range(4):
        flat[304 * n : 304 * n + 304] = parts[n][:304].astype(f32)
        grads.append(parts[n][304:] if split else parts[4 + n][...])
    grads = jnp.concatenate(grads, axis=0)
    low = place[2] == 0
    for across in range(3):
        for n in range(4):
            for tile in range(3):
                for row in range(10):
                    at = 304 * n + 100 * tile + 10 * row + across
                    wide[3 * n + tile, row] = flat[at : at + 8]
        for down in range(3):
            window = wide[:, down : down + 8].reshape(768, 128).astype(bf16)
            out = lax.dot_general(
                window, grads, (((0,), (0,)), ((), ())), preferred_element_type=f32
            )
            tap = (3 * down + across) * 64
            total[0, tap : tap + 64] = jnp.where(low, out[:64], out[64:])
            total[1, tap : tap + 64] = jnp.where(low, out[64:], out[:64])
    for j in range(4):
        kept_ref[j] = total[0, 144 * j : 144 * j + 144]
        sent_ref[j] = total[1, 144 * j : 144 * j + 144]


def slope_terms(parts, split, packing=(), held=()):
    shape = like(4, 144, 128, dtype=f32)
    count = len(parts)
    outs = (shape, shape) + ((like(send_rows, 256),) if packing else ())

    def kernel(place, *refs):
        ins, refs = refs[: count + len(packing)], refs[count + len(packing) + len(held) :]
        if packing:
            pack_ref, frame_ref = ins[count:]
            refs[2][...] = jnp.dot(
                pack_ref[...], frame_ref[...], preferred_element_type=f32
            ).astype(bf16)
        slope_kernel(split, place, *ins[:count], *refs[:2], *refs[len(outs) :])

    return run(
        kernel,
        "slope_terms",
        (*parts, *packing, *held),
        ([moved_in] + [landed] * 3) * (count // 4 - 1)
        + [near] * 4
        + [near] * len(packing)
        + [near] * len(held),
        outs,
        [
            pltpu.VMEM((1216, 128), f32),
            pltpu.VMEM((12, 10, 8, 128), f32),
            pltpu.VMEM((2, 576, 128), f32),
        ],
        2 * 9 * 768 * 128 * 128,
        tuple(range(len(outs))),
    )


def ring(parts, axis):
    return [shifted(part, axis, k) if k else part for k, part in enumerate(parts)]


def pair_kernel(place, kept0, got0, kept1, got1, *chunks):
    for k in range(4):
        at = lax.rem(place[3] + k, 4)
        chunks[k][:144] = kept0[at] + got0[at]
        chunks[k][144:] = kept1[at] + got1[at]


def plane_kernel(place, own, part1, part2, part3, held, out, total):
    total[...] = (own[...] + part1[...]) + (part2[...] + part3[...])
    for j in range(8):
        out[j] = total[36 * j : 36 * j + 36]


def spread_kernel(place, own, other, first_ref, second_ref):
    low = place[2] == 0
    for n, out in enumerate((first_ref, second_ref)):
        at = slice(144 * n, 144 * n + 144)
        for x in range(4):
            row, column = 128 * (x // 2), 128 * (x % 2)
            pair = [
                jnp.concatenate(
                    [part[4 * x + y, at].astype(f32) for y in range(4)], axis=0
                ).reshape(9, 64, 128)
                for part in (own, other)
            ]
            out[:, row : row + 64, column : column + 128] = jnp.where(low, pair[0], pair[1])
            out[:, row + 64 : row + 128, column : column + 128] = jnp.where(low, pair[1], pair[0])
        out.send()


def groups(along):
    axes = ("x", "y", "z", "core")
    out = []
    for fixed in itertools.product(*[range(1 if a in along else sizes[a]) for a in axes]):
        group = []
        for moving in itertools.product(*[range(sizes[a]) for a in along]):
            at = dict(zip(axes, fixed)) | dict(zip(along, moving))
            group.append(place_of(**at))
        out.append(group)
    return out


def trade(values, *along):
    return lax.all_to_all(
        values, ("tile", "ens"), 0, 0, axis_index_groups=groups(along), tiled=True
    )


def copies_of(values, count):
    return jnp.broadcast_to(values[None], (count,) + values.shape)


def finish_slopes(chunks, held, scale):
    terms = run(
        plane_kernel,
        "row_sum",
        (*ring(chunks, "y"), held),
        [near] * 4 + [left],
        like(8, 36, 128, dtype=f32),
        [pltpu.VMEM((288, 128), f32)],
        1000,
        (0,),
    )
    mine = (jnp.sum(trade(terms, "z"), axis=0) * scale).astype(bf16)
    line = trade(copies_of(mine, 8), "z").reshape(288, 128)
    plane = trade(copies_of(line, 16), "x", "y")
    shape = like(9, 256, 256, dtype=f32)
    return run(
        spread_kernel,
        "spread_slopes",
        (plane, shifted(plane, "core", 1)),
        [landed, landed],
        (shape, shape),
        [],
        1000,
    )


def exchange(values):
    return lax.all_to_all(values, "tile", 0, 0, tiled=True)


def per_device(network_conditions, subsequent_targets, w_first, w_second, tile_links):
    field = network_conditions.reshape(192, 256)
    goal = subsequent_targets.reshape(192, 256)
    first_weights, second_weights = w_first.reshape(9, 256, 256), w_second.reshape(9, 256, 256)
    scale = 1.0 / math.sqrt(lax.axis_size("ens") * lax.axis_size("tile") * 192)
    frame_like, sent_like, rows_like = like(128, 256), like(send_rows, 256), like(192, 256)
    inner_like = like(3, 8, 8, 256, dtype=f32)
    conv_flops = 2 * 9 * 192 * 256 * 256

    pack, unpack, frame, sent = run(
        route_kernel,
        "routes",
        (tile_links, field),
        [moved_in, moved_in],
        (like(send_rows, 128), like(128, send_rows + 128), frame_like, sent_like),
        [grid_shape, frame_shape],
        2 * send_rows * 128 * 256,
        (0,1,2,3),
    )
    recv = exchange(sent)
    hidden, pre_first, frame, sent, *parts = run(
        first_kernel,
        "first_layer",
        (tile_links, field, recv, frame, pack, unpack, first_weights),
        [moved_in] + [near] * 6,
        (rows_like, like(192, 256, dtype=f32), frame_like, sent_like) + (like(304, 128),) * 4,
        [grid_shape, frame_shape, frame_shape, flat_shape],
        conv_flops,
        (0,2,3,5,6,7),
    )
    recv = exchange(sent)
    field_parts = ring(parts, "x")
    states, misfit, inner, frame, sent, *parts = run(
        second_kernel,
        "second_layer",
        (
            tile_links, field, goal, hidden, recv, frame, pack, unpack, second_weights,
            *field_parts[1:],
        ),
        [moved_in] * 3 + [near] * 6 + [left] * 3,
        (rows_like, like(192, 256, dtype=f32), inner_like, frame_like, sent_like)
        + (like(496, 128),) * 4,
        [grid_shape, frame_shape, frame_shape, flat_shape, column_shape],
        2 * conv_flops,
        (2,3,4,5,6,7,8),
    )
    recv = exchange(sent)
    closing_parts = ring(parts, "x")
    closing = slope_terms(closing_parts, True)
    last, frame, *parts = run(
        third_kernel,
        "first_gradient",
        (tile_links, inner, pre_first, recv, frame, unpack, first_weights, *closing_parts[1:]),
        [moved_in, near, moved_in] + [near] * 3 + [moved_in] + [left] * 3,
        (inner_like, frame_like) + (like(192, 128),) * 4,
        [grid_shape, frame_shape, frame_shape, column_shape],
        conv_flops,
        (1,2,3,4,5),
    )
    got_closing = shifted(closing[1], "core", 1)
    *opening, sent = slope_terms(
        field_parts + ring(parts, "x"), False, (pack, frame), (closing[0],)
    )
    recv = exchange(sent)
    chunks = run(
        pair_kernel,
        "pair_sum",
        (opening[0], shifted(opening[1], "core", 1), closing[0], got_closing),
        [near] * 4,
        (like(288, 128, dtype=f32),) * 4,
        [],
        1000,
        (0, 1, 2, 3),
    )
    condition_derivative = run(
        last_kernel,
        "last_gradient",
        (last, misfit, recv, frame, unpack),
        [moved_in] * 2 + [near] * 3,
        inner_like,
        [grid_shape, frame_shape],
        1000,
    )
    slopes = finish_slopes(chunks, recv, scale)
    return (
        states.reshape(network_conditions.shape),
        condition_derivative[None],
        slopes[0].reshape(w_first.shape),
        slopes[1].reshape(w_second.shape),
    )


def solution(mesh):
    return jax.shard_map(
        per_device,
        mesh=mesh,
        in_specs=(
            P("ens", "tile", None, None, None),
            P("ens", "tile", None, None, None),
            P(),
            P(),
            P("tile", None),
        ),
        out_specs=(
            P("ens", "tile", None, None, None),
            P("ens", "tile", None, None, None),
            P(),
            P(),
        ),
        check_vma=False,
    )
```

```python
import itertools
import math

import jax
import jax.numpy as jnp
from jax import lax
from jax.experimental import pallas as pl
from jax.experimental.pallas import tpu as pltpu
from jax.sharding import PartitionSpec as P

tanh_scale = 0.7978845608028654
cubic_term = 0.044715
slot_rows = 32
send_rows = 1024
bf16, f32 = jnp.bfloat16, jnp.float32


def gelu_value(inputs):
    return (
        0.5
        * inputs
        * (1.0 + jnp.tanh(tanh_scale * (inputs + cubic_term * inputs * inputs * inputs)))
    )


def gelu_slope(inputs):
    tangent = jnp.tanh(tanh_scale * (inputs + cubic_term * inputs * inputs * inputs))
    return 0.5 * (1.0 + tangent) + 0.5 * inputs * (1.0 - tangent * tangent) * tanh_scale * (
        1.0 + 3.0 * cubic_term * inputs * inputs
    )


sizes = {"x": 4, "y": 4, "z": 8, "core": 2}


def place_of(x, y, z, core):
    return ((y * 2 + z % 2) * 4 + x) * 8 + (z // 2) * 2 + core


def shifted(values, axis, by):
    pairs = []
    for x in range(4):
        for y in range(4):
            for z in range(8):
                for core in range(2):
                    at = {"x": x, "y": y, "z": z, "core": core}
                    to = dict(at)
                    to[axis] = (at[axis] + by) % sizes[axis]
                    pairs.append((place_of(**at), place_of(**to)))
    return lax.ppermute(values, ("tile", "ens"), pairs)


def placing():
    tile, ens = lax.axis_index("tile"), lax.axis_index("ens")
    return tile, lax.rem(tile, 4), lax.rem(ens, 2), tile // 8


edge_starts = ((0, 3), (0, 1), (1, 2), (2, 3))
corner_ends = ((0, 0), (7, 0), (7, 7), (0, 7))
corner_cells = ((0, 0), (0, 1), (1, 1), (1, 0))
strips = [(tile, edge) for tile in range(3) for edge in range(4)]


def edge_slices(tile, edge, low, high):
    inner = slice(1, 9)
    return (
        (tile, low, inner),
        (tile, inner, high),
        (tile, high, inner),
        (tile, inner, low),
    )[edge]


def corner_at(corner, low, high):
    down, across = corner_cells[corner]
    return (high if down else low), (high if across else low)


def take_frame(grid, frame, links, low, high, kept):
    for i, (tile, edge) in enumerate(strips):
        frame[8 * i : 8 * i + 8] = grid[edge_slices(tile, edge, low, high)]
    for tile in range(3):
        for corner in range(4):
            row, column = corner_at(corner, low, high)
            cell = grid[tile, row, column : column + 1, :]
            if kept:
                cell = jnp.where(links[tile, 12 + corner] == 4, cell, 0.0)
            at = 96 + 4 * tile + corner
            frame[at : at + 1] = cell
    frame[108:128] = jnp.zeros((20, 256), f32)


def fill_ghosts(grid, got, links):
    for i, (tile, edge) in enumerate(strips):
        grid[edge_slices(tile, edge, 0, 9)] = got[8 * i : 8 * i + 8]
    for tile in range(3):
        for corner in range(4):
            row, column = corner_at(corner, 0, 9)
            at = 96 + 4 * tile + corner
            beside = [
                8 * (4 * tile + edge) + end
                for edge, end in zip(edge_starts[corner], corner_ends[corner])
            ]
            blend = 0.5 * (got[beside[0] : beside[0] + 1] + got[beside[1] : beside[1] + 1])
            grid[tile, row, column : column + 1, :] = jnp.where(
                links[tile, 12 + corner] == 4, got[at : at + 1], blend
            )


def split_corners(grid, links):
    for tile in range(3):
        for corner in range(4):
            row, column = corner_at(corner, 0, 9)
            near_row, near_column = corner_at(corner, 1, 8)
            cell = grid[tile, row, column : column + 1, :]
            half = jnp.where(links[tile, 12 + corner] == 3, 0.5 * cell, 0.0)
            grid[tile, row, near_column : near_column + 1, :] += half
            grid[tile, near_row, column : column + 1, :] += half


def add_returns(grid, got):
    for i, (tile, edge) in enumerate(strips):
        grid[edge_slices(tile, edge, 1, 8)] += got[8 * i : 8 * i + 8]
    for tile in range(3):
        for corner in range(4):
            row, column = corner_at(corner, 1, 8)
            at = 96 + 4 * tile + corner
            grid[tile, row, column : column + 1, :] += got[at : at + 1]


def pack_frame(pack_ref, frame, frame_ref, sent_ref):
    cells = frame[...].astype(bf16)
    frame_ref[...] = cells
    sent_ref[...] = jnp.dot(pack_ref[...], cells, preferred_element_type=f32).astype(bf16)


def unpack_frame(unpack_ref, recv_ref, frame_ref, got):
    got[...] = jnp.dot(
        unpack_ref[:, :send_rows], recv_ref[...], preferred_element_type=f32
    ) + jnp.dot(unpack_ref[:, send_rows:], frame_ref[...], preferred_element_type=f32)


def convolve(grid, weights):
    windows = []
    for down in range(3):
        for across in range(3):
            window = grid[:, down : down + 8, across : across + 8, :]
            windows.append(window.reshape(192, 256).astype(bf16))
    return jnp.dot(
        jnp.concatenate(windows, axis=1),
        weights[...].reshape(2304, 256),
        preferred_element_type=f32,
    )


def spread_back(gradient, weights, grid, column):
    grid[...] = jnp.zeros_like(grid)
    for across in range(3):
        column[...] = jnp.zeros_like(column)
        for down in range(3):
            part = lax.dot_general(
                gradient,
                weights[3 * down + across],
                (((1,), (1,)), ((), ())),
                preferred_element_type=f32,
            )
            column[:, down : down + 8] += part.reshape(3, 8, 8, 256)
        grid[:, :, across : across + 8, :] += column[...]


def halves(place, flat, pick):
    for k in range(4):
        quarter = lax.rem(place[1] + k, 4)
        side = quarter // 2 if pick == 0 else lax.rem(quarter, 2)
        yield k, jnp.where(side == 0, flat[:, :128], flat[:, 128:]).astype(bf16)


def flatten_grid(grid, flat):
    flat[300:304] = jnp.zeros((4, 256), f32)
    for tile in range(3):
        for row in range(10):
            at = 100 * tile + 10 * row
            flat[at : at + 10] = grid[tile, row]


def route_kernel(place, links, field_ref, pack_ref, unpack_ref, frame_ref, sent_ref, grid, frame):
    here = place[0]

    def rows_of(tiles, sides, valid, base, width, local_base):
        device = [tile // 3 for tile in tiles]
        source = [lax.rem(tile, 3) * 4 + side for tile, side in zip(tiles, sides)]
        out = []
        for i in range(12):
            send_rank = take_rank = jnp.int32(0)
            for j in range(12):
                near = (device[j] == device[i]) & valid[j]
                if j < i:
                    send_rank += jnp.where(near, width, 0)
                if j != i:
                    take_rank += jnp.where(near & (source[j] < source[i]), width, 0)
            first = device[i] * slot_rows + base
            own = device[i] == here
            send = jnp.where(own | ~valid[i], -1000, first + send_rank)
            take = jnp.where(own, local_base + source[i] * width, first + take_rank)
            out.append((send, jnp.where(valid[i], take, -1000)))
        return out

    codes = [links[tile, 4 + edge] for tile, edge in strips]
    edges = rows_of(
        [links[tile, edge] for tile, edge in strips],
        [lax.rem(code, 4) for code in codes],
        [links[tile, edge] >= 0 for tile, edge in strips],
        0,
        8,
        send_rows,
    )
    across = [links[tile, 8 + corner] for tile, corner in strips]
    corners = rows_of(
        [jnp.maximum(c, 0) // 4 for c in across],
        [lax.rem(jnp.maximum(c, 0), 4) for c in across],
        [c >= 0 for c in across],
        24,
        1,
        send_rows + 96,
    )
    lane = lax.broadcasted_iota(jnp.int32, (8, 128), 1)
    row = lax.broadcasted_iota(jnp.int32, (128, 128), 0)
    send = jnp.full((8, 128), -1000, jnp.int32)
    take = jnp.full((128, 128), -1000, jnp.int32)
    for i in range(12):
        send = jnp.where(lane // 8 == i, edges[i][0] + lane % 8, send)
        send = jnp.where(lane == 96 + i, corners[i][0], send)
        turned = codes[i] // 4 == 1
        step = jnp.where(turned, 7 - row % 8, row % 8)
        take = jnp.where(row // 8 == i, edges[i][1] + step, take)
        take = jnp.where(row == 96 + i, corners[i][1], take)
    slot = lax.broadcasted_iota(jnp.int32, (send_rows, 128), 0)
    pack_ref[...] = jnp.where(slot == send[:1], 1.0, 0.0).astype(bf16)
    column = lax.broadcasted_iota(jnp.int32, (128, 128), 1)
    for m in range(9):
        unpack_ref[:, 128 * m : 128 * m + 128] = jnp.where(
            take == column + 128 * m, 1.0, 0.0
        ).astype(bf16)
    grid[:, 1:9, 1:9, :] = field_ref[...].astype(f32).reshape(3, 8, 8, 256)
    take_frame(grid, frame, links, 1, 8, False)
    pack_frame(pack_ref, frame, frame_ref, sent_ref)


def first_kernel(
    place, links, field_ref, recv_ref, old_ref, pack_ref, unpack_ref, weights,
    hidden_ref, pre_ref, frame_ref, sent_ref, part0, part1, part2, part3,
    grid, frame, got, flat,
):
    unpack_frame(unpack_ref, recv_ref, old_ref, got)
    grid[:, 1:9, 1:9, :] = field_ref[...].astype(f32).reshape(3, 8, 8, 256)
    fill_ghosts(grid, got, links)
    pre_first = convolve(grid, weights)
    pre_ref[...] = pre_first
    hidden = gelu_value(pre_first).astype(bf16)
    hidden_ref[...] = hidden
    flatten_grid(grid, flat)
    grid[:, 1:9, 1:9, :] = hidden.astype(f32).reshape(3, 8, 8, 256)
    take_frame(grid, frame, links, 1, 8, False)
    pack_frame(pack_ref, frame, frame_ref, sent_ref)
    parts = (part0, part1, part2, part3)
    for k, half in halves(place, flat, 0):
        parts[k][...] = half


def second_kernel(
    place, links, field_ref, goal_ref, hidden_ref, recv_ref, old_ref, pack_ref, unpack_ref, weights,
    held0, held1, held2,
    state_ref, misfit_ref, inner_ref, frame_ref, sent_ref, part0, part1, part2, part3,
    grid, frame, got, flat, column,
):
    unpack_frame(unpack_ref, recv_ref, old_ref, got)
    grid[:, 1:9, 1:9, :] = hidden_ref[...].astype(f32).reshape(3, 8, 8, 256)
    fill_ghosts(grid, got, links)
    states = field_ref[...].astype(f32) + convolve(grid, weights)
    state_ref[...] = states.astype(bf16)
    misfit = states - goal_ref[...].astype(f32)
    misfit_ref[...] = misfit
    low = misfit.astype(bf16)
    flatten_grid(grid, flat)
    spread_back(low, weights, grid, column)
    split_corners(grid, links)
    take_frame(grid, frame, links, 0, 9, True)
    pack_frame(pack_ref, frame, frame_ref, sent_ref)
    inner_ref[...] = grid[:, 1:9, 1:9, :]
    parts = (part0, part1, part2, part3)
    for k, half in halves(place, flat, 0):
        parts[k][:304] = half
    for k, half in halves(place, low.astype(f32), 1):
        parts[k][304:] = half


def third_kernel(
    place, links, inner_ref, pre_ref, recv_ref, old_ref, unpack_ref, weights, *refs,
):
    last_ref, frame_ref, part0, part1, part2, part3, grid, frame, got, column = refs
    unpack_frame(unpack_ref, recv_ref, old_ref, got)
    grid[:, 1:9, 1:9, :] = inner_ref[...]
    add_returns(grid, got)
    hidden_grad = grid[:, 1:9, 1:9, :].reshape(192, 256)
    low = (hidden_grad * gelu_slope(pre_ref[...])).astype(bf16)
    parts = (part0, part1, part2, part3)
    for k, half in halves(place, low.astype(f32), 1):
        parts[k][...] = half
    spread_back(low, weights, grid, column)
    split_corners(grid, links)
    take_frame(grid, frame, links, 0, 9, True)
    frame_ref[...] = frame[...].astype(bf16)
    last_ref[...] = grid[:, 1:9, 1:9, :]


def last_kernel(place, last_ref, misfit_ref, recv_ref, old_ref, unpack_ref, out_ref, grid, got):
    unpack_frame(unpack_ref, recv_ref, old_ref, got)
    grid[:, 1:9, 1:9, :] = last_ref[...] + misfit_ref[...].reshape(3, 8, 8, 256)
    add_returns(grid, got)
    out_ref[...] = grid[:, 1:9, 1:9, :]


moved_in = pl.BlockSpec(memory_space=pltpu.HBM)
landed = pl.BlockSpec(memory_space=pl.ANY)
left = pl.BlockSpec()
near = pl.BlockSpec(memory_space=pltpu.VMEM)
resting = pl.BlockSpec(memory_space=pltpu.HBM)
grid_shape = pltpu.VMEM((3, 10, 10, 256), f32)
frame_shape = pltpu.VMEM((128, 256), f32)
flat_shape = pltpu.VMEM((304, 256), f32)
column_shape = pltpu.VMEM((3, 10, 8, 256), f32)


def like(*shape, dtype=bf16):
    return jax.ShapeDtypeStruct(shape, dtype)


class Arriving:
    def __init__(self, ref, copy):
        self.ref, self.copy = ref, copy

    def settle(self):
        if self.copy is not None:
            self.copy.wait()
            self.copy = None

    def __getitem__(self, at):
        self.settle()
        return self.ref[at]


class Leaving:
    def __init__(self, ref, copy):
        self.ref, self.copy, self.started = ref, copy, False

    def send(self):
        if not self.started:
            self.copy.start()
            self.started = True

    def __getitem__(self, at):
        return self.ref[at]

    def __setitem__(self, at, value):
        self.ref[at] = value
        if at is Ellipsis:
            self.send()


def run(kernel, name, args, specs, outs, scratch, flops, kept=()):
    single = not isinstance(outs, tuple)
    outs = (outs,) if single else outs
    moved = [i for i, spec in enumerate(specs) if spec is moved_in or spec is landed]
    buffers = [
        (pltpu.SMEM if args[i].dtype == jnp.int32 else pltpu.VMEM)(args[i].shape, args[i].dtype)
        for i in moved
    ]
    away = [n for n in range(len(outs)) if n not in kept]
    stores = [pltpu.VMEM(outs[n].shape, outs[n].dtype) for n in away]

    def body(*refs):
        ins, refs = refs[: len(args)], refs[len(args) :]
        targets, refs = refs[: len(outs)], refs[len(outs) :]
        held, refs = refs[: len(moved)], refs[len(moved) :]
        made, refs = refs[: len(away)], refs[len(away) :]
        arrived, left_for, refs = refs[0], refs[1], refs[2:]
        copies = [
            pltpu.make_async_copy(ins[i], held[n], arrived.at[n]) for n, i in enumerate(moved)
        ]
        for copy in copies:
            copy.start()
        given = list(ins)
        for n, i in enumerate(moved):
            given[i] = Arriving(held[n], copies[n])
        results = list(targets)
        for m, n in enumerate(away):
            copy = pltpu.make_async_copy(made[m], targets[n], left_for.at[m])
            results[n] = Leaving(made[m], copy)
        kernel(placing(), *given, *results, *refs)
        for n in range(len(moved)):
            given[moved[n]].settle()
        for n in away:
            results[n].send()
        for n in away:
            results[n].copy.wait()

    made = pl.pallas_call(
        body,
        out_shape=tuple(
            pltpu.HBM(out.shape, out.dtype) if n in away else out for n, out in enumerate(outs)
        ),
        in_specs=[landed if spec is left else spec for spec in specs],
        out_specs=tuple(moved_in if n in away else near for n in range(len(outs))),
        scratch_shapes=[
            *buffers,
            *stores,
            pltpu.SemaphoreType.DMA((max(1, len(moved)),)),
            pltpu.SemaphoreType.DMA((max(1, len(away)),)),
            *scratch,
        ],
        compiler_params=pltpu.CompilerParams(vmem_limit_bytes=40 * 2**20),
        cost_estimate=pl.CostEstimate(flops=flops, bytes_accessed=3000000, transcendentals=0),
        name=name,
    )(
        *[
            pltpu.with_memory_space_constraint(arg, pltpu.HBM)
            if spec is moved_in or spec is resting
            else arg
            for arg, spec in zip(args, specs)
        ]
    )
    return made[0] if single else made


def slope_kernel(split, place, *refs):
    count = 4 if split else 8
    parts = refs[:count]
    kept_ref, sent_ref, flat, wide, total = refs[count:]
    grads = []
    for n in range(4):
        flat[304 * n : 304 * n + 304] = parts[n][:304].astype(f32)
        grads.append(parts[n][304:] if split else parts[4 + n][...])
    grads = jnp.concatenate(grads, axis=0)
    low = place[2] == 0
    for across in range(3):
        for n in range(4):
            for tile in range(3):
                for row in range(10):
                    at = 304 * n + 100 * tile + 10 * row + across
                    wide[3 * n + tile, row] = flat[at : at + 8]
        for down in range(3):
            window = wide[:, down : down + 8].reshape(768, 128).astype(bf16)
            out = lax.dot_general(
                window, grads, (((0,), (0,)), ((), ())), preferred_element_type=f32
            )
            tap = (3 * down + across) * 64
            total[0, tap : tap + 64] = jnp.where(low, out[:64], out[64:])
            total[1, tap : tap + 64] = jnp.where(low, out[64:], out[:64])
    for j in range(4):
        kept_ref[j] = total[0, 144 * j : 144 * j + 144]
        sent_ref[j] = total[1, 144 * j : 144 * j + 144]


def slope_terms(parts, split, packing=(), held=()):
    shape = like(4, 144, 128, dtype=f32)
    count = len(parts)
    outs = (shape, shape) + ((like(send_rows, 256),) if packing else ())

    def kernel(place, *refs):
        ins, refs = refs[: count + len(packing)], refs[count + len(packing) + len(held) :]
        if packing:
            pack_ref, frame_ref = ins[count:]
            refs[2][...] = jnp.dot(
                pack_ref[...], frame_ref[...], preferred_element_type=f32
            ).astype(bf16)
        slope_kernel(split, place, *ins[:count], *refs[:2], *refs[len(outs) :])

    return run(
        kernel,
        "slope_terms",
        (*parts, *packing, *held),
        ([moved_in] + [landed] * 3) * (count // 4 - 1)
        + [near] * 4
        + [near] * len(packing)
        + [near] * len(held),
        outs,
        [
            pltpu.VMEM((1216, 128), f32),
            pltpu.VMEM((12, 10, 8, 128), f32),
            pltpu.VMEM((2, 576, 128), f32),
        ],
        2 * 9 * 768 * 128 * 128,
        tuple(range(len(outs))),
    )


def ring(parts, axis):
    return [shifted(part, axis, k) if k else part for k, part in enumerate(parts)]


def pair_kernel(place, kept0, got0, kept1, got1, *chunks):
    for k in range(4):
        at = lax.rem(place[3] + k, 4)
        chunks[k][:144] = kept0[at] + got0[at]
        chunks[k][144:] = kept1[at] + got1[at]


def plane_kernel(place, own, part1, part2, part3, held, out, total):
    total[...] = (own[...] + part1[...]) + (part2[...] + part3[...])
    for j in range(8):
        out[j] = total[36 * j : 36 * j + 36]


def spread_kernel(place, own, other, first_ref, second_ref):
    low = place[2] == 0
    for n, out in enumerate((first_ref, second_ref)):
        at = slice(144 * n, 144 * n + 144)
        for x in range(4):
            row, column = 128 * (x // 2), 128 * (x % 2)
            pair = [
                jnp.concatenate(
                    [part[4 * x + y, at].astype(f32) for y in range(4)], axis=0
                ).reshape(9, 64, 128)
                for part in (own, other)
            ]
            out[:, row : row + 64, column : column + 128] = jnp.where(low, pair[0], pair[1])
            out[:, row + 64 : row + 128, column : column + 128] = jnp.where(low, pair[1], pair[0])
        out.send()


def groups(along):
    axes = ("x", "y", "z", "core")
    out = []
    for fixed in itertools.product(*[range(1 if a in along else sizes[a]) for a in axes]):
        group = []
        for moving in itertools.product(*[range(sizes[a]) for a in along]):
            at = dict(zip(axes, fixed)) | dict(zip(along, moving))
            group.append(place_of(**at))
        out.append(group)
    return out


def trade(values, *along):
    return lax.all_to_all(
        values, ("tile", "ens"), 0, 0, axis_index_groups=groups(along), tiled=True
    )


def copies_of(values, count):
    return jnp.broadcast_to(values[None], (count,) + values.shape)


def finish_slopes(chunks, held, scale):
    terms = run(
        plane_kernel,
        "row_sum",
        (*ring(chunks, "y"), held),
        [near] * 4 + [left],
        like(8, 36, 128, dtype=f32),
        [pltpu.VMEM((288, 128), f32)],
        1000,
        (0,),
    )
    mine = (jnp.sum(trade(terms, "z"), axis=0) * scale).astype(bf16)
    line = trade(copies_of(mine, 8), "z").reshape(288, 128)
    plane = trade(copies_of(line, 16), "x", "y")
    shape = like(9, 256, 256, dtype=f32)
    return run(
        spread_kernel,
        "spread_slopes",
        (plane, shifted(plane, "core", 1)),
        [landed, landed],
        (shape, shape),
        [],
        1000,
    )


def exchange(values):
    return lax.all_to_all(values, "tile", 0, 0, tiled=True)


def per_device(network_conditions, subsequent_targets, w_first, w_second, tile_links):
    field = network_conditions.reshape(192, 256)
    goal = subsequent_targets.reshape(192, 256)
    first_weights, second_weights = w_first.reshape(9, 256, 256), w_second.reshape(9, 256, 256)
    scale = 1.0 / math.sqrt(lax.axis_size("ens") * lax.axis_size("tile") * 192)
    frame_like, sent_like, rows_like = like(128, 256), like(send_rows, 256), like(192, 256)
    inner_like = like(3, 8, 8, 256, dtype=f32)
    conv_flops = 2 * 9 * 192 * 256 * 256

    pack, unpack, frame, sent = run(
        route_kernel,
        "routes",
        (tile_links, field),
        [moved_in, moved_in],
        (like(send_rows, 128), like(128, send_rows + 128), frame_like, sent_like),
        [grid_shape, frame_shape],
        2 * send_rows * 128 * 256,
        (0,1,2,3),
    )
    recv = exchange(sent)
    hidden, pre_first, frame, sent, *parts = run(
        first_kernel,
        "first_layer",
        (tile_links, field, recv, frame, pack, unpack, first_weights),
        [moved_in] + [near] * 6,
        (rows_like, like(192, 256, dtype=f32), frame_like, sent_like) + (like(304, 128),) * 4,
        [grid_shape, frame_shape, frame_shape, flat_shape],
        conv_flops,
        (0,2,3,5,6,7),
    )
    recv = exchange(sent)
    field_parts = ring(parts, "x")
    states, misfit, inner, frame, sent, *parts = run(
        second_kernel,
        "second_layer",
        (
            tile_links, field, goal, hidden, recv, frame, pack, unpack, second_weights,
            *field_parts[1:],
        ),
        [moved_in] * 3 + [near] * 6 + [left] * 3,
        (rows_like, like(192, 256, dtype=f32), inner_like, frame_like, sent_like)
        + (like(496, 128),) * 4,
        [grid_shape, frame_shape, frame_shape, flat_shape, column_shape],
        2 * conv_flops,
        (2,3,4,5,6,7,8),
    )
    recv = exchange(sent)
    closing_parts = ring(parts, "x")
    closing = slope_terms(closing_parts, True)
    last, frame, *parts = run(
        third_kernel,
        "first_gradient",
        (tile_links, inner, pre_first, recv, frame, unpack, first_weights),
        [moved_in, near, moved_in] + [near] * 3 + [moved_in],
        (inner_like, frame_like) + (like(192, 128),) * 4,
        [grid_shape, frame_shape, frame_shape, column_shape],
        conv_flops,
        (1,2,3,4,5),
    )
    got_closing = shifted(closing[1], "core", 1)
    *opening, sent = slope_terms(
        field_parts + ring(parts, "x"), False, (pack, frame), (closing[0],)
    )
    recv = exchange(sent)
    chunks = run(
        pair_kernel,
        "pair_sum",
        (opening[0], shifted(opening[1], "core", 1), closing[0], got_closing),
        [near] * 4,
        (like(288, 128, dtype=f32),) * 4,
        [],
        1000,
        (0, 1, 2, 3),
    )
    condition_derivative = run(
        last_kernel,
        "last_gradient",
        (last, misfit, recv, frame, unpack),
        [moved_in] * 2 + [near] * 3,
        inner_like,
        [grid_shape, frame_shape],
        1000,
    )
    slopes = finish_slopes(chunks, recv, scale)
    return (
        states.reshape(network_conditions.shape),
        condition_derivative[None],
        slopes[0].reshape(w_first.shape),
        slopes[1].reshape(w_second.shape),
    )


def solution(mesh):
    return jax.shard_map(
        per_device,
        mesh=mesh,
        in_specs=(
            P("ens", "tile", None, None, None),
            P("ens", "tile", None, None, None),
            P(),
            P(),
            P("tile", None),
        ),
        out_specs=(
            P("ens", "tile", None, None, None),
            P("ens", "tile", None, None, None),
            P(),
            P(),
        ),
        check_vma=False,
    )
```

```python
import itertools
import math

import jax
import jax.numpy as jnp
from jax import lax
from jax.experimental import pallas as pl
from jax.experimental.pallas import tpu as pltpu
from jax.sharding import PartitionSpec as P

tanh_scale = 0.7978845608028654
cubic_term = 0.044715
slot_rows = 32
send_rows = 1024
bf16, f32 = jnp.bfloat16, jnp.float32


def gelu_value(inputs):
    return (
        0.5
        * inputs
        * (1.0 + jnp.tanh(tanh_scale * (inputs + cubic_term * inputs * inputs * inputs)))
    )


def gelu_slope(inputs):
    tangent = jnp.tanh(tanh_scale * (inputs + cubic_term * inputs * inputs * inputs))
    return 0.5 * (1.0 + tangent) + 0.5 * inputs * (1.0 - tangent * tangent) * tanh_scale * (
        1.0 + 3.0 * cubic_term * inputs * inputs
    )


sizes = {"x": 4, "y": 4, "z": 8, "core": 2}


def place_of(x, y, z, core):
    return ((y * 2 + z % 2) * 4 + x) * 8 + (z // 2) * 2 + core


def shifted(values, axis, by):
    pairs = []
    for x in range(4):
        for y in range(4):
            for z in range(8):
                for core in range(2):
                    at = {"x": x, "y": y, "z": z, "core": core}
                    to = dict(at)
                    to[axis] = (at[axis] + by) % sizes[axis]
                    pairs.append((place_of(**at), place_of(**to)))
    return lax.ppermute(values, ("tile", "ens"), pairs)


def placing():
    tile, ens = lax.axis_index("tile"), lax.axis_index("ens")
    return tile, lax.rem(tile, 4), lax.rem(ens, 2), tile // 8


edge_starts = ((0, 3), (0, 1), (1, 2), (2, 3))
corner_ends = ((0, 0), (7, 0), (7, 7), (0, 7))
corner_cells = ((0, 0), (0, 1), (1, 1), (1, 0))
strips = [(tile, edge) for tile in range(3) for edge in range(4)]


def edge_slices(tile, edge, low, high):
    inner = slice(1, 9)
    return (
        (tile, low, inner),
        (tile, inner, high),
        (tile, high, inner),
        (tile, inner, low),
    )[edge]


def corner_at(corner, low, high):
    down, across = corner_cells[corner]
    return (high if down else low), (high if across else low)


def take_frame(grid, frame, links, low, high, kept):
    for i, (tile, edge) in enumerate(strips):
        frame[8 * i : 8 * i + 8] = grid[edge_slices(tile, edge, low, high)]
    for tile in range(3):
        for corner in range(4):
            row, column = corner_at(corner, low, high)
            cell = grid[tile, row, column : column + 1, :]
            if kept:
                cell = jnp.where(links[tile, 12 + corner] == 4, cell, 0.0)
            at = 96 + 4 * tile + corner
            frame[at : at + 1] = cell
    frame[108:128] = jnp.zeros((20, 256), f32)


def fill_ghosts(grid, got, links):
    for i, (tile, edge) in enumerate(strips):
        grid[edge_slices(tile, edge, 0, 9)] = got[8 * i : 8 * i + 8]
    for tile in range(3):
        for corner in range(4):
            row, column = corner_at(corner, 0, 9)
            at = 96 + 4 * tile + corner
            beside = [
                8 * (4 * tile + edge) + end
                for edge, end in zip(edge_starts[corner], corner_ends[corner])
            ]
            blend = 0.5 * (got[beside[0] : beside[0] + 1] + got[beside[1] : beside[1] + 1])
            grid[tile, row, column : column + 1, :] = jnp.where(
                links[tile, 12 + corner] == 4, got[at : at + 1], blend
            )


def split_corners(grid, links):
    for tile in range(3):
        for corner in range(4):
            row, column = corner_at(corner, 0, 9)
            near_row, near_column = corner_at(corner, 1, 8)
            cell = grid[tile, row, column : column + 1, :]
            half = jnp.where(links[tile, 12 + corner] == 3, 0.5 * cell, 0.0)
            grid[tile, row, near_column : near_column + 1, :] += half
            grid[tile, near_row, column : column + 1, :] += half


def add_returns(grid, got):
    for i, (tile, edge) in enumerate(strips):
        grid[edge_slices(tile, edge, 1, 8)] += got[8 * i : 8 * i + 8]
    for tile in range(3):
        for corner in range(4):
            row, column = corner_at(corner, 1, 8)
            at = 96 + 4 * tile + corner
            grid[tile, row, column : column + 1, :] += got[at : at + 1]


def pack_frame(pack_ref, frame, frame_ref, sent_ref):
    cells = frame[...].astype(bf16)
    frame_ref[...] = cells
    sent_ref[...] = jnp.dot(pack_ref[...], cells, preferred_element_type=f32).astype(bf16)


def unpack_frame(unpack_ref, recv_ref, frame_ref, got):
    got[...] = jnp.dot(
        unpack_ref[:, :send_rows], recv_ref[...], preferred_element_type=f32
    ) + jnp.dot(unpack_ref[:, send_rows:], frame_ref[...], preferred_element_type=f32)


def convolve(grid, weights):
    windows = []
    for down in range(3):
        for across in range(3):
            window = grid[:, down : down + 8, across : across + 8, :]
            windows.append(window.reshape(192, 256).astype(bf16))
    return jnp.dot(
        jnp.concatenate(windows, axis=1),
        weights[...].reshape(2304, 256),
        preferred_element_type=f32,
    )


def spread_back(gradient, weights, grid, column):
    grid[...] = jnp.zeros_like(grid)
    for across in range(3):
        column[...] = jnp.zeros_like(column)
        for down in range(3):
            part = lax.dot_general(
                gradient,
                weights[3 * down + across],
                (((1,), (1,)), ((), ())),
                preferred_element_type=f32,
            )
            column[:, down : down + 8] += part.reshape(3, 8, 8, 256)
        grid[:, :, across : across + 8, :] += column[...]


def halves(place, flat, pick):
    for k in range(4):
        quarter = lax.rem(place[1] + k, 4)
        side = quarter // 2 if pick == 0 else lax.rem(quarter, 2)
        yield k, jnp.where(side == 0, flat[:, :128], flat[:, 128:]).astype(bf16)


def flatten_grid(grid, flat):
    flat[300:304] = jnp.zeros((4, 256), f32)
    for tile in range(3):
        for row in range(10):
            at = 100 * tile + 10 * row
            flat[at : at + 10] = grid[tile, row]


def route_kernel(place, links, field_ref, pack_ref, unpack_ref, frame_ref, sent_ref, grid, frame):
    here = place[0]

    def rows_of(tiles, sides, valid, base, width, local_base):
        device = [tile // 3 for tile in tiles]
        source = [lax.rem(tile, 3) * 4 + side for tile, side in zip(tiles, sides)]
        out = []
        for i in range(12):
            send_rank = take_rank = jnp.int32(0)
            for j in range(12):
                near = (device[j] == device[i]) & valid[j]
                if j < i:
                    send_rank += jnp.where(near, width, 0)
                if j != i:
                    take_rank += jnp.where(near & (source[j] < source[i]), width, 0)
            first = device[i] * slot_rows + base
            own = device[i] == here
            send = jnp.where(own | ~valid[i], -1000, first + send_rank)
            take = jnp.where(own, local_base + source[i] * width, first + take_rank)
            out.append((send, jnp.where(valid[i], take, -1000)))
        return out

    codes = [links[tile, 4 + edge] for tile, edge in strips]
    edges = rows_of(
        [links[tile, edge] for tile, edge in strips],
        [lax.rem(code, 4) for code in codes],
        [links[tile, edge] >= 0 for tile, edge in strips],
        0,
        8,
        send_rows,
    )
    across = [links[tile, 8 + corner] for tile, corner in strips]
    corners = rows_of(
        [jnp.maximum(c, 0) // 4 for c in across],
        [lax.rem(jnp.maximum(c, 0), 4) for c in across],
        [c >= 0 for c in across],
        24,
        1,
        send_rows + 96,
    )
    lane = lax.broadcasted_iota(jnp.int32, (8, 128), 1)
    row = lax.broadcasted_iota(jnp.int32, (128, 128), 0)
    send = jnp.full((8, 128), -1000, jnp.int32)
    take = jnp.full((128, 128), -1000, jnp.int32)
    for i in range(12):
        send = jnp.where(lane // 8 == i, edges[i][0] + lane % 8, send)
        send = jnp.where(lane == 96 + i, corners[i][0], send)
        turned = codes[i] // 4 == 1
        step = jnp.where(turned, 7 - row % 8, row % 8)
        take = jnp.where(row // 8 == i, edges[i][1] + step, take)
        take = jnp.where(row == 96 + i, corners[i][1], take)
    slot = lax.broadcasted_iota(jnp.int32, (send_rows, 128), 0)
    pack_ref[...] = jnp.where(slot == send[:1], 1.0, 0.0).astype(bf16)
    column = lax.broadcasted_iota(jnp.int32, (128, 128), 1)
    for m in range(9):
        unpack_ref[:, 128 * m : 128 * m + 128] = jnp.where(
            take == column + 128 * m, 1.0, 0.0
        ).astype(bf16)
    grid[:, 1:9, 1:9, :] = field_ref[...].astype(f32).reshape(3, 8, 8, 256)
    take_frame(grid, frame, links, 1, 8, False)
    pack_frame(pack_ref, frame, frame_ref, sent_ref)


def first_kernel(
    place, links, field_ref, recv_ref, old_ref, pack_ref, unpack_ref, weights,
    hidden_ref, pre_ref, frame_ref, sent_ref, part0, part1, part2, part3,
    grid, frame, got, flat,
):
    unpack_frame(unpack_ref, recv_ref, old_ref, got)
    grid[:, 1:9, 1:9, :] = field_ref[...].astype(f32).reshape(3, 8, 8, 256)
    fill_ghosts(grid, got, links)
    pre_first = convolve(grid, weights)
    pre_ref[...] = pre_first
    hidden = gelu_value(pre_first).astype(bf16)
    hidden_ref[...] = hidden
    flatten_grid(grid, flat)
    grid[:, 1:9, 1:9, :] = hidden.astype(f32).reshape(3, 8, 8, 256)
    take_frame(grid, frame, links, 1, 8, False)
    pack_frame(pack_ref, frame, frame_ref, sent_ref)
    parts = (part0, part1, part2, part3)
    for k, half in halves(place, flat, 0):
        parts[k][...] = half


def second_kernel(
    place, links, field_ref, goal_ref, hidden_ref, recv_ref, old_ref, pack_ref, unpack_ref, weights,
    state_ref, misfit_ref, inner_ref, frame_ref, sent_ref, part0, part1, part2, part3,
    grid, frame, got, flat, column,
):
    unpack_frame(unpack_ref, recv_ref, old_ref, got)
    grid[:, 1:9, 1:9, :] = hidden_ref[...].astype(f32).reshape(3, 8, 8, 256)
    fill_ghosts(grid, got, links)
    states = field_ref[...].astype(f32) + convolve(grid, weights)
    state_ref[...] = states.astype(bf16)
    misfit = states - goal_ref[...].astype(f32)
    misfit_ref[...] = misfit
    low = misfit.astype(bf16)
    flatten_grid(grid, flat)
    spread_back(low, weights, grid, column)
    split_corners(grid, links)
    take_frame(grid, frame, links, 0, 9, True)
    pack_frame(pack_ref, frame, frame_ref, sent_ref)
    inner_ref[...] = grid[:, 1:9, 1:9, :]
    parts = (part0, part1, part2, part3)
    for k, half in halves(place, flat, 0):
        parts[k][:304] = half
    for k, half in halves(place, low.astype(f32), 1):
        parts[k][304:] = half


def third_kernel(
    place, links, inner_ref, pre_ref, recv_ref, old_ref, unpack_ref, weights, *refs,
):
    last_ref, frame_ref, part0, part1, part2, part3, grid, frame, got, column = refs[3:]
    unpack_frame(unpack_ref, recv_ref, old_ref, got)
    grid[:, 1:9, 1:9, :] = inner_ref[...]
    add_returns(grid, got)
    hidden_grad = grid[:, 1:9, 1:9, :].reshape(192, 256)
    low = (hidden_grad * gelu_slope(pre_ref[...])).astype(bf16)
    parts = (part0, part1, part2, part3)
    for k, half in halves(place, low.astype(f32), 1):
        parts[k][...] = half
    spread_back(low, weights, grid, column)
    split_corners(grid, links)
    take_frame(grid, frame, links, 0, 9, True)
    frame_ref[...] = frame[...].astype(bf16)
    last_ref[...] = grid[:, 1:9, 1:9, :]


def last_kernel(place, last_ref, misfit_ref, recv_ref, old_ref, unpack_ref, out_ref, grid, got):
    unpack_frame(unpack_ref, recv_ref, old_ref, got)
    grid[:, 1:9, 1:9, :] = last_ref[...] + misfit_ref[...].reshape(3, 8, 8, 256)
    add_returns(grid, got)
    out_ref[...] = grid[:, 1:9, 1:9, :]


moved_in = pl.BlockSpec(memory_space=pltpu.HBM)
landed = pl.BlockSpec(memory_space=pl.ANY)
left = pl.BlockSpec()
near = pl.BlockSpec(memory_space=pltpu.VMEM)
resting = pl.BlockSpec(memory_space=pltpu.HBM)
grid_shape = pltpu.VMEM((3, 10, 10, 256), f32)
frame_shape = pltpu.VMEM((128, 256), f32)
flat_shape = pltpu.VMEM((304, 256), f32)
column_shape = pltpu.VMEM((3, 10, 8, 256), f32)


def like(*shape, dtype=bf16):
    return jax.ShapeDtypeStruct(shape, dtype)


class Arriving:
    def __init__(self, ref, copy):
        self.ref, self.copy = ref, copy

    def settle(self):
        if self.copy is not None:
            self.copy.wait()
            self.copy = None

    def __getitem__(self, at):
        self.settle()
        return self.ref[at]


class Leaving:
    def __init__(self, ref, copy):
        self.ref, self.copy, self.started = ref, copy, False

    def send(self):
        if not self.started:
            self.copy.start()
            self.started = True

    def __getitem__(self, at):
        return self.ref[at]

    def __setitem__(self, at, value):
        self.ref[at] = value
        if at is Ellipsis:
            self.send()


def run(kernel, name, args, specs, outs, scratch, flops, kept=()):
    single = not isinstance(outs, tuple)
    outs = (outs,) if single else outs
    moved = [i for i, spec in enumerate(specs) if spec is moved_in or spec is landed]
    buffers = [
        (pltpu.SMEM if args[i].dtype == jnp.int32 else pltpu.VMEM)(args[i].shape, args[i].dtype)
        for i in moved
    ]
    away = [n for n in range(len(outs)) if n not in kept]
    stores = [pltpu.VMEM(outs[n].shape, outs[n].dtype) for n in away]

    def body(*refs):
        ins, refs = refs[: len(args)], refs[len(args) :]
        targets, refs = refs[: len(outs)], refs[len(outs) :]
        held, refs = refs[: len(moved)], refs[len(moved) :]
        made, refs = refs[: len(away)], refs[len(away) :]
        arrived, left_for, refs = refs[0], refs[1], refs[2:]
        copies = [
            pltpu.make_async_copy(ins[i], held[n], arrived.at[n]) for n, i in enumerate(moved)
        ]
        for copy in copies:
            copy.start()
        given = list(ins)
        for n, i in enumerate(moved):
            given[i] = Arriving(held[n], copies[n])
        results = list(targets)
        for m, n in enumerate(away):
            copy = pltpu.make_async_copy(made[m], targets[n], left_for.at[m])
            results[n] = Leaving(made[m], copy)
        kernel(placing(), *given, *results, *refs)
        for n in range(len(moved)):
            given[moved[n]].settle()
        for n in away:
            results[n].send()
        for n in away:
            results[n].copy.wait()

    made = pl.pallas_call(
        body,
        out_shape=tuple(
            pltpu.HBM(out.shape, out.dtype) if n in away else out for n, out in enumerate(outs)
        ),
        in_specs=[landed if spec is left else spec for spec in specs],
        out_specs=tuple(moved_in if n in away else near for n in range(len(outs))),
        scratch_shapes=[
            *buffers,
            *stores,
            pltpu.SemaphoreType.DMA((max(1, len(moved)),)),
            pltpu.SemaphoreType.DMA((max(1, len(away)),)),
            *scratch,
        ],
        compiler_params=pltpu.CompilerParams(vmem_limit_bytes=40 * 2**20),
        cost_estimate=pl.CostEstimate(flops=flops, bytes_accessed=3000000, transcendentals=0),
        name=name,
    )(
        *[
            pltpu.with_memory_space_constraint(arg, pltpu.HBM)
            if spec is moved_in or spec is resting
            else arg
            for arg, spec in zip(args, specs)
        ]
    )
    return made[0] if single else made


def slope_kernel(split, place, *refs):
    count = 4 if split else 8
    parts = refs[:count]
    kept_ref, sent_ref, flat, wide, total = refs[count:]
    grads = []
    for n in range(4):
        flat[304 * n : 304 * n + 304] = parts[n][:304].astype(f32)
        grads.append(parts[n][304:] if split else parts[4 + n][...])
    grads = jnp.concatenate(grads, axis=0)
    low = place[2] == 0
    for across in range(3):
        for n in range(4):
            for tile in range(3):
                for row in range(10):
                    at = 304 * n + 100 * tile + 10 * row + across
                    wide[3 * n + tile, row] = flat[at : at + 8]
        for down in range(3):
            window = wide[:, down : down + 8].reshape(768, 128).astype(bf16)
            out = lax.dot_general(
                window, grads, (((0,), (0,)), ((), ())), preferred_element_type=f32
            )
            tap = (3 * down + across) * 64
            total[0, tap : tap + 64] = jnp.where(low, out[:64], out[64:])
            total[1, tap : tap + 64] = jnp.where(low, out[64:], out[:64])
    for j in range(4):
        kept_ref[j] = total[0, 144 * j : 144 * j + 144]
        sent_ref[j] = total[1, 144 * j : 144 * j + 144]


def slope_terms(parts, split, packing=(), held=()):
    shape = like(4, 144, 128, dtype=f32)
    count = len(parts)
    outs = (shape, shape) + ((like(send_rows, 256),) if packing else ())

    def kernel(place, *refs):
        ins, refs = refs[: count + len(packing)], refs[count + len(packing) + len(held) :]
        if packing:
            pack_ref, frame_ref = ins[count:]
            refs[2][...] = jnp.dot(
                pack_ref[...], frame_ref[...], preferred_element_type=f32
            ).astype(bf16)
        slope_kernel(split, place, *ins[:count], *refs[:2], *refs[len(outs) :])

    return run(
        kernel,
        "slope_terms",
        (*parts, *packing, *held),
        ([moved_in] + [landed] * 3) * (count // 4 - 1)
        + [near] * 4
        + [near] * len(packing)
        + [near] * len(held),
        outs,
        [
            pltpu.VMEM((1216, 128), f32),
            pltpu.VMEM((12, 10, 8, 128), f32),
            pltpu.VMEM((2, 576, 128), f32),
        ],
        2 * 9 * 768 * 128 * 128,
        tuple(range(len(outs))),
    )


def ring(parts, axis):
    return [shifted(part, axis, k) if k else part for k, part in enumerate(parts)]


def pair_kernel(place, kept0, got0, kept1, got1, *chunks):
    for k in range(4):
        at = lax.rem(place[3] + k, 4)
        chunks[k][:144] = kept0[at] + got0[at]
        chunks[k][144:] = kept1[at] + got1[at]


def plane_kernel(place, own, part1, part2, part3, held, out, total):
    total[...] = (own[...] + part1[...]) + (part2[...] + part3[...])
    for j in range(8):
        out[j] = total[36 * j : 36 * j + 36]


def spread_kernel(place, own, other, first_ref, second_ref):
    low = place[2] == 0
    for n, out in enumerate((first_ref, second_ref)):
        at = slice(144 * n, 144 * n + 144)
        for x in range(4):
            row, column = 128 * (x // 2), 128 * (x % 2)
            pair = [
                jnp.concatenate(
                    [part[4 * x + y, at].astype(f32) for y in range(4)], axis=0
                ).reshape(9, 64, 128)
                for part in (own, other)
            ]
            out[:, row : row + 64, column : column + 128] = jnp.where(low, pair[0], pair[1])
            out[:, row + 64 : row + 128, column : column + 128] = jnp.where(low, pair[1], pair[0])
        out.send()


def groups(along):
    axes = ("x", "y", "z", "core")
    out = []
    for fixed in itertools.product(*[range(1 if a in along else sizes[a]) for a in axes]):
        group = []
        for moving in itertools.product(*[range(sizes[a]) for a in along]):
            at = dict(zip(axes, fixed)) | dict(zip(along, moving))
            group.append(place_of(**at))
        out.append(group)
    return out


def trade(values, *along):
    return lax.all_to_all(
        values, ("tile", "ens"), 0, 0, axis_index_groups=groups(along), tiled=True
    )


def copies_of(values, count):
    return jnp.broadcast_to(values[None], (count,) + values.shape)


def finish_slopes(chunks, held, scale):
    terms = run(
        plane_kernel,
        "row_sum",
        (*ring(chunks, "y"), held),
        [near] * 4 + [left],
        like(8, 36, 128, dtype=f32),
        [pltpu.VMEM((288, 128), f32)],
        1000,
        (0,),
    )
    mine = (jnp.sum(trade(terms, "z"), axis=0) * scale).astype(bf16)
    line = trade(copies_of(mine, 8), "z").reshape(288, 128)
    plane = trade(copies_of(line, 16), "x", "y")
    shape = like(9, 256, 256, dtype=f32)
    return run(
        spread_kernel,
        "spread_slopes",
        (plane, shifted(plane, "core", 1)),
        [landed, landed],
        (shape, shape),
        [],
        1000,
    )


def exchange(values):
    return lax.all_to_all(values, "tile", 0, 0, tiled=True)


def per_device(network_conditions, subsequent_targets, w_first, w_second, tile_links):
    field = network_conditions.reshape(192, 256)
    goal = subsequent_targets.reshape(192, 256)
    first_weights, second_weights = w_first.reshape(9, 256, 256), w_second.reshape(9, 256, 256)
    scale = 1.0 / math.sqrt(lax.axis_size("ens") * lax.axis_size("tile") * 192)
    frame_like, sent_like, rows_like = like(128, 256), like(send_rows, 256), like(192, 256)
    inner_like = like(3, 8, 8, 256, dtype=f32)
    conv_flops = 2 * 9 * 192 * 256 * 256

    pack, unpack, frame, sent = run(
        route_kernel,
        "routes",
        (tile_links, field),
        [moved_in, moved_in],
        (like(send_rows, 128), like(128, send_rows + 128), frame_like, sent_like),
        [grid_shape, frame_shape],
        2 * send_rows * 128 * 256,
        (0,1,2,3),
    )
    recv = exchange(sent)
    hidden, pre_first, frame, sent, *parts = run(
        first_kernel,
        "first_layer",
        (tile_links, field, recv, frame, pack, unpack, first_weights),
        [moved_in] + [near] * 6,
        (rows_like, like(192, 256, dtype=f32), frame_like, sent_like) + (like(304, 128),) * 4,
        [grid_shape, frame_shape, frame_shape, flat_shape],
        conv_flops,
        (0,2,3,5,6,7),
    )
    recv = exchange(sent)
    field_parts = ring(parts, "x")
    states, misfit, inner, frame, sent, *parts = run(
        second_kernel,
        "second_layer",
        (
            tile_links, field, goal, hidden, recv, frame, pack, unpack, second_weights,
        ),
        [moved_in] * 3 + [near] * 6,
        (rows_like, like(192, 256, dtype=f32), inner_like, frame_like, sent_like)
        + (like(496, 128),) * 4,
        [grid_shape, frame_shape, frame_shape, flat_shape, column_shape],
        2 * conv_flops,
        (2,3,4,5,6,7,8),
    )
    recv = exchange(sent)
    closing_parts = ring(parts, "x")
    closing = slope_terms(closing_parts, True)
    last, frame, *parts = run(
        third_kernel,
        "first_gradient",
        (tile_links, inner, pre_first, recv, frame, unpack, first_weights, *field_parts[1:]),
        [moved_in, near, moved_in] + [near] * 3 + [moved_in] + [left] * 3,
        (inner_like, frame_like) + (like(192, 128),) * 4,
        [grid_shape, frame_shape, frame_shape, column_shape],
        conv_flops,
        (1,2,3,4,5),
    )
    got_closing = shifted(closing[1], "core", 1)
    *opening, sent = slope_terms(
        field_parts + ring(parts, "x"), False, (pack, frame), (closing[0],)
    )
    recv = exchange(sent)
    chunks = run(
        pair_kernel,
        "pair_sum",
        (opening[0], shifted(opening[1], "core", 1), closing[0], got_closing),
        [near] * 4,
        (like(288, 128, dtype=f32),) * 4,
        [],
        1000,
        (0, 1, 2, 3),
    )
    condition_derivative = run(
        last_kernel,
        "last_gradient",
        (last, misfit, recv, frame, unpack),
        [moved_in] * 2 + [near] * 3,
        inner_like,
        [grid_shape, frame_shape],
        1000,
    )
    slopes = finish_slopes(chunks, recv, scale)
    return (
        states.reshape(network_conditions.shape),
        condition_derivative[None],
        slopes[0].reshape(w_first.shape),
        slopes[1].reshape(w_second.shape),
    )


def solution(mesh):
    return jax.shard_map(
        per_device,
        mesh=mesh,
        in_specs=(
            P("ens", "tile", None, None, None),
            P("ens", "tile", None, None, None),
            P(),
            P(),
            P("tile", None),
        ),
        out_specs=(
            P("ens", "tile", None, None, None),
            P("ens", "tile", None, None, None),
            P(),
            P(),
        ),
        check_vma=False,
    )
```
